128 devices in a mesh: seq: 32 (over z, y, core), head: 4 (over x).
Axes of the slice: x: 4, y: 4, z: 4, core: 2. Of those that a mesh axis runs over, the one named last changes fastest.
Arguments:
- hidden_in: bfloat16 [4096, 2048], P('seq'), may hold values from -6 to 6
- cotangent: bfloat16 [4096, 2048], P('seq'), may hold values from -6 to 6
- segment_ids: int32 [4096], replicated, may hold values from 0 to 4, as said below
- norm_gain: float32 [2, 2048], replicated, may hold values from 0.5 to 1.5
- weight_zx: bfloat16 [2, 2048, 2, 4096], P(None, None, None, 'head'), may hold values from -0.125 to 0.125
- weight_bc: bfloat16 [2, 2048, 256], replicated, may hold values from -0.125 to 0.125
- weight_dt: bfloat16 [2, 2048, 64], P(None, None, 'head'), may hold values from -0.125 to 0.125
- dt_bias: float32 [2, 64], P(None, 'head'), may hold values from -3 to -0.5
- a_log: float32 [2, 64], P(None, 'head'), may hold values from -12 to 0
- skip_scale: float32 [2, 64], P(None, 'head'), may hold values from 0.5 to 1.5
- conv_x: float32 [2, 4, 4096], P(None, None, 'head'), may hold values from -3 to 3
- conv_x_bias: float32 [2, 4096], P(None, 'head'), may hold values from -1.8 to 1.8
- conv_bc: float32 [2, 4, 256], replicated, may hold values from -3 to 3
- conv_bc_bias: float32 [2, 256], replicated, may hold values from -1.8 to 1.8
- gate_gain: float32 [2, 4096], P(None, 'head'), may hold values from 0.5 to 1.5
- weight_out: bfloat16 [2, 4096, 2048], P(None, 'head'), may hold values from -0.09375 to 0.09375
Outputs:
- out_hidden: bfloat16 [4096, 2048], P('seq')
- grad_in: bfloat16 [4096, 2048], P('seq')
- grad_norm_gain: float32 [2, 2048], P(None, 'seq')
- grad_weight_zx: float32 [2, 2048, 2, 4096], P(None, 'seq', None, 'head')
- grad_weight_bc: float32 [2, 2048, 256], P(None, 'seq')
- grad_weight_dt: float32 [2, 2048, 64], P(None, 'seq', 'head')
- grad_dt_bias: float32 [2, 64], P(None, 'head')
- grad_a_log: float32 [2, 64], P(None, 'head')
- grad_skip_scale: float32 [2, 64], P(None, 'head')
- grad_conv_x: float32 [2, 4, 4096], P(None, None, 'head')
- grad_conv_x_bias: float32 [2, 4096], P(None, 'head')
- grad_conv_bc: float32 [2, 4, 256], replicated
- grad_conv_bc_bias: float32 [2, 256], replicated
- grad_gate_gain: float32 [2, 4096], P(None, 'head')
- grad_weight_out: float32 [2, 4096, 2048], P(None, 'head', 'seq')
The draws below stay inside these ranges and needn't reach their ends.
Inputs may be any that keep to these rules, and one draw needn't show every extreme that they name: `segment_ids`: ids never fall along the sequence, start at 0, and end at (4096 - 1) // 1000; every document but the first and the last holds 100 to 1000 tokens.
All inputs are finite; a program needn't handle non-finite values.
Results may differ from the reference program's by a relative error of at most 0.025.
Values may be sent and summed in bfloat16 or wider, within the bound.
A program may use at most 256 MiB of HBM per device.

```python
import math
import jax
import jax.numpy as jnp
from jax import lax

D = 2048
HEADS = 64
HEAD_DIM = 64
STATE = 128
CONV = 4
LAYERS = 2
TOK_DEV = 128
INNER = 4096
SEQ = 4096


def draw_segment_ids(key, part):
    key = jax.random.fold_in(key, 11)
    length_key, offset_key = jax.random.split(key, 2)
    shortest = 25 * TOK_DEV // 32
    longest = 125 * TOK_DEV // 16
    count = SEQ // shortest + 2
    lengths = jax.random.randint(length_key, (count,), shortest, longest + 1)
    offset = jax.random.randint(offset_key, (), 0, shortest)
    bounds = jnp.cumsum(lengths) - offset
    positions = jnp.arange(SEQ, dtype=jnp.int32)
    numbers = jnp.sum((positions[:, None] >= bounds[None, :]).astype(jnp.int32), axis=1)
    return jnp.minimum(numbers, (SEQ - 1) // longest).astype(jnp.int32)


def draw_a_log(key, part):
    key = jax.random.fold_in(key, 23)
    return jax.random.uniform(key, (LAYERS, HEADS), jnp.float32, math.log(1.0 / SEQ), math.log(0.3))


def level_of(rng, extent, cuts, smallest, high):
    loudness, own = 1.0, jax.random.fold_in(rng, 6)
    for axis_at, blocks in cuts:
        steps = jnp.exp(jax.random.uniform(jax.random.fold_in(own, axis_at), (blocks,), jnp.float32, smallest / len(cuts), high / len(cuts)))
        loudness = loudness * jnp.repeat(steps, extent[axis_at] // blocks).reshape([-1 if axis == axis_at else 1 for axis in range(len(extent))])
    return loudness


def bell_draw(own_key, shape, width, most, cuts=(), kind=jnp.bfloat16):
    values = jax.random.normal(own_key, shape, jnp.float32) * width
    if len(cuts) > 0:
        values = level_of(own_key, shape, cuts, -0.22, 0.18) * values
    return jnp.clip(values, min=-most, max=most).astype(kind)


def setup_inputs(seed: int = 0) -> dict:
    key_list = jax.random.split(jax.random.key(seed), 17)
    return {
        "hidden_in": bell_draw(key_list[0], (SEQ, D), 1.0, 6.0, ((0, 32),)),
        "cotangent": bell_draw(key_list[1], (SEQ, D), 1.0, 6.0, ((0, 32),)),
        "segment_ids": draw_segment_ids(jax.random.fold_in(key_list[16], 71), 0),
        "norm_gain": jnp.clip(1.0 + 0.1 * jax.random.normal(key_list[3], (LAYERS, D), jnp.float32), 0.5, 1.5),
        "weight_zx": bell_draw(key_list[4], (LAYERS, D, 2, INNER), D ** -0.5, 0.125, ((3, 4),)),
        "weight_bc": bell_draw(key_list[5], (LAYERS, D, 2 * STATE), D ** -0.5, 0.125),
        "weight_dt": bell_draw(key_list[6], (LAYERS, D, HEADS), D ** -0.5, 0.125, ((2, 4),)),
        "dt_bias": jnp.clip(-3.0 + 2.5 * jax.random.uniform(key_list[7], (LAYERS, HEADS), jnp.float32) ** level_of(key_list[7], (LAYERS, HEADS), ((1, 4),), -0.2, 0.2), -3.0, -0.5),
        "a_log": draw_a_log(jax.random.fold_in(key_list[16], 71), 0),
        "skip_scale": jnp.clip(0.5 + 1.0 * jax.random.uniform(key_list[9], (LAYERS, HEADS), jnp.float32) ** level_of(key_list[9], (LAYERS, HEADS), ((1, 4),), -0.2, 0.2), 0.5, 1.5),
        "conv_x": bell_draw(key_list[10], (LAYERS, CONV, INNER), CONV ** -0.5, 3.0, ((2, 4),), jnp.float32),
        "conv_x_bias": bell_draw(key_list[11], (LAYERS, INNER), 0.3, 1.8, ((1, 4),), jnp.float32),
        "conv_bc": bell_draw(key_list[12], (LAYERS, CONV, 2 * STATE), CONV ** -0.5, 3.0, (), jnp.float32),
        "conv_bc_bias": bell_draw(key_list[13], (LAYERS, 2 * STATE), 0.3, 1.8, (), jnp.float32),
        "gate_gain": jnp.clip(1.0 + 0.1 * jax.random.normal(key_list[14], (LAYERS, INNER), jnp.float32), 0.5, 1.5),
        "weight_out": bell_draw(key_list[15], (LAYERS, INNER, D), INNER ** -0.5, 0.09375, ((1, 4),)),
    }


EPSILON = 1e-05
PRECISE = lax.Precision.HIGHEST

@jax.custom_vjp
def low(v):
    return lax.optimization_barrier(v.astype(jnp.bfloat16)).astype(jnp.float32)

@jax.custom_vjp
def low_back(v):
    return v

def low_keep(v):
    return (low(v), None)

def low_pass(kept, grad):
    return (grad,)

def back_keep(v):
    return (v, None)

def back_low(kept, grad):
    return (low(grad),)
low.defvjp(low_keep, low_pass)
low_back.defvjp(back_keep, back_low)

def convolve(extended, weights, biases, extended_ids):
    taps = weights.shape[0]
    length = extended.shape[0] - (taps - 1)
    current = extended_ids[taps - 1:]
    totals = jnp.zeros((length, extended.shape[1]), extended.dtype) + biases[None, :]
    for offset in range(taps):
        keep = (extended_ids[offset:offset + length] == current)[:, None]
        totals = totals + jnp.where(keep, weights[offset][None, :] * extended[offset:offset + length], 0.0)
    return jax.nn.silu(totals)

def block_step(carried, block_inputs):
    ssm_state, prior_id = carried
    values, keys, queries, steps, rates, block_ids = block_inputs
    cumul = jnp.cumsum(rates, axis=0)
    length = rates.shape[0]
    row_index = lax.broadcasted_iota(jnp.int32, (length, length), 0)
    col_index = lax.broadcasted_iota(jnp.int32, (length, length), 1)
    allowed = ((row_index >= col_index) & (block_ids[:, None] == block_ids[None, :]))[:, :, None]
    spread = cumul[:, None, :] - cumul[None, :, :]
    decays = jnp.where(allowed, jnp.exp(jnp.where(allowed, spread, 0.0)), 0.0)
    intersection = jnp.dot(queries, keys.T, precision=PRECISE)
    mixing = intersection[:, :, None] * decays * steps[None, :, :]
    outputs = jnp.einsum('tsh,shp->thp', mixing, values, precision=PRECISE)
    carry_flag = (block_ids == prior_id).astype(rates.dtype)
    entering = jnp.exp(cumul) * carry_flag[:, None]
    outputs = outputs + jnp.einsum('tn,th,hpn->thp', queries, entering, ssm_state, precision=PRECISE)
    ending = (block_ids == block_ids[-1]).astype(rates.dtype)
    leaving = jnp.exp(cumul[-1][None, :] - cumul) * ending[:, None] * steps
    new_state = entering[-1][:, None, None] * ssm_state + jnp.einsum('sh,shp,sn->hpn', leaving, values, keys, precision=PRECISE)
    return ((new_state, block_ids[-1]), outputs)

def state_space(values, keys, queries, steps, rates, block_ids):
    length = values.shape[0]
    block_len = min(256, length)
    blocks_total = length // block_len

    def split_blocks(tensor):
        return tensor.reshape((blocks_total, block_len) + tensor.shape[1:])
    initial = jnp.zeros((values.shape[1], values.shape[2], keys.shape[1]), values.dtype)
    carried, outputs = lax.scan(jax.checkpoint(block_step), (initial, jnp.int32(-1)), tuple((split_blocks(tensor) for tensor in (values, keys, queries, steps, rates, block_ids))))
    return outputs.reshape(values.shape)

def mixer_layer(resid, norm_row, zx_matrix, bc_matrix, dt_matrix, dt_offset, decay_log, skip_row, xconv_taps, xconv_bias, bconv_taps, bconv_bias, gate_row, out_matrix, segment_ids):
    seq_len = resid.shape[0]
    inv_root = lax.rsqrt(lax.optimization_barrier(jnp.mean(resid * resid, axis=1, keepdims=True)) + EPSILON)
    normed = low(resid * inv_root * norm_row[None, :])
    projected = low_back(jnp.einsum('td,dki->tki', normed, zx_matrix, precision=PRECISE))
    bc_raw = low_back(jnp.dot(normed, bc_matrix, precision=PRECISE))
    dt_raw = low_back(jnp.dot(normed, dt_matrix, precision=PRECISE))
    taps = xconv_taps.shape[0]
    conv_in = jnp.concatenate([projected[:, 1], bc_raw], axis=1)
    extended = jnp.concatenate([jnp.zeros((taps - 1, conv_in.shape[1]), conv_in.dtype), conv_in], axis=0)
    extended_ids = jnp.concatenate([jnp.full((taps - 1,), -1, jnp.int32), segment_ids.astype(jnp.int32)])
    activated = convolve(extended, jnp.concatenate([xconv_taps, bconv_taps], axis=1), jnp.concatenate([xconv_bias, bconv_bias]), extended_ids)
    values = low(activated[:, :INNER]).reshape(seq_len, HEADS, HEAD_DIM)
    keys = low(activated[:, INNER:INNER + STATE])
    queries = low(activated[:, INNER + STATE:])
    steps = jax.nn.softplus(dt_raw + dt_offset[None, :])
    rates = -steps * jnp.exp(decay_log)[None, :]
    mixed = state_space(values, keys, queries, steps, rates, segment_ids.astype(jnp.int32))
    mixed = mixed + skip_row[None, :, None] * values
    gated = mixed.reshape(seq_len, INNER) * jax.nn.silu(projected[:, 0])
    gate_root = lax.rsqrt(lax.optimization_barrier(jnp.mean(gated * gated, axis=1, keepdims=True)) + EPSILON)
    scaled = low(gated * gate_root * gate_row[None, :])
    branch = low_back(jnp.dot(scaled, out_matrix, precision=PRECISE))
    return resid + branch

def reference(hidden_in, cotangent, segment_ids, norm_gain, weight_zx, weight_bc, weight_dt, dt_bias, a_log, skip_scale, conv_x, conv_x_bias, conv_bc, conv_bc_bias, gate_gain, weight_out):
    weight_list = tuple((tensor.astype(jnp.float32) for tensor in (norm_gain, weight_zx, weight_bc, weight_dt, dt_bias, a_log, skip_scale, conv_x, conv_x_bias, conv_bc, conv_bc_bias, gate_gain, weight_out)))

    def forward(resid, *parameters):
        for layer_index in range(LAYERS):
            resid = mixer_layer(resid, *[parameter[layer_index] for parameter in parameters], segment_ids)
        return resid
    result, pullback = jax.vjp(forward, hidden_in.astype(jnp.float32), *weight_list)
    gradients = pullback(cotangent.astype(jnp.float32))
    return (result.astype(jnp.bfloat16), gradients[0].astype(jnp.bfloat16), gradients[1], gradients[2], gradients[3], gradients[4], gradients[5], gradients[6], gradients[7], gradients[8], gradients[9], gradients[10], gradients[11], gradients[12], gradients[13])
```

```python
import types

import jax
import jax.numpy as jnp
from jax import lax
from jax.experimental import pallas as pl
from jax.experimental.pallas import tpu as pltpu
from jax.sharding import Mesh
from jax.sharding import PartitionSpec as P

D = 2048
INNER = 4096
IL = 1024
TOK = 128
ST = 128
HL = 16
NS = 32
NX = 4
HALO = 16
SEQ = ("z", "y", "c")
EPS = 1e-05
F32 = jnp.float32
BF = jnp.bfloat16
MESH = pl.DeviceIdType.MESH
WIDE, NARROW = 1024, 768


def dot(a, b, ca, cb):
    return lax.dot_general(a, b, (((ca,), (cb,)), ((), ())), preferred_element_type=F32)


def nn(a, b):
    return dot(a, b, 1, 0)


def nt(a, b):
    return dot(a, b, 1, 1)


def tn(a, b):
    return dot(a, b, 0, 0)


def pieces(a, count):
    out = []
    for _ in range(count):
        p = a.astype(BF)
        out.append(p)
        a = a - p.astype(F32)
    return out


def split_left(f, a, exact, count=2):
    return sum(f(p, exact) for p in pieces(a, count))


def split_right(f, exact, a, count=2):
    return sum(f(exact, p) for p in pieces(a, count))


def sigmoid(v):
    return 1.0 / (1.0 + jnp.exp(-v))


def seq_at(s):
    return {"z": s // 8, "y": lax.rem(s // 2, 4), "c": lax.rem(s, 2)}


def position():
    return lax.axis_index("z") * 8 + lax.axis_index("y") * 2 + lax.axis_index("c")


def lanes(j, width=128, base=0):
    return pl.ds(pl.multiple_of(base + j * width, 128), width)


def wait_for(ref, sem):
    pltpu.make_async_copy(ref, ref, sem).wait()


IN = dict(
    hid=0, cot=0, idc=0, idr=0, ng=0, gg=0, hp=0, ct=0, wzx_h=1, wbc_h=1, wdt_h=1, wout_h=1
)
OUT = dict(
    oh=((TOK, D), BF, 1),
    gi=((TOK, D), BF, 1),
    zx_o=((2, 2, 64, IL), F32, 1),
    out_o=((2, 64, IL), F32, 1),
    bc_o=((2, 64, 256), F32, 1),
    dt_o=((2, 64, 128), F32, 1),
    sums=((NS, 8, 128), F32, 0),
)
SCRATCH = dict(
    wz=((2, 2, 4, 4, 128, IL), BF),
    wb=((2, D, 256), BF),
    wd=((2, HL, D), BF),
    wo=((2, 8, 128, D), BF),
    nrm=((2, HALO + TOK, D), BF),
    dbr0=((TOK, D), BF),
    z=((2, TOK, IL), F32),
    v=((2, HALO + TOK, 1280), F32),
    xbc=((2, TOK, 1280), BF),
    xdt=((2, TOK, IL), BF),
    L=((2, HL, TOK, TOK), BF),
    G=((2, TOK, TOK), F32),
    y=((2, TOK, IL), F32),
    S=((2, IL, ST), BF),
    dtr=((2, TOK, 128), F32),
    dt=((2, TOK, 128), F32),
    rate=((2, TOK, 128), F32),
    cum=((2, TOK, 128), F32),
    entry=((2, TOK, 128), F32),
    wl=((2, TOK, 128), F32),
    dtot=((2, 128, 128), F32),
    q=((2, TOK, 128), F32),
    skE=((2, 8, IL), F32),
    u=((2, 32, D), F32),
    br=((32, D), F32),
    mk=((3, TOK, 128), F32),
    mkb=((3, TOK, 128), F32),
    E=((128, IL), BF),
    Et=((IL, 128), BF),
    tri=((TOK, TOK), BF),
    sb=((NS, 48, 128), BF),
    rb=((2, NS, 48, 128), BF),
    eb=((NS, 32, 128), BF),
    sin=((2, NS, 32, 128), BF),
    sbb=((NS, 32, 128), BF),
    rbb=((2, NS, 32, 128), BF),
    lam=((2, NS, 32, 128), BF),
    sq=((2, 8, 128), F32),
    sqx=((2, NX, 8, 128), F32),
    pb=((TOK, D), BF),
    rs=((2, NX, 32, D), BF),
    gs=((TOK, IL), BF),
    ds=((TOK, IL), F32),
    dbc=((TOK, 256), F32),
    dyb=((TOK, IL), BF),
    dye=((TOK, IL), BF),
    U=((TOK, IL), F32),
    rows=((TOK, 128), F32),
    dsk=((8, IL), F32),
    entE=((TOK, IL), F32),
    wlE=((TOK, IL), F32),
    dtE=((TOK, IL), F32),
    dpre=((2, TOK + 8, 1280), F32),
    scol=((TOK, 128), F32),
    du=((32, D), F32),
    edge=((2, 32, D), BF),
    dbp=((TOK, 256), BF),
    bx=((2, NX, TOK, 256), BF),
    ro=((2, TOK, WIDE), BF),
    re=((2, TOK, NARROW), BF),
    nsib=((TOK, D), BF),
    dsib=((TOK, D), BF),
    rsib=((2, TOK, WIDE), BF),
    part=((4, 4, 128, WIDE), BF),
    land=((4, 2, 4, 128, 512), BF),
    total=((128, WIDE), F32),
    sm=((NS, 8, 128), F32),
    smr=((NS, 8, 128), F32),
    smt=((8, 128), F32),
    smx=((NX, 8, 128), F32),
)


class K:
    (
        WZ, WX, WB, WD, WO, ST, EN, SB, EB, SQ, RS, RB, AG, HA, DP, SC, OH, GI, NSIB, DSIB, BX,
        SM, SX, SG, OWN,
    ) = range(25)


class J:
    RX, Y1, Z1, Y2, Z2, OUT, OWN = range(7)


def chain_kernel(*refs):
    R = types.SimpleNamespace(**dict(zip([*IN, *OUT, *SCRATCH, "sem", "jsem"], refs)))
    iz, iy, ic, mx = (lax.axis_index(a) for a in ("z", "y", "c", "x"))
    me = position()
    mine = pl.ds(pl.multiple_of(mx * 32, 32), 32)

    def sem(kind, l, side):
        return R.sem.at[kind, l, side]

    def send(src, dst, s, r, to):
        pltpu.make_async_remote_copy(
            src, dst, s, r, device_id=to, device_id_type=MESH
        ).start()

    def exchange(src, dst, kind, l):
        dst[pl.ds(me, 1)] = src[pl.ds(me, 1)]

        @pl.loop(1, NS)
        def _(k):
            d = lax.rem(me + k, NS)
            send(src.at[d], dst.at[me], sem(kind, l, 0), sem(kind, l, 1), seq_at(d))

    def exchanged(src, dst, kind, l):
        wait_for(dst.at[pl.ds(0, NS - 1)], sem(kind, l, 1))
        wait_for(src.at[pl.ds(0, NS - 1)], sem(kind, l, 0))

    def to_x(make, kind, l):
        for k in (2, 1, 3):
            d = lax.rem(mx + k, NX)
            src, dst = make(d)
            send(src, dst, sem(kind, l, 0), sem(kind, l, 1), {"x": d})

    def from_x(ref, kind, l):
        wait_for(ref, sem(kind, l, 1))
        wait_for(ref, sem(kind, l, 0))

    def scatter_x(dst, kind, l):
        dst[pl.ds(mx, 1)] = R.pb[mine][None]
        to_x(
            lambda d: (R.pb.at[pl.ds(pl.multiple_of(d * 32, 32), 32)], dst.at[mx]), kind, l
        )

    def neighbour(src, dst, kind, l, step):
        other = me + step

        @pl.when((other >= 0) & (other < NS))
        def _():
            send(src, dst, sem(kind, l, 0), sem(kind, l, 1), seq_at(other))

    def neighbour_done(src, dst, kind, l, step):
        @pl.when((me + step >= 0) & (me + step < NS))
        def _():
            wait_for(src, sem(kind, l, 0))

        @pl.when((me - step >= 0) & (me - step < NS))
        def _():
            wait_for(dst, sem(kind, l, 1))

    def to_sibling(src, dst, kind, l):
        send(src, dst, sem(kind, l, 0), sem(kind, l, 1), {"c": 1 - ic})

    def weight(kind, l):
        src, dst = {
            K.WZ: (R.wzx_h.at[l, 0], R.wz.at[l, 0]),
            K.WX: (R.wzx_h.at[l, 1], R.wz.at[l, 1]),
            K.WB: (R.wbc_h.at[l], R.wb.at[l]),
            K.WD: (R.wdt_h.at[l], R.wd.at[l]),
            K.WO: (R.wout_h.at[l], R.wo.at[l]),
        }[kind]
        return pltpu.make_async_copy(src, dst, sem(kind, l, 0))

    for l in (0, 1):
        for kind in (K.WZ, K.WX, K.WB, K.WD, K.WO):
            weight(kind, l).start()

    barrier = pltpu.get_barrier_semaphore()

    @pl.loop(1, NS)
    def _(k):
        pl.semaphore_signal(
            barrier, inc=1, device_id=seq_at(lax.rem(me + k, NS)), device_id_type=MESH
        )

    for k in range(1, NX):
        pl.semaphore_signal(
            barrier, inc=1, device_id={"x": lax.rem(mx + k, NX)}, device_id_type=MESH
        )

    h_of = lax.broadcasted_iota(jnp.int32, (128, IL), 0)
    c_of = lax.broadcasted_iota(jnp.int32, (128, IL), 1)
    R.E[...] = jnp.where(c_of // 64 == h_of, 1.0, 0.0).astype(BF)
    c_of = lax.broadcasted_iota(jnp.int32, (IL, 128), 0)
    h_of = lax.broadcasted_iota(jnp.int32, (IL, 128), 1)
    R.Et[...] = jnp.where(c_of // 64 == h_of, 1.0, 0.0).astype(BF)
    row = lax.broadcasted_iota(jnp.int32, (TOK, TOK), 0)
    col = lax.broadcasted_iota(jnp.int32, (TOK, TOK), 1)
    R.tri[...] = jnp.where(row >= col, 1.0, 0.0).astype(BF)
    own = R.idc[HALO : HALO + TOK]
    for k in range(3):
        j = 3 - k
        R.mk[k] = jnp.where(R.idc[HALO - j : HALO + TOK - j] == own, 1.0, 0.0)
        R.mkb[k] = jnp.where(R.idc[HALO + j : HALO + TOK + j] == own, 1.0, 0.0)
    R.sm[...] = jnp.zeros((NS, 8, 128), F32)
    R.re[1, :, 640:] = jnp.zeros((TOK, 128), BF)
    for l in (0, 1):
        R.skE[l] = split_left(nn, R.hp[l], R.E[...], 3)

    @pl.when(me == 0)
    def _():
        R.nrm[:, 0:HALO] = jnp.zeros((2, HALO, D), BF)

    @pl.when(me == NS - 1)
    def _():
        R.dpre[:, TOK:] = jnp.zeros((2, 8, 1280), F32)

    lo = lax.broadcasted_iota(jnp.int32, (TOK, 128), 1) < 64

    def halves(pair):
        zero = jnp.zeros_like(pair)
        return jnp.where(lo, pair, zero), jnp.where(lo, zero, pair)

    def expand(src, dst):
        parts = pieces(src, 2)
        for j in range(4):
            c = slice(256 * j, 256 * j + 256)
            dst[:, c] = sum(nn(p, R.E[:, c]) for p in parts)

    def mixing(l, h):
        return (R.G[l] * R.L[l, h].astype(F32)).astype(BF)

    def normalize(u, l):
        r = lax.rsqrt(jnp.mean(u * u, axis=1, keepdims=True) + EPS)
        return (u * r * R.ng[l : l + 1, :]).astype(BF)

    def halo(l):
        return R.nrm.at[l, pl.ds(TOK, HALO)], R.nrm.at[l, pl.ds(0, HALO)]

    def project(l):
        weight(K.WZ, l).wait()

        @pl.loop(0, 4)
        def _(j):
            c = lanes(j, 256)
            R.z[l, :, c] = nn(R.nrm[l, HALO:], R.wz[l, 0, :, :, :, c].reshape(D, 256))

        neighbour_done(*halo(l), K.HA, l, 1)
        weight(K.WX, l).wait()

        @pl.loop(0, 4)
        def _(j):
            c = lanes(j, 256)
            R.v[l, :, c] = nn(R.nrm[l], R.wz[l, 1, :, :, :, c].reshape(D, 256))

        weight(K.WB, l).wait()
        R.v[l, :, IL:] = nn(R.nrm[l], R.wb[l])
        weight(K.WD, l).wait()
        wd = jnp.concatenate([R.wd[l], jnp.zeros((128 - HL, D), BF)], axis=0)
        R.dtr[l] = nt(R.nrm[l, HALO:], wd)

    def conv_sum(l, c):
        acc = R.ct[l, 4:5, c] + R.ct[l, 3:4, c] * R.v[l, HALO:, c]
        for k in range(3):
            acc = acc + (R.ct[l, k : k + 1, c] * R.mk[k]) * (
                R.v[l, HALO - 3 + k : HALO + TOK - 3 + k, c]
            )
        return acc

    def convolve(l):
        @pl.loop(0, 10)
        def _(j):
            c = lanes(j)
            acc = conv_sum(l, c)
            R.xbc[l, :, c] = (acc * sigmoid(acc)).astype(BF)

    def steps(l):
        raw = R.dtr[l] + R.hp[l, 0:1]
        dt = jnp.maximum(raw, 0.0) + jnp.log1p(jnp.exp(-jnp.abs(raw)))
        rate = -dt * jnp.exp(R.hp[l, 1:2])
        cum = split_right(nn, R.tri[...], rate, 3)
        R.dt[l] = dt
        R.rate[l] = rate
        R.cum[l] = cum
        flag = jnp.where(own == R.idc[HALO - 1 : HALO], 1.0, 0.0)
        ending = jnp.where(own == R.idc[HALO + TOK - 1 : HALO + TOK], 1.0, 0.0)
        entry = jnp.exp(cum) * flag
        R.entry[l] = entry
        R.wl[l] = jnp.exp(cum[TOK - 1 : TOK] - cum) * ending
        entry_t = entry.T
        heads = lax.broadcasted_iota(jnp.int32, (128, 128), 0) < HL
        R.dtot[l] = jnp.where(
            heads, jnp.broadcast_to(entry_t[:, TOK - 1 : TOK], (128, 128)), 0.0
        )

    def ssd(l):
        b_mat = R.xbc[l, :, IL : IL + ST]
        c_mat = R.xbc[l, :, IL + ST :]
        expand(R.dt[l], R.dtE)
        expand(R.wl[l], R.wlE)

        @pl.loop(0, 8)
        def _(j):
            c = lanes(j)
            xdt = (R.xbc[l, :, c].astype(F32) * R.dtE[:, c]).astype(BF)
            R.xdt[l, :, c] = xdt
            xw = (xdt.astype(F32) * R.wlE[:, c]).astype(BF)
            s = tn(xw, b_mat).astype(BF)
            R.S[l, c, :] = s
            R.sb[pl.ds(4 * j, 4), 0:32] = s.reshape(4, 32, 128)

        upper = lax.broadcasted_iota(jnp.int32, (16, 128), 0) < 8
        for h in range(HL):
            d = R.dtot[l, h : h + 1]
            hi = d.astype(BF).astype(F32)
            tile = jnp.where(
                upper, jnp.broadcast_to(hi, (16, 128)), jnp.broadcast_to(d - hi, (16, 128))
            ).astype(BF)
            R.sb[2 * h, 32:48] = tile
            R.sb[2 * h + 1, 32:48] = tile
        exchange(R.sb, R.rb.at[l], K.ST, l)
        R.G[l] = nt(c_mat, b_mat)
        keep = (own == R.idr[0:1]) & (row >= col)
        cum = R.cum[l]
        cum_t = cum.T
        for h in range(HL):
            spread = cum[:, h : h + 1] - cum_t[h : h + 1, :]
            ell = jnp.where(keep, jnp.exp(jnp.where(keep, spread, 0.0)), 0.0)
            R.L[l, h] = ell.astype(BF)

        @pl.loop(0, 8)
        def _(j):
            c = lanes(j)
            a, b = halves(R.xdt[l, :, c])
            R.y[l, :, c] = nn(mixing(l, 2 * j), a) + nn(mixing(l, 2 * j + 1), b)

    def scan_states(l):
        exchanged(R.sb, R.rb.at[l], K.ST, l)

        def step(b, state):
            R.eb[b] = state.reshape(32, 128).astype(BF)
            tile = R.rb[l, b, 32:48].astype(F32)
            d = tile[0:8] + tile[8:16]
            return state * d[None] + R.rb[l, b, 0:32].astype(F32).reshape(4, 8, 128)

        lax.fori_loop(0, NS, step, jnp.zeros((4, 8, 128), F32))
        exchange(R.eb, R.sin.at[l], K.EN, l)

    def gate(l):
        c_mat = R.xbc[l, :, IL + ST :]
        expand(R.entry[l], R.entE)
        exchanged(R.eb, R.sin.at[l], K.EN, l)

        def block(j, acc):
            c = lanes(j)
            sin = R.sin[l, pl.ds(4 * j, 4)].reshape(128, 128)
            xs = R.xbc[l, :, c].astype(F32)
            y = R.y[l, :, c] + nt(c_mat, sin) * R.entE[:, c] + R.skE[l, 2:3, c] * xs
            R.y[l, :, c] = y
            z = R.z[l, :, c]
            g = y * (z * sigmoid(z))
            gg = g * R.gg[l : l + 1, c]
            R.gs[:, c] = gg.astype(BF)
            if l == 0:
                return (acc[0] + g * g,)
            return (acc[0] + g * g, acc[1] + gg * R.ds[:, c])

        sums = lax.fori_loop(0, 8, block, (jnp.zeros((TOK, 128), F32),) * (l + 1))
        ones = jnp.ones((8, 128), BF)
        parts = [split_right(nt, ones, s, 2) for s in sums]
        if l == 0:
            R.sq[l] = parts[0]
        else:
            at = lax.broadcasted_iota(jnp.int32, (8, 128), 0)
            R.sq[l] = jnp.where(at == 0, parts[0], parts[1])
        R.sqx[l, pl.ds(mx, 1)] = R.sq[l][None]
        to_x(lambda d: (R.sq.at[l], R.sqx.at[l, mx]), K.SQ, l)

    def root(l):
        from_x(R.sqx.at[l, pl.ds(0, 3)], K.SQ, l)
        total = R.sqx[l, 0] + R.sqx[l, 1] + R.sqx[l, 2] + R.sqx[l, 3]
        q = lax.rsqrt(total[0:1] * (1.0 / INNER) + EPS)
        R.q[l] = jnp.broadcast_to(q, (128, 128)).T
        if l == 1:
            R.scol[...] = jnp.broadcast_to(total[1:2], (128, 128)).T

    def project_out(l):
        if l == 0:
            weight(K.WO, l).wait()

        @pl.loop(0, 8)
        def _(j):
            c = lanes(j, 256)
            R.pb[:, c] = nn(R.gs[...], R.wo[l, :, :, c].reshape(IL, 256)).astype(BF)

        scatter_x(R.rs.at[l], K.RS, l)

    def next_resid(l, before):
        from_x(R.rs.at[l, pl.ds(0, 3)], K.RS, l)
        total = sum(R.rs[l, k].astype(F32) for k in range(NX))
        if l == 0:
            R.br[...] = total
        return before + R.q[l, mine][:, 0:1] * total

    def gather_x(ref, kind, l):
        to_x(lambda d: (ref, ref), kind, l)

    def backward_gate(l):
        def block(j, acc):
            c = lanes(j)
            z, y = R.z[l, :, c], R.y[l, :, c]
            xs = R.xbc[l, :, c].astype(F32)
            sg = sigmoid(z)
            silu = z * sg
            g = y * silu
            ds, gain, q = R.ds[:, c], R.gg[l : l + 1, c], R.q[l]
            gq = g * q
            dg = ds * gain * q - gq * (q * q * R.scol[...] * (1.0 / INNER))
            dy = dg * silu
            R.ro[0, :, c] = (dg * y * (sg * (1.0 + z * (1.0 - sg)))).astype(BF)
            R.ro[1, :, c] = (gq * gain).astype(BF)
            R.sm[17 + l, pl.ds(j, 1)] = jnp.sum(ds * gq, axis=0, keepdims=True)
            R.dsk[:, c] = jnp.broadcast_to(
                jnp.sum(dy * xs, axis=0, keepdims=True), (8, 128)
            )
            sk = R.skE[l, 2:3, c]
            dyb = dy.astype(BF)
            dyf = dyb.astype(F32)
            R.dyb[:, c] = dyb
            R.dye[:, c] = (dyf * R.entE[:, c]).astype(BF)
            R.ds[:, c] = sk * dy
            direct = tn(R.dye[:, c], R.xbc[l, :, IL + ST :])
            R.sbb[pl.ds(4 * j, 4)] = direct.astype(BF).reshape(4, 32, 128)
            return acc + split_left(nn, dyf * (y - sk * xs), R.Et[c, :])

        R.rows[...] = lax.fori_loop(0, 8, block, jnp.zeros((TOK, 128), F32))
        exchange(R.sbb, R.rbb.at[l], K.SB, l)

    def backward_local(l):
        b_mat = R.xbc[l, :, IL : IL + ST]
        c_mat = R.xbc[l, :, IL + ST :]

        def block(j, dgram):
            c = lanes(j)
            a, b = halves(R.dyb[:, c])
            R.U[:, c] = tn(mixing(l, 2 * j), a) + tn(mixing(l, 2 * j + 1), b)
            xdt = R.xdt[l, :, c]
            return (
                dgram
                + nt(a, xdt) * R.L[l, 2 * j].astype(F32)
                + nt(b, xdt) * R.L[l, 2 * j + 1].astype(F32)
            )

        dgram = lax.fori_loop(0, 8, block, jnp.zeros((TOK, TOK), F32)).astype(BF)
        sin = R.sin[l].reshape(IL, ST)
        R.dbc[:, ST:] = nn(dgram, b_mat) + nn(R.dye[...], sin)
        R.dbc[:, 0:ST] = tn(dgram, c_mat)
        expand(R.dt[l], R.dtE)
        expand(R.wl[l], R.wlE)

    def scan_back(l):
        exchanged(R.sbb, R.rbb.at[l], K.SB, l)

        def step(i, state):
            b = NS - 1 - i
            R.eb[b] = state.reshape(32, 128).astype(BF)
            tile = R.rb[l, b, 32:48].astype(F32)
            d = tile[0:8] + tile[8:16]
            return state * d[None] + R.rbb[l, b].astype(F32).reshape(4, 8, 128)

        lax.fori_loop(0, NS, step, jnp.zeros((4, 8, 128), F32))
        exchange(R.eb, R.lam.at[l], K.EB, l)

    def backward_state(l):
        b_mat = R.xbc[l, :, IL : IL + ST]
        exchanged(R.eb, R.lam.at[l], K.EB, l)

        def block(j, carry):
            c = lanes(j)
            lam = R.lam[l, pl.ds(4 * j, 4)].reshape(128, 128)
            wl = R.wlE[:, c]
            ut = R.U[:, c] + wl * nt(b_mat, lam)
            xdt = R.xdt[l, :, c].astype(F32)
            R.ds[:, c] += R.dtE[:, c] * ut
            xw = (xdt * wl).astype(BF)
            lamf = lam.astype(F32)
            et = R.Et[c, :]
            sin = R.sin[l, pl.ds(4 * j, 4)].reshape(128, 128).astype(F32)
            return (
                carry[0] + nn(xw, lam),
                carry[1] + split_right(tn, et, lamf * R.S[l, c, :].astype(F32)),
                carry[2] + split_right(tn, et, lamf * sin),
                carry[3] + split_left(nn, xdt * ut, et),
                carry[4] + split_left(nn, R.xbc[l, :, c].astype(F32) * ut, et),
            )

        zero = jnp.zeros((128, 128), F32)
        db, ks, kd, less, ddt = lax.fori_loop(0, 8, block, (zero,) * 5)
        R.dbc[:, 0:ST] += db
        held = split_right(nt, jnp.ones((8, 128), BF), ks + R.dtot[l] * kd)
        last = lax.broadcasted_iota(jnp.int32, (TOK, 128), 0) == TOK - 1
        dcum = R.rows[...] - less + jnp.where(last, held[0:1], 0.0)
        drate = split_right(tn, R.tri[...], dcum, 3)
        ddt = ddt - drate * jnp.exp(R.hp[l, 1:2])
        ddtr = ddt * sigmoid(R.dtr[l] + R.hp[l, 0:1])
        R.re[0, :, 640:] = ddtr.astype(BF)
        at = 4 * l
        R.sm[19, at : at + 1] = jnp.sum(ddtr, axis=0, keepdims=True)
        R.sm[19, at + 1 : at + 2] = jnp.sum(drate * R.rate[l], axis=0, keepdims=True)
        R.sm[19, at + 2 : at + 3] = split_left(nn, R.dsk[...], R.Et[...])[0:1]

    def backward_conv(l):
        def block(c, dact):
            pre = conv_sum(l, c)
            sg = sigmoid(pre)
            R.dpre[l, 0:TOK, c] = dact * (sg * (1.0 + pre * (1.0 - sg)))

        @pl.loop(0, 8)
        def _(j):
            block(lanes(j), R.ds[:, lanes(j)])

        for j in range(2):
            block(pl.ds(IL + 128 * j, 128), R.dbc[:, 128 * j : 128 * j + 128])
        head, tail = R.dpre.at[l, pl.ds(0, 8)], R.dpre.at[l, pl.ds(TOK, 8)]
        neighbour(head, tail, K.DP, l, -1)

        def tap_sums(c):
            dpre = R.dpre[l, 0:TOK, c]
            out = []
            for k in range(3):
                shifted = R.v[l, HALO - 3 + k : HALO + TOK - 3 + k, c]
                out.append(jnp.sum(dpre * shifted * R.mk[k], axis=0, keepdims=True))
            out.append(jnp.sum(dpre * R.v[l, HALO:, c], axis=0, keepdims=True))
            return [*out, jnp.sum(dpre, axis=0, keepdims=True)]

        @pl.loop(0, 8)
        def _(j):
            for k, s in enumerate(tap_sums(lanes(j))):
                R.sm[7 + 5 * l + k, pl.ds(j, 1)] = s

        for j in range(2):
            for k, s in enumerate(tap_sums(pl.ds(IL + 128 * j, 128))):
                at = 12 * l + 2 * k + j
                R.sm[4 + at // 8, at % 8 : at % 8 + 1] = s
        neighbour_done(head, tail, K.DP, l, -1)

        def back(c):
            out = R.ct[l, 3:4, c] * R.dpre[l, 0:TOK, c]
            for k in range(3):
                out = out + (R.ct[l, k : k + 1, c] * R.mkb[k]) * (
                    R.dpre[l, 3 - k : TOK + 3 - k, c]
                )
            return out.astype(BF)

        for j in range(2):
            R.dbp[:, 128 * j : 128 * j + 128] = back(pl.ds(IL + 128 * j, 128))
        R.bx[l, pl.ds(mx, 1)] = R.dbp[...][None]
        to_x(lambda d: (R.dbp, R.bx.at[l, mx]), K.BX, l)

        @pl.loop(0, 8)
        def _(j):
            R.re[j // 4, :, lanes(lax.rem(j, 4))] = back(lanes(j))

    def sum_bc(l):
        from_x(R.bx.at[l, pl.ds(0, 3)], K.BX, l)
        both = sum(R.bx[l, k].astype(F32) for k in range(NX)).astype(BF)
        R.re[0, :, 512:640] = both[:, 0:128]
        R.re[1, :, 512:640] = both[:, 128:256]

    def backward_project(l):
        @pl.loop(0, 8)
        def _(j):
            rows = pl.ds(2 * lax.rem(j, 2), 2)
            wz = R.wz[l, 0, j // 2, rows].reshape(256, IL)
            wx = R.wz[l, 1, j // 2, rows].reshape(256, IL)
            c = lanes(j, 256)
            part = nt(R.ro[0], wz)
            part += nt(R.re[0, :, 0:512], wx[:, 0:512])
            part += nt(R.re[1, :, 0:512], wx[:, 512:])
            part += nt(R.dbp[...], R.wb[l, c, :])
            part += nn(R.re[0, :, 640 : 640 + HL], R.wd[l, :, c])
            R.pb[:, c] = part.astype(BF)

        scatter_x(R.rs.at[1 - l], K.RB, l)

    def backward_norm(l, above):
        from_x(R.rs.at[1 - l, pl.ds(0, 3)], K.RB, l)
        dn = sum(R.rs[1 - l, k].astype(F32) for k in range(NX))
        u = R.u[l]
        r = lax.rsqrt(jnp.mean(u * u, axis=1, keepdims=True) + EPS)
        gw = dn * R.ng[l : l + 1, :]
        gain = jnp.sum(dn * u * r, axis=0, keepdims=True)
        for i in range(16):
            R.sm[2 * l + i // 8, i % 8 : i % 8 + 1] = gain[:, 128 * i : 128 * i + 128]
        s = jnp.sum(gw * u, axis=1, keepdims=True) * (1.0 / D)
        return above + gw * r - u * (r * r * r * s)

    def back_scaled(l, src):
        @pl.loop(0, 4)
        def _(j):
            R.ds[:, lanes(j, 256)] = nt(src[...], R.wo[l, pl.ds(2 * j, 2)].reshape(256, D))

    def job(n):
        wide = n % 2 == 0
        half = (WIDE if wide else NARROW) // 2
        part = (R.part, R.wz.at[1, 0], R.part, R.wz.at[0, 0])[n]
        if n == 1:
            return part, half, lambda a, p: R.wz.at[
                1, 1, 2 * a + p // 2, :, :, lanes(lax.rem(p, 2), 512)
            ].at[:, :, pl.ds(0, half)]
        space = (R.wo.at[1], None, R.wo.at[1], R.wo.at[0])[n]
        return part, half, lambda a, p: space.at[
            pl.ds(4 * a, 4), :, pl.ds(pl.multiple_of(512 * p, 128), half)
        ]

    def jsem(n, kind, side):
        return R.jsem.at[n, kind, side]

    def job_rhs(n):
        src = R.ro if n % 2 == 0 else R.re
        dst = R.rsib.at[n % 2, :, pl.ds(0, WIDE if n % 2 == 0 else NARROW)]
        send(src.at[1 - ic], dst, jsem(n, J.RX, 0), jsem(n, J.RX, 1), {"c": 1 - ic})

    def job_product(n, l, lhs_own, lhs_sib):
        part, half, _ = job(n)
        src = R.ro if n % 2 == 0 else R.re

        @pl.loop(0, 4)
        def _(b):
            c = lanes(b, 512)
            left = jnp.concatenate([lhs_own(c), lhs_sib[:, c]], axis=0).T
            for k in range(2 * half // 256):
                w = slice(256 * k, 256 * k + 256)
                right = jnp.concatenate([src[ic, :, w], R.rsib[n % 2, :, w]], axis=0)
                part[b, :, :, w] = nn(left, right).astype(BF).reshape(4, 128, 256)

    def job_rhs_done(n):
        width = WIDE if n % 2 == 0 else NARROW
        ref = R.rsib.at[n % 2, :, pl.ds(0, width)]
        wait_for(ref, jsem(n, J.RX, 1))
        wait_for(ref, jsem(n, J.RX, 0))

    def job_multiply(n, l):
        job_rhs_done(n)

        def by_norm(c):
            return R.nrm[l, HALO:, c]

        if n % 2:
            job_product(n, l, by_norm, R.nsib)
            return
        branch = R.cot if l == 1 else R.dbr0

        @pl.when(ic == 0)
        def _():
            job_product(n, l, by_norm, R.nsib)

        @pl.when(ic == 1)
        def _():
            job_product(n, l, lambda c: branch[:, c], R.dsib)

    def job_send1(n):
        part, half, land = job(n)
        for k in (2, 1, 3):
            d = lax.rem(iy + k, 4)
            send(
                part.at[:, d, :, pl.ds(0, half)], land(0, iy),
                jsem(n, J.Y1, 0), jsem(n, J.Y1, 1), {"y": d},
            )
            d = lax.rem(iz + k, 4)
            send(
                part.at[d, :, :, pl.ds(half, half)], land(1, iz),
                jsem(n, J.Z1, 0), jsem(n, J.Z1, 1), {"z": d},
            )

    def job_sum1(n):
        part, half, land = job(n)
        three = part.at[pl.ds(0, 3), :, :, pl.ds(0, half)]
        wait_for(three, jsem(n, J.Y1, 1))
        wait_for(three, jsem(n, J.Y1, 0))
        slots = [land(0, lax.rem(iy + k, 4)) for k in (1, 2, 3)]

        @pl.loop(0, 4)
        def _(b):
            for w in range(0, half, 128):
                w = slice(w, w + 128)
                s = part[b, iy, :, w].astype(F32)
                for slot in slots:
                    s = s + slot[b, :, w].astype(F32)
                part[b, iy, :, w] = s.astype(BF)

        for k in (2, 1, 3):
            d = lax.rem(iz + k, 4)
            send(
                part.at[d, iy, :, pl.ds(0, half)], R.land.at[n, 0, iz, :, pl.ds(0, half)],
                jsem(n, J.Y2, 0), jsem(n, J.Y2, 1), {"z": d},
            )
        wait_for(three, jsem(n, J.Z1, 1))
        wait_for(three, jsem(n, J.Z1, 0))
        slots = [land(1, lax.rem(iz + k, 4)) for k in (1, 2, 3)]

        @pl.loop(0, 4)
        def _(b):
            for w in range(0, half, 128):
                at, w = slice(half + w, half + w + 128), slice(w, w + 128)
                s = part[iz, b, :, at].astype(F32)
                for slot in slots:
                    s = s + slot[b, :, w].astype(F32)
                part[iz, b, :, at] = s.astype(BF)

        for k in (2, 1, 3):
            d = lax.rem(iy + k, 4)
            send(
                part.at[iz, d, :, pl.ds(half, half)], R.land.at[n, 1, iy, :, pl.ds(0, half)],
                jsem(n, J.Z2, 0), jsem(n, J.Z2, 1), {"y": d},
            )

    def job_outputs(n, half_at, to_self):
        l = 1 - n // 2
        rows = pl.ds(pl.multiple_of(64 * half_at, 64), 64)
        kind = J.OWN if to_self else J.OUT

        def put(columns, dst):
            src = R.total.at[rows, columns]
            if to_self:
                pltpu.make_async_copy(src, dst, jsem(n, kind, 0)).start()
            else:
                send(src, dst, jsem(n, kind, 0), jsem(n, kind, 1), {"c": 1 - ic})

        @pl.when(ic == 0)
        def _():
            if n % 2 == 0:
                put(pl.ds(0, IL), R.zx_o.at[l, 0])
            else:
                put(pl.ds(0, 512), R.zx_o.at[l, 1, :, pl.ds(0, 512)])
                put(pl.ds(512, 128), R.bc_o.at[l, :, pl.ds(0, 128)])
                put(pl.ds(640, 128), R.dt_o.at[l])

        @pl.when(ic == 1)
        def _():
            if n % 2 == 0:
                put(pl.ds(0, IL), R.out_o.at[l])
            else:
                put(pl.ds(0, 512), R.zx_o.at[l, 1, :, pl.ds(512, 512)])
                put(pl.ds(512, 128), R.bc_o.at[l, :, pl.ds(128, 128)])

    def job_sum2(n):
        part, half, _ = job(n)
        three = R.land.at[n, 0, pl.ds(0, 3), :, pl.ds(0, half)]
        for kind in (J.Y2, J.Z2):
            wait_for(three, jsem(n, kind, 1))
            wait_for(three, jsem(n, kind, 0))
        for a, at in ((0, iz), (1, iy)):
            for w in range(0, half, 128):
                here, w = slice(a * half + w, a * half + w + 128), slice(w, w + 128)
                s = part[iz, iy, :, here].astype(F32)
                for k in (1, 2, 3):
                    s = s + R.land[n, a, lax.rem(at + k, 4), :, w].astype(F32)
                R.total[:, here] = s
        job_outputs(n, ic, True)
        job_outputs(n, 1 - ic, False)

    def job_done(n):
        def all_of(width, kind, side):
            wait_for(R.total.at[pl.ds(0, 64), pl.ds(0, width)], jsem(n, kind, side))

        if n % 2 == 0:
            for kind, side in ((J.OWN, 0), (J.OUT, 0), (J.OUT, 1)):
                all_of(IL, kind, side)
            return

        @pl.when(ic == 0)
        def _():
            for kind, side, width in ((J.OWN, 0, 768), (J.OUT, 0, 768), (J.OUT, 1, 640)):
                all_of(width, kind, side)

        @pl.when(ic == 1)
        def _():
            for kind, side, width in ((J.OWN, 0, 640), (J.OUT, 0, 640), (J.OUT, 1, 768)):
                all_of(width, kind, side)

    def sibling_done(ref, kind, l):
        wait_for(ref, sem(kind, l, 1))
        wait_for(ref, sem(kind, l, 0))

    def edge_out(i, dst, value):
        R.edge[i] = value.astype(BF)
        here = dst.at[mine]
        pltpu.make_async_copy(R.edge.at[i], here, sem(K.OWN, i, 0)).start()
        kind = (K.OH, K.GI)[i]
        to_x(lambda d: (R.edge.at[i], here), kind, 0)

    def edge_done(i, dst):
        wait_for(R.edge.at[i], sem(K.OWN, i, 0))
        from_x(dst.at[pl.ds(0, 96)], (K.OH, K.GI)[i], 0)

    @pl.loop(0, 4)
    def _(j):
        rows = pl.ds(pl.multiple_of(j * 32, 32), 32)
        at = pl.ds(pl.multiple_of(HALO + j * 32, 16), 32)
        R.nrm[0, at] = normalize(R.hid[rows].astype(F32), 0)

    R.u[0] = R.hid[mine].astype(F32)
    pl.semaphore_wait(barrier, NS - 1 + NX - 1)
    neighbour(*halo(0), K.HA, 0, 1)
    project(0)
    convolve(0)
    steps(0)
    ssd(0)
    scan_states(0)
    gate(0)
    project_out(0)
    root(0)
    R.u[1] = next_resid(0, R.u[0])
    at = pl.ds(pl.multiple_of(HALO + mx * 32, 16), 32)
    R.nrm[1, at] = normalize(R.u[1], 1)
    gather_x(R.nrm.at[1, at], K.AG, 1)
    from_x(R.nrm.at[1, pl.ds(HALO, 96)], K.AG, 1)
    neighbour(*halo(1), K.HA, 1, 1)
    project(1)
    convolve(1)
    steps(1)
    ssd(1)
    to_sibling(R.nrm.at[1, pl.ds(HALO, TOK)], R.nsib, K.NSIB, 1)
    to_sibling(R.cot, R.dsib, K.DSIB, 1)
    weight(K.WO, 1).wait()
    back_scaled(1, R.cot)
    scan_states(1)
    gate(1)
    project_out(1)
    root(1)
    backward_gate(1)
    job_rhs(0)
    edge_out(0, R.oh, next_resid(1, R.u[1]))
    backward_local(1)
    scan_back(1)
    sibling_done(R.nsib, K.NSIB, 1)
    sibling_done(R.dsib, K.DSIB, 1)
    job_multiply(0, 1)
    job_send1(0)
    backward_state(1)
    backward_conv(1)
    backward_project(1)
    sum_bc(1)
    job_rhs(1)
    job_multiply(1, 1)
    R.du[...] = backward_norm(1, R.cot[mine].astype(F32))
    R.dbr0[mine] = R.du[...].astype(BF)
    gather_x(R.dbr0.at[mine], K.AG, 0)
    s = jnp.sum(R.du[...].astype(BF).astype(F32) * R.br[...], axis=1, keepdims=True)
    R.scol[mine] = jnp.broadcast_to(s, (32, 128))
    gather_x(R.scol.at[mine], K.SC, 0)
    edge_done(0, R.oh)
    from_x(R.dbr0.at[pl.ds(0, 96)], K.AG, 0)
    back_scaled(0, R.dbr0)
    from_x(R.scol.at[pl.ds(0, 96)], K.SC, 0)
    expand(R.entry[0], R.entE)
    backward_gate(0)
    backward_local(0)
    job_sum1(0)
    scan_back(0)
    job_rhs(2)
    to_sibling(R.nrm.at[0, pl.ds(HALO, TOK)], R.nsib, K.NSIB, 0)
    to_sibling(R.dbr0, R.dsib, K.DSIB, 0)
    job_send1(1)
    job_sum2(0)
    sibling_done(R.nsib, K.NSIB, 0)
    sibling_done(R.dsib, K.DSIB, 0)
    job_multiply(2, 0)
    backward_state(0)
    job_send1(2)
    backward_conv(0)
    backward_project(0)
    sum_bc(0)
    job_rhs(3)
    job_multiply(3, 0)
    job_send1(3)
    edge_out(1, R.gi, backward_norm(0, R.du[...]))
    exchange(R.sm, R.smr, K.SM, 0)
    job_sum1(1)
    job_sum1(2)
    exchanged(R.sm, R.smr, K.SM, 0)
    mine_sum = sum(R.smr[k] for k in range(NS))
    R.smt[...] = mine_sum
    R.smx[pl.ds(mx, 1)] = mine_sum[None]
    to_x(lambda d: (R.smt, R.smx.at[mx]), K.SX, 0)
    job_done(0)
    job_sum2(1)
    from_x(R.smx.at[pl.ds(0, 3)], K.SX, 0)
    over_x = R.smx[0] + R.smx[1] + R.smx[2] + R.smx[3]
    R.smt[...] = jnp.where(me < 7, over_x, R.smt[...])
    R.sums[pl.ds(me, 1)] = R.smt[...][None]

    @pl.loop(1, NS)
    def _(k):
        send(
            R.smt, R.sums.at[me], sem(K.SG, 0, 0), sem(K.SG, 0, 1), seq_at(lax.rem(me + k, NS))
        )

    job_sum1(3)
    job_done(1)
    job_sum2(2)
    job_done(2)
    job_sum2(3)
    wait_for(R.sums.at[pl.ds(0, NS - 1)], sem(K.SG, 0, 1))
    wait_for(R.sums.at[pl.ds(0, NS - 1)], sem(K.SG, 0, 0))
    edge_done(1, R.gi)
    job_done(3)


def chain(*args):
    vmem = pl.BlockSpec(memory_space=pltpu.VMEM)
    held = pl.BlockSpec(memory_space=pl.ANY)
    return pl.pallas_call(
        chain_kernel,
        out_shape=[jax.ShapeDtypeStruct(s, t) for s, t, _ in OUT.values()],
        in_specs=[held if far else vmem for far in IN.values()],
        out_specs=[held if far else vmem for _, _, far in OUT.values()],
        scratch_shapes=[pltpu.VMEM(s, t) for s, t in SCRATCH.values()]
        + [pltpu.SemaphoreType.DMA((25, 2, 2)), pltpu.SemaphoreType.DMA((4, 7, 2))],
        compiler_params=pltpu.CompilerParams(
            collective_id=1, has_side_effects=True, vmem_limit_bytes=64 * 2**20
        ),
        name="chain",
    )(*args)


def local(
    hidden_in, cotangent, segment_ids, norm_gain, weight_zx, weight_bc, weight_dt, dt_bias, a_log,
    skip_scale, conv_x, conv_x_bias, conv_bc, conv_bc_bias, gate_gain, weight_out,
):
    me = position()
    padded = jnp.concatenate(
        [jnp.full((HALO,), -1, jnp.int32), segment_ids, jnp.full((HALO,), -2, jnp.int32)]
    )
    ids = lax.dynamic_slice_in_dim(padded, me * TOK, TOK + 2 * HALO)
    idc = jnp.broadcast_to(ids[:, None], (TOK + 2 * HALO, 128))
    idr = jnp.broadcast_to(ids[None, HALO : HALO + TOK], (8, 128))
    hp = jnp.pad(jnp.stack([dt_bias, a_log, skip_scale], axis=1), ((0, 0), (0, 5), (0, 128 - HL)))
    ct = jnp.concatenate(
        [
            jnp.concatenate([conv_x, conv_bc], axis=2),
            jnp.concatenate([conv_x_bias, conv_bc_bias], axis=1)[:, None],
            jnp.zeros((2, 3, 1280), F32),
        ],
        axis=1,
    )
    oh, gi, zx, out, bc, dt, sums = chain(
        hidden_in, cotangent, idc, idr, norm_gain, gate_gain, hp, ct,
        jnp.swapaxes(weight_zx, 1, 2).reshape(2, 2, 4, 4, 128, IL), weight_bc,
        jnp.swapaxes(weight_dt, 1, 2), weight_out.reshape(2, 8, 128, D),
    )
    norms = sums[0:4].reshape(2, D)
    by_bc = sums[4:7].reshape(2, 12, 128)[:, :10].reshape(2, 5, 256)
    by_x = sums[7:17].reshape(2, 5, IL)
    heads = sums[19].reshape(2, 4, 128)[:, :, :HL]
    return (
        oh, gi, lax.dynamic_slice_in_dim(norms, me * 64, 64, axis=1), jnp.swapaxes(zx, 1, 2), bc,
        dt[:, :, :HL], heads[:, 0], heads[:, 1], heads[:, 2], by_x[:, :4], by_x[:, 4],
        by_bc[:, :4], by_bc[:, 4], sums[17:19].reshape(2, IL), jnp.swapaxes(out, 1, 2),
    )


def solution(mesh):
    finer = Mesh(mesh.devices.reshape(4, 4, 2, 4), ("z", "y", "c", "x"))
    in_specs = (
        P(SEQ, None), P(SEQ, None), P(), P(), P(None, None, None, "x"), P(), P(None, None, "x"),
        P(None, "x"), P(None, "x"), P(None, "x"), P(None, None, "x"), P(None, "x"), P(), P(),
        P(None, "x"), P(None, "x", None),
    )
    out_specs = (
        P(SEQ, None), P(SEQ, None), P(None, SEQ), P(None, SEQ, None, "x"), P(None, SEQ, None),
        P(None, SEQ, "x"), P(None, "x"), P(None, "x"), P(None, "x"), P(None, None, "x"),
        P(None, "x"), P(), P(), P(None, "x"), P(None, "x", SEQ),
    )
    return jax.shard_map(local, mesh=finer, in_specs=in_specs, out_specs=out_specs, check_vma=False)
```

```python
import types

import jax
import jax.numpy as jnp
from jax import lax
from jax.experimental import pallas as pl
from jax.experimental.pallas import tpu as pltpu
from jax.sharding import Mesh
from jax.sharding import PartitionSpec as P

D = 2048
INNER = 4096
IL = 1024
TOK = 128
ST = 128
HL = 16
NS = 32
NX = 4
HALO = 16
SEQ = ("z", "y", "c")
EPS = 1e-05
F32 = jnp.float32
BF = jnp.bfloat16
MESH = pl.DeviceIdType.MESH
WIDE, NARROW = 1024, 768


def dot(a, b, ca, cb):
    return lax.dot_general(a, b, (((ca,), (cb,)), ((), ())), preferred_element_type=F32)


def nn(a, b):
    return dot(a, b, 1, 0)


def nt(a, b):
    return dot(a, b, 1, 1)


def tn(a, b):
    return dot(a, b, 0, 0)


def pieces(a, count):
    out = []
    for _ in range(count):
        p = a.astype(BF)
        out.append(p)
        a = a - p.astype(F32)
    return out


def split_left(f, a, exact, count=2):
    return sum(f(p, exact) for p in pieces(a, count))


def split_right(f, exact, a, count=2):
    return sum(f(exact, p) for p in pieces(a, count))


def sigmoid(v):
    return 1.0 / (1.0 + jnp.exp(-v))


def seq_at(s):
    return {"z": s // 8, "y": lax.rem(s // 2, 4), "c": lax.rem(s, 2)}


def position():
    return lax.axis_index("z") * 8 + lax.axis_index("y") * 2 + lax.axis_index("c")


def lanes(j, width=128, base=0):
    return pl.ds(pl.multiple_of(base + j * width, 128), width)


def wait_for(ref, sem):
    pltpu.make_async_copy(ref, ref, sem).wait()


IN = dict(
    hid=1, cot=0, seg=0, ng=0, gg=0, dtb=0, alog=0, skip=0, cx=0, cxb=0, cbc=0, cbcb=0,
    wzx_h=1, wbc_h=1, wdt_h=1, wout_h=1,
)
OUT = dict(
    oh=((TOK, D), BF, 1),
    gi=((TOK, D), BF, 1),
    zx_o=((2, 64, 2, IL), F32, 1),
    out_o=((2, 64, IL), F32, 1),
    bc_o=((2, 64, 256), F32, 1),
    dt_o=((2, 64, 128), F32, 1),
    sums=((NS, 8, 128), F32, 0),
)
SCRATCH = dict(
    wz=((2, D, 2, IL), BF),
    wb=((2, D, 256), BF),
    wd=((2, HL, D), BF),
    wo=((2, 8, 128, D), BF),
    nrm=((2, HALO + TOK, D), BF),
    dbr0=((TOK, D), BF),
    z=((2, TOK, IL), F32),
    v=((2, HALO + TOK, 1280), F32),
    xbc=((2, TOK, 1280), BF),
    xdt=((2, TOK, IL), BF),
    L=((2, HL, TOK, TOK), BF),
    G=((2, TOK, TOK), F32),
    y=((2, TOK, IL), F32),
    S=((2, IL, ST), BF),
    dtr=((2, TOK, 128), F32),
    dt=((2, TOK, 128), F32),
    rate=((2, TOK, 128), F32),
    cum=((2, TOK, 128), F32),
    entry=((2, TOK, 128), F32),
    wl=((2, TOK, 128), F32),
    dtot=((2, 128, 128), F32),
    q=((2, TOK, 128), F32),
    skE=((2, 8, IL), F32),
    u=((2, 32, D), F32),
    br=((32, D), F32),
    mk=((3, TOK, 128), F32),
    mkb=((3, TOK, 128), F32),
    E=((128, IL), BF),
    Et=((IL, 128), BF),
    tri=((TOK, TOK), BF),
    sb=((NS, 48, 128), BF),
    rb=((2, NS, 48, 128), BF),
    eb=((NS, 32, 128), BF),
    sin=((2, NS, 32, 128), BF),
    rbb=((NS, 32, 128), BF),
    lam=((NS, 32, 128), BF),
    sq=((2, 8, 128), F32),
    sqx=((2, NX, 8, 128), F32),
    pb=((TOK, D), BF),
    rs=((2, NX, 32, D), BF),
    ds=((TOK, IL), F32),
    dbc=((TOK, 256), F32),
    dyb=((TOK, IL), BF),
    dye=((TOK, IL), BF),
    U=((8, TOK, 128), F32),
    rows=((TOK, 128), F32),
    dsk=((8, IL), F32),
    dpre=((2, TOK + 8, 1280), F32),
    scol=((TOK, 128), F32),
    du=((32, D), F32),
    edge=((2, 32, D), BF),
    dbp=((TOK, 256), BF),
    bx=((NX, TOK, 256), BF),
    ro=((2, TOK, WIDE), BF),
    re=((2, TOK, NARROW), BF),
    idc=((TOK + 2 * HALO, 128), F32),
    hp=((2, 8, 128), F32),
    ct=((2, 8, 1280), F32),
    nx=((17, 16, 2 * D), BF),
    pick=((128, 512), BF),
    nbt=((4, 4, 128, 128), BF),
    dbt=((4, 4, 128, 128), BF),
    nl=((2, 2, 4, 128, 1024), BF),
    dl=((2, 2, 4, 128, 1024), BF),
    land=((3, 2, 4, 8, 16, 512), BF),
    total=((2, 128, WIDE), F32),
    x2t=((IL, 256), BF),
    sm=((NS, 8, 128), F32),
    smr=((NS, 8, 128), F32),
    smt=((8, 128), F32),
    smx=((NX, 8, 128), F32),
)


class K:
    (
        HID, WZ, WB, WD, WO, ST, EN, SB, EB, SQ, RS, RB, AG, HA, DP, SC, OH, GI, NY, NZ, DY, DZ,
        FY, FZ, BX, SM, SX, SG, OWN,
    ) = range(29)


class J:
    Y1, Z1, Y2, Z2, OUT, OWN = range(6)


def chain_kernel(*refs):
    R = types.SimpleNamespace(**dict(zip([*IN, *OUT, *SCRATCH, "sem", "jsem"], refs)))
    iz, iy, ic, mx = (lax.axis_index(a) for a in ("z", "y", "c", "x"))
    R.sbb = R.sb.at[:, pl.ds(0, 32)]
    me = position()
    mine = pl.ds(pl.multiple_of(mx * 32, 32), 32)

    def sem(kind, l, side):
        return R.sem.at[kind, l, side]

    def send(src, dst, s, r, to):
        pltpu.make_async_remote_copy(
            src, dst, s, r, device_id=to, device_id_type=MESH
        ).start()

    def exchange(src, dst, kind, l):
        dst[pl.ds(me, 1)] = src[pl.ds(me, 1)]

        @pl.loop(1, NS)
        def _(k):
            d = lax.rem(me + k, NS)
            send(src.at[d], dst.at[me], sem(kind, l, 0), sem(kind, l, 1), seq_at(d))

    def exchanged(src, dst, kind, l):
        wait_for(dst.at[pl.ds(0, NS - 1)], sem(kind, l, 1))
        wait_for(src.at[pl.ds(0, NS - 1)], sem(kind, l, 0))

    def to_x(make, kind, l):
        for k in (2, 1, 3):
            d = lax.rem(mx + k, NX)
            src, dst = make(d)
            send(src, dst, sem(kind, l, 0), sem(kind, l, 1), {"x": d})

    def from_x(ref, kind, l):
        wait_for(ref, sem(kind, l, 1))
        wait_for(ref, sem(kind, l, 0))

    def scatter_x(dst, kind, l, piece):
        c = pl.ds(512 * piece, 512)
        dst[mx, :, c] = R.pb[mine, c]
        to_x(
            lambda d: (
                R.pb.at[pl.ds(pl.multiple_of(d * 32, 32), 32), c], dst.at[mx, :, c]
            ),
            kind, l,
        )

    def neighbour(src, dst, kind, l, step):
        other = me + step

        @pl.when((other >= 0) & (other < NS))
        def _():
            send(src, dst, sem(kind, l, 0), sem(kind, l, 1), seq_at(other))

    def neighbour_done(src, dst, kind, l, step):
        @pl.when((me + step >= 0) & (me + step < NS))
        def _():
            wait_for(src, sem(kind, l, 0))

        @pl.when((me - step >= 0) & (me - step < NS))
        def _():
            wait_for(dst, sem(kind, l, 1))

    def weight(kind, l):
        src, dst = {
            K.WZ: (R.wzx_h.at[l], R.wz.at[l]),
            K.WB: (R.wbc_h.at[l], R.wb.at[l]),
            K.WD: (R.wdt_h.at[l], R.wd.at[l]),
            K.WO: (R.wout_h.at[l], R.wo.at[l]),
        }[kind]
        return pltpu.make_async_copy(src, dst, sem(kind, l, 0))

    resid_in = pltpu.make_async_copy(R.hid, R.pb, sem(K.HID, 0, 0))
    resid_in.start()
    for l in (0, 1):
        for kind in (K.WZ, K.WB, K.WD, K.WO):
            weight(kind, l).start()

    barrier = pltpu.get_barrier_semaphore()

    @pl.loop(1, NS)
    def _(k):
        pl.semaphore_signal(
            barrier, inc=1, device_id=seq_at(lax.rem(me + k, NS)), device_id_type=MESH
        )

    for k in range(1, NX):
        pl.semaphore_signal(
            barrier, inc=1, device_id={"x": lax.rem(mx + k, NX)}, device_id_type=MESH
        )

    last_x = mx == NX - 1

    @pl.when(last_x & (me < NS - 1))
    def _():
        for k in range(NX - 1):
            pl.semaphore_signal(
                barrier, inc=1, device_id={**seq_at(me + 1), "x": k}, device_id_type=MESH
            )

    @pl.when((mx < NX - 1) & (me > 0))
    def _():
        pl.semaphore_signal(
            barrier, inc=1, device_id={**seq_at(me - 1), "x": NX - 1}, device_id_type=MESH
        )

    def everyone_is_here():
        has_next, has_prev = 1 - (me + 1) // NS, (me + NS - 1) // NS
        at_end = mx // (NX - 1)
        pl.semaphore_wait(
            barrier, NS - 1 + NX - 1 + at_end * has_next * (NX - 1) + (1 - at_end) * has_prev
        )

    def ids_of(s):
        return jnp.broadcast_to(R.seg[pl.ds(s, 1)].astype(F32), (128, 128))

    R.idc[HALO : HALO + TOK] = ids_of(me).T
    R.idc[0:HALO] = jnp.where(me == 0, -1.0, ids_of(lax.rem(me + NS - 1, NS)).T[TOK - HALO :])
    R.idc[HALO + TOK :] = jnp.where(me == NS - 1, -2.0, ids_of(lax.rem(me + 1, NS)).T[0:HALO])
    R.hp[...] = jnp.zeros((2, 8, 128), F32)
    R.ct[...] = jnp.zeros((2, 8, 1280), F32)
    for l in (0, 1):
        for i, ref in enumerate((R.dtb, R.alog, R.skip)):
            R.hp[l, i : i + 1, 0:HL] = ref[l : l + 1]
        R.ct[l, 0:4, 0:IL] = R.cx[l]
        R.ct[l, 0:4, IL:] = R.cbc[l]
        R.ct[l, 4:5, 0:IL] = R.cxb[l : l + 1]
        R.ct[l, 4:5, IL:] = R.cbcb[l : l + 1]
    r_of = lax.broadcasted_iota(jnp.int32, (128, 512), 0)
    c_of = lax.broadcasted_iota(jnp.int32, (128, 512), 1)
    R.pick[...] = jnp.where((c_of == 2 * r_of) | (c_of == 2 * r_of + 257), 1.0, 0.0).astype(BF)
    h_of = lax.broadcasted_iota(jnp.int32, (128, IL), 0)
    c_of = lax.broadcasted_iota(jnp.int32, (128, IL), 1)
    R.E[...] = jnp.where(c_of // 64 == h_of, 1.0, 0.0).astype(BF)
    c_of = lax.broadcasted_iota(jnp.int32, (IL, 128), 0)
    h_of = lax.broadcasted_iota(jnp.int32, (IL, 128), 1)
    R.Et[...] = jnp.where(c_of // 64 == h_of, 1.0, 0.0).astype(BF)
    row = lax.broadcasted_iota(jnp.int32, (TOK, TOK), 0)
    col = lax.broadcasted_iota(jnp.int32, (TOK, TOK), 1)
    R.tri[...] = jnp.where(row >= col, 1.0, 0.0).astype(BF)
    own = R.idc[HALO : HALO + TOK]
    for k in range(3):
        j = 3 - k
        R.mk[k] = jnp.where(R.idc[HALO - j : HALO + TOK - j] == own, 1.0, 0.0)
        R.mkb[k] = jnp.where(R.idc[HALO + j : HALO + TOK + j] == own, 1.0, 0.0)
    R.sm[...] = jnp.zeros((NS, 8, 128), F32)
    R.re[1, :, 640:] = jnp.zeros((TOK, 128), BF)
    for l in (0, 1):
        R.skE[l] = split_left(nn, R.hp[l], R.E[...], 3)

    @pl.when(me == 0)
    def _():
        R.nrm[:, 0:HALO] = jnp.zeros((2, HALO, D), BF)

    @pl.when(me == NS - 1)
    def _():
        R.dpre[:, TOK:] = jnp.zeros((2, 8, 1280), F32)

    lo = lax.broadcasted_iota(jnp.int32, (TOK, 128), 1) < 64

    def halves(pair):
        zero = jnp.zeros_like(pair)
        return jnp.where(lo, pair, zero), jnp.where(lo, zero, pair)

    def expanded(parts, c):
        return sum(nn(p, R.E[:, c]) for p in parts)

    def mixing(l, h):
        return (R.G[l] * R.L[l, h].astype(F32)).astype(BF)

    def normalize(u, l):
        r = lax.rsqrt(jnp.mean(u * u, axis=1, keepdims=True) + EPS)
        return (u * r * R.ng[l : l + 1, :]).astype(BF)

    def halo(l):
        return R.nrm.at[l, pl.ds(TOK, HALO)], R.nrm.at[l, pl.ds(0, HALO)]

    def spread_rows(l, first, rows, at):
        @pl.loop(0, 16, unroll=8)
        def _(j):
            n = R.nrm[l, first : first + rows, lanes(j)]
            if at is None:
                both = nn(n, R.pick[...]).astype(BF)
                R.nx[0:8, :, lanes(j, 256)] = both[:, 0:256].reshape(8, 16, 256)
                R.nx[9:, :, lanes(j, 256)] = both[:, 256:].reshape(8, 16, 256)
            else:
                R.nx[at // 16, :, lanes(j, 256)] = nn(n, R.pick[:, 256:]).astype(BF)

    def halo_done(l):
        if l == 0:
            neighbour_done(*halo(0), K.HA, 0, 1)
            return

        @pl.when(last_x & (me < NS - 1))
        def _():
            four = R.nrm.at[1, pl.ds(0, 4 * HALO)]
            wait_for(four, sem(K.HA, 1, 0))

        @pl.when(me > 0)
        def _():
            wait_for(halo(1)[1], sem(K.HA, 1, 1))

    def project(l):
        spread_rows(l, HALO, TOK, None)
        halo_done(l)
        spread_rows(l, 0, HALO, TOK)
        weight(K.WZ, l).wait()

        @pl.loop(0, 4)
        def _(j):
            c = lanes(j, 256)
            both = nn(R.nx[...].reshape(17 * 16, 2 * D), R.wz[l, :, :, c].reshape(2 * D, 256))
            R.z[l, :, c] = both[0:TOK]
            R.v[l, :, c] = both[TOK:]

        weight(K.WB, l).wait()
        R.v[l, :, IL:] = nn(R.nrm[l], R.wb[l])
        weight(K.WD, l).wait()
        wd = jnp.concatenate([R.wd[l], jnp.zeros((128 - HL, D), BF)], axis=0)
        R.dtr[l] = nt(R.nrm[l, HALO:], wd)

    def conv_sum(l, c):
        acc = R.ct[l, 4:5, c] + R.ct[l, 3:4, c] * R.v[l, HALO:, c]
        for k in range(3):
            acc = acc + (R.ct[l, k : k + 1, c] * R.mk[k]) * (
                R.v[l, HALO - 3 + k : HALO + TOK - 3 + k, c]
            )
        return acc

    def convolve(l):
        @pl.loop(0, 10, unroll=2)
        def _(j):
            c = lanes(j)
            acc = conv_sum(l, c)
            R.xbc[l, :, c] = (acc * sigmoid(acc)).astype(BF)

    def steps(l):
        raw = R.dtr[l] + R.hp[l, 0:1]
        dt = jnp.maximum(raw, 0.0) + jnp.log1p(jnp.exp(-jnp.abs(raw)))
        rate = -dt * jnp.exp(R.hp[l, 1:2])
        cum = split_right(nn, R.tri[...], rate, 3)
        R.dt[l] = dt
        R.rate[l] = rate
        R.cum[l] = cum
        flag = jnp.where(own == R.idc[HALO - 1 : HALO], 1.0, 0.0)
        ending = jnp.where(own == R.idc[HALO + TOK - 1 : HALO + TOK], 1.0, 0.0)
        entry = jnp.exp(cum) * flag
        R.entry[l] = entry
        R.wl[l] = jnp.exp(cum[TOK - 1 : TOK] - cum) * ending
        entry_t = entry.T
        heads = lax.broadcasted_iota(jnp.int32, (128, 128), 0) < HL
        R.dtot[l] = jnp.where(
            heads, jnp.broadcast_to(entry_t[:, TOK - 1 : TOK], (128, 128)), 0.0
        )

    def ssd(l):
        b_mat = R.xbc[l, :, IL : IL + ST]
        c_mat = R.xbc[l, :, IL + ST :]
        dt, wl = pieces(R.dt[l], 2), pieces(R.wl[l], 2)

        @pl.loop(0, 8, unroll=4)
        def _(j):
            c = lanes(j)
            xdt = (R.xbc[l, :, c].astype(F32) * expanded(dt, c)).astype(BF)
            R.xdt[l, :, c] = xdt
            xw = (xdt.astype(F32) * expanded(wl, c)).astype(BF)
            s = tn(xw, b_mat).astype(BF)
            R.S[l, c, :] = s
            R.sb[pl.ds(4 * j, 4), 0:32] = s.reshape(4, 32, 128)

        upper = lax.broadcasted_iota(jnp.int32, (16, 128), 0) < 8
        for h in range(HL):
            d = R.dtot[l, h : h + 1]
            hi = d.astype(BF).astype(F32)
            tile = jnp.where(
                upper, jnp.broadcast_to(hi, (16, 128)), jnp.broadcast_to(d - hi, (16, 128))
            ).astype(BF)
            R.sb[2 * h, 32:48] = tile
            R.sb[2 * h + 1, 32:48] = tile
        exchange(R.sb, R.rb.at[l], K.ST, l)
        R.G[l] = nt(c_mat, b_mat)
        keep = (own == ids_of(me)[0:1]) & (row >= col)
        cum = R.cum[l]
        cum_t = cum.T
        for h in range(HL):
            spread = cum[:, h : h + 1] - cum_t[h : h + 1, :]
            ell = jnp.where(keep, jnp.exp(jnp.where(keep, spread, 0.0)), 0.0)
            R.L[l, h] = ell.astype(BF)

        @pl.loop(0, 8, unroll=4)
        def _(j):
            c = lanes(j)
            a, b = halves(R.xdt[l, :, c])
            R.y[l, :, c] = nn(mixing(l, 2 * j), a) + nn(mixing(l, 2 * j + 1), b)

    def scan_states(l):
        exchanged(R.sb, R.rb.at[l], K.ST, l)

        def step(b, state):
            R.eb[b] = state.reshape(32, 128).astype(BF)
            tile = R.rb[l, b, 32:48].astype(F32)
            d = tile[0:8] + tile[8:16]
            return state * d[None] + R.rb[l, b, 0:32].astype(F32).reshape(4, 8, 128)

        lax.fori_loop(0, NS, step, jnp.zeros((4, 8, 128), F32), unroll=8)
        exchange(R.eb, R.sin.at[l], K.EN, l)

    def gate(l):
        c_mat = R.xbc[l, :, IL + ST :]
        entry = pieces(R.entry[l], 2)
        exchanged(R.eb, R.sin.at[l], K.EN, l)

        def block(j, acc):
            c = lanes(j)
            sin = R.sin[l, pl.ds(4 * j, 4)].reshape(128, 128)
            xs = R.xbc[l, :, c].astype(F32)
            y = R.y[l, :, c] + nt(c_mat, sin) * expanded(entry, c) + R.skE[l, 2:3, c] * xs
            R.y[l, :, c] = y
            z = R.z[l, :, c]
            g = y * (z * sigmoid(z))
            gg = g * R.gg[l : l + 1, c]
            R.dye[:, c] = gg.astype(BF)
            if l == 0:
                return (acc[0] + g * g,)
            return (acc[0] + g * g, acc[1] + gg * R.ds[:, c])

        sums = lax.fori_loop(0, 8, block, (jnp.zeros((TOK, 128), F32),) * (l + 1), unroll=4)
        ones = jnp.ones((8, 128), BF)
        parts = [split_right(nt, ones, s, 2) for s in sums]
        if l == 0:
            R.sq[l] = parts[0]
        else:
            at = lax.broadcasted_iota(jnp.int32, (8, 128), 0)
            R.sq[l] = jnp.where(at == 0, parts[0], parts[1])
        R.sqx[l, pl.ds(mx, 1)] = R.sq[l][None]
        to_x(lambda d: (R.sq.at[l], R.sqx.at[l, mx]), K.SQ, l)

    def root(l):
        from_x(R.sqx.at[l, pl.ds(0, 3)], K.SQ, l)
        total = R.sqx[l, 0] + R.sqx[l, 1] + R.sqx[l, 2] + R.sqx[l, 3]
        q = lax.rsqrt(total[0:1] * (1.0 / INNER) + EPS)
        R.q[l] = jnp.broadcast_to(q, (128, 128)).T
        if l == 1:
            R.scol[...] = jnp.broadcast_to(total[1:2], (128, 128)).T

    def project_out(l):
        if l == 0:
            weight(K.WO, l).wait()

        for p in range(4):
            for j in range(2):
                c = slice(512 * p + 256 * j, 512 * p + 256 * j + 256)
                R.pb[:, c] = nn(R.dye[...], R.wo[l, :, :, c].reshape(IL, 256)).astype(BF)
            scatter_x(R.rs.at[l], K.RS, l, p)

    def next_resid(l, before):
        from_x(R.rs.at[l, pl.ds(0, 3)], K.RS, l)
        total = sum(R.rs[l, k].astype(F32) for k in range(NX))
        if l == 0:
            R.br[...] = total
        return before + R.q[l, mine][:, 0:1] * total

    def gather_x(ref, kind, l):
        to_x(lambda d: (ref, ref), kind, l)

    def backward_gate(l):
        entry = pieces(R.entry[l], 2)

        def block(j, acc):
            c = lanes(j)
            z, y = R.z[l, :, c], R.y[l, :, c]
            xs = R.xbc[l, :, c].astype(F32)
            sg = sigmoid(z)
            silu = z * sg
            g = y * silu
            ds, gain, q = R.ds[:, c], R.gg[l : l + 1, c], R.q[l]
            gq = g * q
            dg = ds * gain * q - gq * (q * q * R.scol[...] * (1.0 / INNER))
            dy = dg * silu
            R.ro[0, :, c] = (dg * y * (sg * (1.0 + z * (1.0 - sg)))).astype(BF)
            R.ro[1, :, c] = (gq * gain).astype(BF)
            R.sm[17 + l, pl.ds(j, 1)] = jnp.sum(ds * gq, axis=0, keepdims=True)
            R.dsk[:, c] = jnp.broadcast_to(
                jnp.sum(dy * xs, axis=0, keepdims=True), (8, 128)
            )
            sk = R.skE[l, 2:3, c]
            dyb = dy.astype(BF)
            dyf = dyb.astype(F32)
            R.dyb[:, c] = dyb
            R.dye[:, c] = (dyf * expanded(entry, c)).astype(BF)
            R.ds[:, c] = sk * dy
            direct = tn(R.dye[:, c], R.xbc[l, :, IL + ST :])
            R.sbb[pl.ds(4 * j, 4)] = direct.astype(BF).reshape(4, 32, 128)
            return acc + split_left(nn, dyf * (y - sk * xs), R.Et[c, :])

        R.rows[...] = lax.fori_loop(0, 8, block, jnp.zeros((TOK, 128), F32), unroll=4)
        exchange(R.sbb, R.rbb, K.SB, l)

    def backward_local(l):
        b_mat = R.xbc[l, :, IL : IL + ST]
        c_mat = R.xbc[l, :, IL + ST :]

        def block(j, dgram):
            c = lanes(j)
            a, b = halves(R.dyb[:, c])
            R.U[j] = tn(mixing(l, 2 * j), a) + tn(mixing(l, 2 * j + 1), b)
            xdt = R.xdt[l, :, c]
            return (
                dgram
                + nt(a, xdt) * R.L[l, 2 * j].astype(F32)
                + nt(b, xdt) * R.L[l, 2 * j + 1].astype(F32)
            )

        dgram = lax.fori_loop(0, 8, block, jnp.zeros((TOK, TOK), F32), unroll=4).astype(BF)
        sin = R.sin[l].reshape(IL, ST)
        R.dbc[:, ST:] = nn(dgram, b_mat) + nn(R.dye[...], sin)
        R.dbc[:, 0:ST] = tn(dgram, c_mat)

    def scan_back(l):
        exchanged(R.sbb, R.rbb, K.SB, l)

        def step(i, state):
            b = NS - 1 - i
            R.eb[b] = state.reshape(32, 128).astype(BF)
            tile = R.rb[l, b, 32:48].astype(F32)
            d = tile[0:8] + tile[8:16]
            return state * d[None] + R.rbb[b].astype(F32).reshape(4, 8, 128)

        lax.fori_loop(0, NS, step, jnp.zeros((4, 8, 128), F32), unroll=8)
        exchange(R.eb, R.lam, K.EB, l)

    def backward_state(l):
        b_mat = R.xbc[l, :, IL : IL + ST]
        dt, wls = pieces(R.dt[l], 2), pieces(R.wl[l], 2)
        exchanged(R.eb, R.lam, K.EB, l)

        def block(j, carry):
            c = lanes(j)
            lam = R.lam[pl.ds(4 * j, 4)].reshape(128, 128)
            wl = expanded(wls, c)
            ut = R.U[j] + wl * nt(b_mat, lam)
            xdt = R.xdt[l, :, c].astype(F32)
            R.ds[:, c] += expanded(dt, c) * ut
            xw = (xdt * wl).astype(BF)
            lamf = lam.astype(F32)
            et = R.Et[c, :]
            sin = R.sin[l, pl.ds(4 * j, 4)].reshape(128, 128).astype(F32)
            return (
                carry[0] + nn(xw, lam),
                carry[1] + split_right(tn, et, lamf * R.S[l, c, :].astype(F32)),
                carry[2] + split_right(tn, et, lamf * sin),
                carry[3] + split_left(nn, xdt * ut, et),
                carry[4] + split_left(nn, R.xbc[l, :, c].astype(F32) * ut, et),
            )

        zero = jnp.zeros((128, 128), F32)
        db, ks, kd, less, ddt = lax.fori_loop(0, 8, block, (zero,) * 5, unroll=4)
        R.dbc[:, 0:ST] += db
        held = split_right(nt, jnp.ones((8, 128), BF), ks + R.dtot[l] * kd)
        last = lax.broadcasted_iota(jnp.int32, (TOK, 128), 0) == TOK - 1
        dcum = R.rows[...] - less + jnp.where(last, held[0:1], 0.0)
        drate = split_right(tn, R.tri[...], dcum, 3)
        ddt = ddt - drate * jnp.exp(R.hp[l, 1:2])
        ddtr = ddt * sigmoid(R.dtr[l] + R.hp[l, 0:1])
        R.re[0, :, 640:] = ddtr.astype(BF)
        at = 4 * l
        R.sm[19, at : at + 1] = jnp.sum(ddtr, axis=0, keepdims=True)
        R.sm[19, at + 1 : at + 2] = jnp.sum(drate * R.rate[l], axis=0, keepdims=True)
        R.sm[19, at + 2 : at + 3] = split_left(nn, R.dsk[...], R.Et[...])[0:1]

    def backward_conv(l):
        def block(c, dact):
            pre = conv_sum(l, c)
            sg = sigmoid(pre)
            R.dpre[l, 0:TOK, c] = dact * (sg * (1.0 + pre * (1.0 - sg)))

        @pl.loop(0, 8, unroll=2)
        def _(j):
            block(lanes(j), R.ds[:, lanes(j)])

        for j in range(2):
            block(pl.ds(IL + 128 * j, 128), R.dbc[:, 128 * j : 128 * j + 128])
        head, tail = R.dpre.at[l, pl.ds(0, 8)], R.dpre.at[l, pl.ds(TOK, 8)]
        neighbour(head, tail, K.DP, l, -1)

        def tap_sums(c):
            dpre = R.dpre[l, 0:TOK, c]
            out = []
            for k in range(3):
                shifted = R.v[l, HALO - 3 + k : HALO + TOK - 3 + k, c]
                out.append(jnp.sum(dpre * shifted * R.mk[k], axis=0, keepdims=True))
            out.append(jnp.sum(dpre * R.v[l, HALO:, c], axis=0, keepdims=True))
            return [*out, jnp.sum(dpre, axis=0, keepdims=True)]

        @pl.loop(0, 8, unroll=2)
        def _(j):
            for k, s in enumerate(tap_sums(lanes(j))):
                R.sm[7 + 5 * l + k, pl.ds(j, 1)] = s

        for j in range(2):
            for k, s in enumerate(tap_sums(pl.ds(IL + 128 * j, 128))):
                at = 12 * l + 2 * k + j
                R.sm[4 + at // 8, at % 8 : at % 8 + 1] = s
        neighbour_done(head, tail, K.DP, l, -1)
        job_share(2 - 2 * l, (1,))

        def back(c):
            out = R.ct[l, 3:4, c] * R.dpre[l, 0:TOK, c]
            for k in range(3):
                out = out + (R.ct[l, k : k + 1, c] * R.mkb[k]) * (
                    R.dpre[l, 3 - k : TOK + 3 - k, c]
                )
            return out.astype(BF)

        for j in range(2):
            R.dbp[:, 128 * j : 128 * j + 128] = back(pl.ds(IL + 128 * j, 128))
        R.bx[pl.ds(mx, 1)] = R.dbp[...][None]
        to_x(lambda d: (R.dbp, R.bx.at[mx]), K.BX, l)

        @pl.loop(0, 8, unroll=2)
        def _(j):
            R.re[j // 4, :, lanes(lax.rem(j, 4))] = back(lanes(j))

    def sum_bc(l):
        from_x(R.bx.at[pl.ds(0, 3)], K.BX, l)
        both = sum(R.bx[k].astype(F32) for k in range(NX)).astype(BF)
        R.re[0, :, 512:640] = both[:, 0:128]
        R.re[1, :, 512:640] = both[:, 128:256]

    def backward_project(l):
        R.x2t[:, 0:TOK] = R.ro[0].T
        for k in range(2):
            R.x2t[512 * k : 512 * k + 512, TOK:] = R.re[k, :, 0:512].T
        dbp_t = R.dbp[...].T
        dt_t = R.re[0, :, 640:].T[0:HL]
        for p in range(4):
            for j in range(2 * p, 2 * p + 2):
                rows = slice(256 * j, 256 * j + 256)
                both = nn(R.wz[l, rows].reshape(512, IL), R.x2t[...])
                part = nn(R.wb[l, rows, :], dbp_t) + tn(R.wd[l, :, rows], dt_t)
                for k in range(2):
                    buf = R.U.reshape(2, 512, 128).at[k]
                    buf[...] = both[:, TOK * k : TOK * k + TOK]
                    part += buf[pl.ds(k, 256, stride=2), :]
                R.pb[:, rows] = part.T.astype(BF)
            scatter_x(R.rs.at[1 - l], K.RB, l, p)

    def backward_norm(l, above):
        from_x(R.rs.at[1 - l, pl.ds(0, 3)], K.RB, l)
        dn = sum(R.rs[1 - l, k].astype(F32) for k in range(NX))
        u = R.u[l]
        r = lax.rsqrt(jnp.mean(u * u, axis=1, keepdims=True) + EPS)
        gw = dn * R.ng[l : l + 1, :]
        gain = jnp.sum(dn * u * r, axis=0, keepdims=True)
        for i in range(16):
            R.sm[2 * l + i // 8, i % 8 : i % 8 + 1] = gain[:, 128 * i : 128 * i + 128]
        s = jnp.sum(gw * u, axis=1, keepdims=True) * (1.0 / D)
        return above + gw * r - u * (r * r * r * s)

    def back_scaled(l, src):
        @pl.loop(0, 4, unroll=2)
        def _(j):
            R.ds[:, lanes(j, 256)] = nt(src[...], R.wo[l, pl.ds(2 * j, 2)].reshape(256, D))

    def transposed(src, dst):
        @pl.loop(0, 16, unroll=8)
        def _(j):
            dst[j // 4, lax.rem(j, 4)] = src(lanes(j)).T

    AXES = (("y", iy), ("z", iz))

    def left_block(src, a, p):
        return src.at[:, p] if a == 0 else src.at[p]

    def share_left(l):
        for a, (axis, at) in enumerate(AXES):
            slot = lanes(2 * at + ic)
            dst = R.nl.at[l, a, :, :, slot]
            for k in (2, 1, 3):
                p = lax.rem(at + k, 4)
                kind = (K.NY, K.NZ)[a]
                send(left_block(R.nbt, a, p), dst, sem(kind, l, 0), sem(kind, l, 1), {axis: p})
            dst[...] = left_block(R.nbt, a, at)[...]

    def pass_left(l):
        for a, (axis, at) in enumerate(AXES):
            kind, three = (K.NY, K.NZ)[a], R.nl.at[l, a, :, :, pl.ds(0, 384)]
            wait_for(three, sem(kind, l, 1))
            wait_for(three, sem(kind, l, 0))
            for k in range(4):
                ref = R.nl.at[l, a, :, :, lanes(2 * k + ic)]
                kind = (K.FY, K.FZ)[a]
                send(ref, ref, sem(kind, l, 0), sem(kind, l, 1), {"c": 1 - ic})

    def left_done(l):
        for a in range(2):
            four = R.nl.at[l, a, :, :, pl.ds(0, 512)]
            wait_for(four, sem((K.FY, K.FZ)[a], l, 1))
            wait_for(four, sem((K.FY, K.FZ)[a], l, 0))

    def share_branch(l):
        for a, (axis, at) in enumerate(AXES):
            slot = lanes(2 * at + ic)
            dst, kind = R.dl.at[l, a, :, :, slot], (K.DY, K.DZ)[a]

            def remote(p, dst=dst, kind=kind, axis=axis, a=a):
                send(
                    left_block(R.dbt, a, p), dst, sem(kind, l, 0), sem(kind, l, 1),
                    {axis: p, "c": 1},
                )

            for k in (2, 1, 3):
                remote(lax.rem(at + k, 4))

            @pl.when(ic == 0)
            def _(remote=remote, at=at):
                remote(at)

            @pl.when(ic == 1)
            def _(dst=dst, a=a, at=at):
                dst[...] = left_block(R.dbt, a, at)[...]

    def branch_done(l):
        for a in range(2):

            def count(blocks, side, a=a):
                ref = R.dl.at[l, a, :, :, pl.ds(0, 128 * blocks)]
                wait_for(ref, sem((K.DY, K.DZ)[a], l, side))

            @pl.when(ic == 1)
            def _(count=count):
                count(7, 1)
                count(3, 0)

            @pl.when(ic == 0)
            def _(count=count):
                count(4, 0)

    def job(n):
        wide = n % 2 == 0
        half = (WIDE if wide else NARROW) // 2

        def land(a, slot):
            return R.wo.at[1, slot, :, pl.ds((0 if wide else 1024) + 512 * a, half)]

        return half, land, R.ro if wide else R.re

    def prod(n, a, block, width):
        at = pl.multiple_of(512 * (4 * a + block), 512)
        return R.nx.at[pl.ds(8 * (n % 2), 8), :, pl.ds(at, width)]

    def land2(n):
        return R.land.at[(0, 1, 0, 2)[n]]

    def jsem(n, kind, side):
        return R.jsem.at[n, kind, side]

    def job_share(n, cores, axes=(0, 1)):
        half, land, src = job(n)
        for a in axes:
            axis, at = AXES[a]
            kind = (J.Y1, J.Z1)[a]
            slot = 2 * at + ic
            c = pl.ds(half * a, half)
            for k in (2, 1, 3, 0):
                p = lax.rem(at + k, 4)
                for core in cores:
                    to = {axis: p, "c": core}

                    def remote(core=core, c=c, a=a, slot=slot, kind=kind, to=to):
                        send(
                            src.at[core, :, c], land(a, slot), jsem(n, kind, 0), jsem(n, kind, 1),
                            to,
                        )

                    if k:
                        remote()
                    else:
                        pl.when(ic != core)(remote)

                        @pl.when(ic == core)
                        def _(core=core, c=c, a=a, slot=slot):
                            land(a, slot)[...] = src[core, :, c]

    def job_multiply(n, l):
        half, land, _ = job(n)
        seven = R.wo.at[1, pl.ds(0, 7), :, pl.ds(0, half)]
        for kind in (J.Y1, J.Z1):
            wait_for(seven, jsem(n, kind, 1))
            wait_for(seven, jsem(n, kind, 0))

        def product(left):
            for a in range(2):
                for w in range(0, half, 256):
                    width = min(256, half - w)
                    at = (0 if n % 2 == 0 else 1024) + 512 * a + w
                    right = R.wo[1, :, :, at : at + width].reshape(1024, width)
                    out = nn(left[a].reshape(512, 1024), right)
                    out = out.astype(BF).reshape(4, 8, 16, width)
                    for b in range(4):
                        at = 512 * (4 * a + b) + w
                        R.nx[8 * (n % 2) : 8 * (n % 2) + 8, :, at : at + width] = out[b]

        if n % 2:
            product(R.nl.at[l])
            return

        @pl.when(ic == 0)
        def _():
            product(R.nl.at[l])

        @pl.when(ic == 1)
        def _():
            product(R.dl.at[l])

    def job_reduce(n):
        half, _, _ = job(n)
        c = pl.ds(0, half)
        for k in (2, 1, 3):
            for a, at, axis, kind in ((0, iz, "z", J.Z2), (1, iy, "y", J.Y2)):
                p = lax.rem(at + k, 4)
                send(
                    prod(n, a, p, half), land2(n).at[a, at, :, :, c], jsem(n, kind, 0),
                    jsem(n, kind, 1), {axis: p},
                )

    def job_outputs(n, half_at, to_self):
        l = 1 - n // 2
        rows = pl.ds(pl.multiple_of(64 * half_at, 64), 64)
        kind = J.OWN if to_self else J.OUT

        def put(columns, dst):
            src = R.total.at[n % 2, rows, columns]
            if to_self:
                pltpu.make_async_copy(src, dst, jsem(n, kind, 0)).start()
            else:
                send(src, dst, jsem(n, kind, 0), jsem(n, kind, 1), {"c": 1 - ic})

        @pl.when(ic == 0)
        def _():
            if n % 2 == 0:
                put(pl.ds(0, IL), R.zx_o.at[l, :, 0])
            else:
                put(pl.ds(0, 512), R.zx_o.at[l, :, 1, pl.ds(0, 512)])
                put(pl.ds(512, 128), R.bc_o.at[l, :, pl.ds(0, 128)])
                put(pl.ds(640, 128), R.dt_o.at[l])

        @pl.when(ic == 1)
        def _():
            if n % 2 == 0:
                put(pl.ds(0, IL), R.out_o.at[l])
            else:
                put(pl.ds(0, 512), R.zx_o.at[l, :, 1, pl.ds(512, 512)])
                put(pl.ds(512, 128), R.bc_o.at[l, :, pl.ds(128, 128)])

    def job_sum2(n):
        half, _, _ = job(n)
        three = land2(n).at[0, pl.ds(0, 3), :, :, pl.ds(0, half)]
        for kind in (J.Y2, J.Z2):
            wait_for(three, jsem(n, kind, 1))
            wait_for(three, jsem(n, kind, 0))
        for a, at in ((0, iz), (1, iy)):
            for w in range(0, half, 128):
                here, w = slice(a * half + w, a * half + w + 128), slice(w, w + 128)
                first = pl.multiple_of(512 * (4 * a + at) + w.start, 128)
                s = R.nx[8 * (n % 2) : 8 * (n % 2) + 8, :, pl.ds(first, 128)].astype(F32)
                for k in (1, 2, 3):
                    s = s + land2(n)[a, lax.rem(at + k, 4), :, :, w].astype(F32)
                R.total[n % 2, :, here] = s.reshape(128, 128)
        job_outputs(n, ic, True)
        job_outputs(n, 1 - ic, False)

    def job_done(n):
        def all_of(width, kind, side):
            wait_for(R.total.at[0, pl.ds(0, 64), pl.ds(0, width)], jsem(n, kind, side))

        if n % 2 == 0:
            for kind, side in ((J.OWN, 0), (J.OUT, 0), (J.OUT, 1)):
                all_of(IL, kind, side)
            return

        @pl.when(ic == 0)
        def _():
            for kind, side, width in ((J.OWN, 0, 768), (J.OUT, 0, 768), (J.OUT, 1, 640)):
                all_of(width, kind, side)

        @pl.when(ic == 1)
        def _():
            for kind, side, width in ((J.OWN, 0, 640), (J.OUT, 0, 640), (J.OUT, 1, 768)):
                all_of(width, kind, side)

    def edge_out(i, dst, value):
        R.edge[i] = value.astype(BF)
        here = dst.at[mine]
        pltpu.make_async_copy(R.edge.at[i], here, sem(K.OWN, i, 0)).start()
        kind = (K.OH, K.GI)[i]
        to_x(lambda d: (R.edge.at[i], here), kind, 0)

    def edge_done(i, dst):
        wait_for(R.edge.at[i], sem(K.OWN, i, 0))
        from_x(dst.at[pl.ds(0, 96)], (K.OH, K.GI)[i], 0)

    resid_in.wait()

    @pl.loop(0, 4)
    def _(j):
        rows = pl.ds(pl.multiple_of(j * 32, 32), 32)
        at = pl.ds(pl.multiple_of(HALO + j * 32, 16), 32)
        R.nrm[0, at] = normalize(R.pb[rows].astype(F32), 0)

    R.u[0] = R.pb[mine].astype(F32)
    everyone_is_here()
    neighbour(*halo(0), K.HA, 0, 1)
    project(0)
    convolve(0)
    steps(0)
    ssd(0)
    transposed(lambda c: R.nrm[0, HALO:, c], R.nbt)
    transposed(lambda c: R.cot[:, c], R.dbt)
    scan_states(0)
    gate(0)
    share_left(0)
    share_branch(1)
    project_out(0)
    root(0)
    R.u[1] = next_resid(0, R.u[0])
    at = pl.ds(pl.multiple_of(HALO + mx * 32, 16), 32)
    R.nrm[1, at] = normalize(R.u[1], 1)

    gather_x(R.nrm.at[1, at], K.AG, 1)

    @pl.when(last_x & (me < NS - 1))
    def _():
        src, dst = halo(1)
        for k in range(NX):
            send(src, dst, sem(K.HA, 1, 0), sem(K.HA, 1, 1), {**seq_at(me + 1), "x": k})

    from_x(R.nrm.at[1, pl.ds(HALO, 96)], K.AG, 1)
    project(1)
    convolve(1)
    steps(1)
    ssd(1)
    pass_left(0)
    transposed(lambda c: R.nrm[1, HALO:, c], R.nbt)
    weight(K.WO, 1).wait()
    back_scaled(1, R.cot)
    scan_states(1)
    gate(1)
    share_left(1)
    project_out(1)
    root(1)
    backward_gate(1)
    backward_local(1)
    scan_back(1)
    job_share(0, (0,))
    edge_out(0, R.oh, next_resid(1, R.u[1]))
    pass_left(1)
    left_done(0)
    branch_done(1)
    backward_state(1)
    backward_conv(1)
    job_share(1, (0, 1), (0,))
    backward_project(1)
    sum_bc(1)
    job_share(1, (0, 1), (1,))
    R.du[...] = backward_norm(1, R.cot[mine].astype(F32))
    R.dbr0[mine] = R.du[...].astype(BF)
    gather_x(R.dbr0.at[mine], K.AG, 0)
    s = jnp.sum(R.du[...].astype(BF).astype(F32) * R.br[...], axis=1, keepdims=True)
    R.scol[mine] = jnp.broadcast_to(s, (32, 128))
    gather_x(R.scol.at[mine], K.SC, 0)
    edge_done(0, R.oh)
    left_done(1)
    job_multiply(0, 1)
    job_reduce(0)
    from_x(R.dbr0.at[pl.ds(0, 96)], K.AG, 0)
    transposed(lambda c: R.dbr0[:, c], R.dbt)
    share_branch(0)
    back_scaled(0, R.dbr0)
    from_x(R.scol.at[pl.ds(0, 96)], K.SC, 0)
    backward_gate(0)
    job_multiply(1, 1)
    job_reduce(1)
    backward_local(0)
    job_sum2(0)
    scan_back(0)
    job_share(2, (0,))
    job_sum2(1)
    backward_state(0)
    backward_conv(0)
    job_share(3, (0, 1), (0,))
    backward_project(0)
    sum_bc(0)
    job_share(3, (0, 1), (1,))
    branch_done(0)
    job_multiply(2, 0)
    job_reduce(2)
    edge_out(1, R.gi, backward_norm(0, R.du[...]))
    exchange(R.sm, R.smr, K.SM, 0)
    job_done(0)
    job_multiply(3, 0)
    job_reduce(3)
    exchanged(R.sm, R.smr, K.SM, 0)
    mine_sum = sum(R.smr[k] for k in range(NS))
    R.smt[...] = mine_sum
    R.smx[pl.ds(mx, 1)] = mine_sum[None]
    to_x(lambda d: (R.smt, R.smx.at[mx]), K.SX, 0)
    job_sum2(2)
    from_x(R.smx.at[pl.ds(0, 3)], K.SX, 0)
    over_x = R.smx[0] + R.smx[1] + R.smx[2] + R.smx[3]
    R.smt[...] = jnp.where(me < 7, over_x, R.smt[...])
    R.sums[pl.ds(me, 1)] = R.smt[...][None]

    @pl.loop(1, NS)
    def _(k):
        send(
            R.smt, R.sums.at[me], sem(K.SG, 0, 0), sem(K.SG, 0, 1), seq_at(lax.rem(me + k, NS))
        )

    job_done(1)
    job_sum2(3)
    edge_done(1, R.gi)
    job_done(2)
    wait_for(R.sums.at[pl.ds(0, NS - 1)], sem(K.SG, 0, 1))
    wait_for(R.sums.at[pl.ds(0, NS - 1)], sem(K.SG, 0, 0))
    job_done(3)


def chain(*args):
    vmem = pl.BlockSpec(memory_space=pltpu.VMEM)
    held = pl.BlockSpec(memory_space=pl.ANY)
    return pl.pallas_call(
        chain_kernel,
        out_shape=[jax.ShapeDtypeStruct(s, t) for s, t, _ in OUT.values()],
        in_specs=[held if far else vmem for far in IN.values()],
        out_specs=[held if far else vmem for _, _, far in OUT.values()],
        scratch_shapes=[pltpu.VMEM(s, t) for s, t in SCRATCH.values()]
        + [pltpu.SemaphoreType.DMA((29, 2, 2)), pltpu.SemaphoreType.DMA((4, 6, 2))],
        compiler_params=pltpu.CompilerParams(
            collective_id=1, has_side_effects=True, vmem_limit_bytes=64 * 2**20
        ),
        name="chain",
    )(*args)


def finish_kernel(
    oh, gi, zx, out, bc, dt, sums,
    oh_o, gi_o, norm_o, zx_o, bc_o, dt_o, bias_o, alog_o, skip_o, cx_o, cxb_o, cbc_o, cbcb_o,
    gate_o, out_o, sem,
):
    me = position()
    moves = [(oh, oh_o), (gi, gi_o), (out, out_o), (bc, bc_o), (zx, zx_o)]
    copies = [pltpu.make_async_copy(a, b, sem.at[i]) for i, (a, b) in enumerate(moves)]
    for c in copies:
        c.start()
    for l in range(2):
        block = me // 2
        row = sums[2 * l + block // 8, pl.ds(lax.rem(block, 8), 1)]
        norm_o[l : l + 1] = jnp.where(lax.rem(me, 2) == 0, row[:, 0:64], row[:, 64:])
        dt_o[l] = dt[l].T[0:HL]
        for i, ref in enumerate((bias_o, alog_o, skip_o)):
            ref[l : l + 1] = sums[19, 4 * l + i : 4 * l + i + 1, 0:HL]
        for j in range(8):
            c = slice(128 * j, 128 * j + 128)
            for k in range(4):
                cx_o[l, k : k + 1, c] = sums[7 + 5 * l + k, j : j + 1]
            cxb_o[l : l + 1, c] = sums[11 + 5 * l, j : j + 1]
            gate_o[l : l + 1, c] = sums[17 + l, j : j + 1]
        for j in range(2):
            c = slice(128 * j, 128 * j + 128)
            for k in range(5):
                at = 12 * l + 2 * k + j
                v = sums[4 + at // 8, at % 8 : at % 8 + 1]
                if k < 4:
                    cbc_o[l, k : k + 1, c] = v
                else:
                    cbcb_o[l : l + 1, c] = v
    for c in copies:
        c.wait()


def finish(*args):
    vmem = pl.BlockSpec(memory_space=pltpu.VMEM)
    held = pl.BlockSpec(memory_space=pl.ANY)
    shapes = [
        ((TOK, D), BF, 0), ((TOK, D), BF, 0), ((2, 64), F32, 0), ((2, 64, 2, IL), F32, 0),
        ((2, 64, 256), F32, 0), ((2, HL, 64), F32, 0), ((2, HL), F32, 0), ((2, HL), F32, 0),
        ((2, HL), F32, 0), ((2, 4, IL), F32, 0), ((2, IL), F32, 0), ((2, 4, 256), F32, 0),
        ((2, 256), F32, 0), ((2, IL), F32, 0), ((2, 64, IL), F32, 0),
    ]
    return pl.pallas_call(
        finish_kernel,
        out_shape=[jax.ShapeDtypeStruct(s, t) for s, t, _ in shapes],
        in_specs=[held] * 5 + [vmem] * 2,
        out_specs=[held if far else vmem for _, _, far in shapes],
        scratch_shapes=[pltpu.SemaphoreType.DMA((8,))],
        name="finish",
    )(*args)


def local(
    hidden_in, cotangent, segment_ids, norm_gain, weight_zx, weight_bc, weight_dt, dt_bias, a_log,
    skip_scale, conv_x, conv_x_bias, conv_bc, conv_bc_bias, gate_gain, weight_out,
):
    done = finish(
        *chain(
            hidden_in, cotangent, segment_ids.reshape(NS, TOK), norm_gain, gate_gain, dt_bias,
            a_log, skip_scale, conv_x, conv_x_bias, conv_bc, conv_bc_bias, weight_zx, weight_bc,
            jnp.swapaxes(weight_dt, 1, 2), weight_out.reshape(2, 8, 128, D),
        )
    )
    return (*done[:5], jnp.swapaxes(done[5], 1, 2), *done[6:14], jnp.swapaxes(done[14], 1, 2))


def solution(mesh):
    finer = Mesh(mesh.devices.reshape(4, 4, 2, 4), ("z", "y", "c", "x"))
    in_specs = (
        P(SEQ, None), P(SEQ, None), P(), P(), P(None, None, None, "x"), P(), P(None, None, "x"),
        P(None, "x"), P(None, "x"), P(None, "x"), P(None, None, "x"), P(None, "x"), P(), P(),
        P(None, "x"), P(None, "x", None),
    )
    out_specs = (
        P(SEQ, None), P(SEQ, None), P(None, SEQ), P(None, SEQ, None, "x"), P(None, SEQ, None),
        P(None, SEQ, "x"), P(None, "x"), P(None, "x"), P(None, "x"), P(None, None, "x"),
        P(None, "x"), P(), P(), P(None, "x"), P(None, "x", SEQ),
    )
    return jax.shard_map(local, mesh=finer, in_specs=in_specs, out_specs=out_specs, check_vma=False)
```

```python
import types

import jax
import jax.numpy as jnp
from jax import lax
from jax.experimental import pallas as pl
from jax.experimental.pallas import tpu as pltpu
from jax.sharding import Mesh
from jax.sharding import PartitionSpec as P

D = 2048
INNER = 4096
IL = 1024
TOK = 128
ST = 128
HL = 16
NS = 32
NX = 4
HALO = 16
SEQ = ("z", "y", "c")
EPS = 1e-05
F32 = jnp.float32
BF = jnp.bfloat16
MESH = pl.DeviceIdType.MESH


def partners():
    left = [(z, y, c) for z in range(4) for y in range(4) for c in range(2)][1:]
    left.sort(key=lambda o: min(o[0], 4 - o[0]) + min(o[1], 4 - o[1]))
    left.reverse()
    order = []
    while left:
        z, y, c = left[0]
        for o in ((z, y), (-z % 4, -y % 4), (y, z), (-y % 4, -z % 4)):
            if (*o, c) in left:
                left.remove((*o, c))
                order.append((*o, c))
    return order


ORDER = partners()
OWNERS = 20
WIDE, NARROW = 1024, 768


def dot(a, b, ca, cb):
    return lax.dot_general(a, b, (((ca,), (cb,)), ((), ())), preferred_element_type=F32)


def nn(a, b):
    return dot(a, b, 1, 0)


def nt(a, b):
    return dot(a, b, 1, 1)


def tn(a, b):
    return dot(a, b, 0, 0)


def pieces(a, count):
    out = []
    for _ in range(count):
        p = a.astype(BF)
        out.append(p)
        a = a - p.astype(F32)
    return out


def split_left(f, a, exact, count=2):
    return sum(f(p, exact) for p in pieces(a, count))


def split_right(f, exact, a, count=2):
    return sum(f(exact, p) for p in pieces(a, count))


def sigmoid(v):
    return 1.0 / (1.0 + jnp.exp(-v))


def seq_at(s):
    return {"z": s // 8, "y": lax.rem(s // 2, 4), "c": lax.rem(s, 2)}


def position():
    return lax.axis_index("z") * 8 + lax.axis_index("y") * 2 + lax.axis_index("c")


def lanes(j, width=128, base=0):
    return pl.ds(pl.multiple_of(base + j * width, 128), width)


def wait_for(ref, sem):
    pltpu.make_async_copy(ref, ref, sem).wait()


IN = dict(
    hid=1, cot=0, seg=0, ng=0, gg=0, dtb=0, alog=0, skip=0, cx=0, cxb=0, cbc=0, cbcb=0,
    wzx_h=1, wbc_h=1, wdt_h=1, wout_h=1,
)
OUT = dict(
    oh=((TOK, D), BF, 1),
    gi=((TOK, D), BF, 1),
    zx_o=((2, 64, 2, IL), F32, 1),
    out_o=((2, 64, IL), F32, 1),
    bc_o=((2, 64, 256), F32, 1),
    dt_o=((2, 64, 128), F32, 1),
    sums=((NS, 8, 128), F32, 0),
    norm=((2, 128), F32, 0),
    late=((2, 2, 8, TOK, 512), BF, 1),
)
SCRATCH = dict(
    wz=((2, D, 2, IL), BF),
    wb=((2, D, 256), BF),
    wd=((2, HL, D), BF),
    wo=((2, 8, 128, D), BF),
    nrm=((2, HALO + TOK, D), BF),
    dbr0=((TOK, D), BF),
    z=((2, TOK, IL), F32),
    v=((2, HALO + TOK, 1280), F32),
    xbc=((2, TOK, 1280), BF),
    xdt=((2, TOK, IL), BF),
    L=((2, HL, TOK, TOK), BF),
    G=((2, TOK, TOK), F32),
    y=((2, TOK, IL), F32),
    S=((2, IL, ST), BF),
    dtr=((2, TOK, 128), F32),
    dt=((2, TOK, 128), F32),
    rate=((2, TOK, 128), F32),
    cum=((2, TOK, 128), F32),
    entry=((2, TOK, 128), F32),
    wl=((2, TOK, 128), F32),
    dtot=((2, 128, 128), F32),
    q=((2, TOK, 128), F32),
    skE=((2, 8, IL), F32),
    u=((2, 32, D), F32),
    br=((32, D), F32),
    mk=((3, TOK, 128), F32),
    mkb=((3, TOK, 128), F32),
    E=((128, IL), BF),
    Et=((IL, 128), BF),
    tri=((TOK, TOK), BF),
    sb=((NS, 32, 128), BF),
    rb=((NS, 32, 128), BF),
    last=((2, 1, 128), F32),
    dec=((2, NS, 1, 128), F32),
    decay=((2, NS, 128), F32),
    eb=((NS, 32, 128), BF),
    sin=((2, NS, 32, 128), BF),
    lam=((NS, 32, 128), BF),
    sq=((2, 8, 128), F32),
    sqx=((2, NX, 8, 128), F32),
    pb=((TOK, D), BF),
    rs=((2, NX, 32, D), BF),
    ds=((TOK, IL), F32),
    dbc=((TOK, 256), F32),
    dyb=((TOK, IL), BF),
    dye=((TOK, IL), BF),
    U=((8, TOK, 128), F32),
    rows=((TOK, 128), F32),
    dsk=((8, IL), F32),
    dpre=((2, TOK + 8, 1280), F32),
    scol=((TOK, 128), F32),
    du=((32, D), F32),
    edge=((2, 32, D), BF),
    dbp=((TOK, 256), BF),
    bx=((NX, TOK, 256), BF),
    ro=((2, TOK, WIDE), BF),
    re=((2, TOK, NARROW), BF),
    idc=((TOK + 2 * HALO, 128), F32),
    hp=((2, 8, 128), F32),
    ct=((2, 8, 1280), F32),
    nx=((17, 16, 2 * D), BF),
    pick=((128, 512), BF),
    nbt=((4, 4, 128, 128), BF),
    dbt=((4, 4, 128, 128), BF),
    nl=((2, 2, 4, 128, 1024), BF),
    dl=((2, 2, 4, 128, 1024), BF),
    land=((3, 2, 4, 8, 16, 512), BF),
    total=((2, 128, WIDE), F32),
    x2t=((IL, 256), BF),
    gain=((2, D), F32),
    gsm=((NS, 2, 128), F32),
    gsr=((NS, 2, 128), F32),
    qrow=((1, 128), F32),
    qx=((2, 8, 1, 128), F32),
    sm=((NS, 8, 128), F32),
    smr=((NS, 8, 128), F32),
    smt=((8, 128), F32),
    gst=((2, 128), F32),
    gsx=((NX, 2, 128), F32),
    smx=((NX, 8, 128), F32),
)


class K:
    (
        HID, WZ, WB, WD, WO, ST, EN, SB, EB, SQ, RS, RB, AG, HA, DP, SC, OH, GI, NY, NZ, DY, DZ,
        FY, FZ, LY, LZ, CY, CZ, QY, QZ, DC, BX, SM, SX, SG, OWN,
        AP, AQ, BP, BQ,
    ) = range(40)


class J:
    Y1, Z1, Y2, Z2, OUT, OWN = range(6)


def chain_kernel(*refs):
    R = types.SimpleNamespace(**dict(zip([*IN, *OUT, *SCRATCH, "sem", "jsem"], refs)))
    iz, iy, ic, mx = (lax.axis_index(a) for a in ("z", "y", "c", "x"))
    me = position()
    mine = pl.ds(pl.multiple_of(mx * 32, 32), 32)

    def sem(kind, l, side):
        return R.sem.at[kind, l, side]

    def send(src, dst, s, r, to):
        pltpu.make_async_remote_copy(
            src, dst, s, r, device_id=to, device_id_type=MESH
        ).start()

    def others():
        for dz, dy, dc in ORDER:
            to = {"z": lax.rem(iz + dz, 4), "y": lax.rem(iy + dy, 4), "c": lax.rem(ic + dc, 2)}
            yield to, to["z"] * 8 + to["y"] * 2 + to["c"]

    def exchange(src, dst, kind, l):
        dst[pl.ds(me, 1)] = src[pl.ds(me, 1)]
        for to, d in others():
            send(src.at[d], dst.at[me], sem(kind, l, 0), sem(kind, l, 1), to)

    def exchanged(dst, kind, l):
        wait_for(dst.at[pl.ds(0, NS - 1)], sem(kind, l, 1))
        wait_for(dst.at[pl.ds(0, NS - 1)], sem(kind, l, 0))

    def to_x(make, kind, l):
        for k in (2, 1, 3):
            d = lax.rem(mx + k, NX)
            src, dst = make(d)
            send(src, dst, sem(kind, l, 0), sem(kind, l, 1), {"x": d})

    def from_x(ref, kind, l):
        wait_for(ref, sem(kind, l, 1))
        wait_for(ref, sem(kind, l, 0))

    def scatter_x(dst, kind, l, piece):
        c = pl.ds(512 * piece, 512)
        dst[mx, :, c] = R.pb[mine, c]
        to_x(
            lambda d: (
                R.pb.at[pl.ds(pl.multiple_of(d * 32, 32), 32), c], dst.at[mx, :, c]
            ),
            kind, l,
        )

    def neighbour(src, dst, kind, l, step):
        other = me + step

        @pl.when((other >= 0) & (other < NS))
        def _():
            send(src, dst, sem(kind, l, 0), sem(kind, l, 1), seq_at(other))

    def neighbour_done(src, dst, kind, l, step):
        @pl.when((me + step >= 0) & (me + step < NS))
        def _():
            wait_for(src, sem(kind, l, 0))

        @pl.when((me - step >= 0) & (me - step < NS))
        def _():
            wait_for(dst, sem(kind, l, 1))

    def weight(kind, l):
        src, dst = {
            K.WZ: (R.wzx_h.at[l], R.wz.at[l]),
            K.WB: (R.wbc_h.at[l], R.wb.at[l]),
            K.WD: (R.wdt_h.at[l], R.wd.at[l]),
            K.WO: (R.wout_h.at[l], R.wo.at[l]),
        }[kind]
        return pltpu.make_async_copy(src, dst, sem(kind, l, 0))

    resid_in = pltpu.make_async_copy(R.hid, R.pb, sem(K.HID, 0, 0))
    resid_in.start()
    for l in (0, 1):
        for kind in (K.WZ, K.WB, K.WD, K.WO):
            weight(kind, l).start()

    barrier = pltpu.get_barrier_semaphore()

    @pl.loop(1, NS)
    def _(k):
        pl.semaphore_signal(
            barrier, inc=1, device_id=seq_at(lax.rem(me + k, NS)), device_id_type=MESH
        )

    for k in range(1, NX):
        pl.semaphore_signal(
            barrier, inc=1, device_id={"x": lax.rem(mx + k, NX)}, device_id_type=MESH
        )

    def everyone_is_here():
        pl.semaphore_wait(barrier, NS - 1 + NX - 1)

    def ids_of(s):
        return jnp.broadcast_to(R.seg[pl.ds(s, 1)].astype(F32), (128, 128))

    R.idc[HALO : HALO + TOK] = ids_of(me).T
    R.idc[0:HALO] = jnp.where(me == 0, -1.0, ids_of(lax.rem(me + NS - 1, NS)).T[TOK - HALO :])
    R.idc[HALO + TOK :] = jnp.where(me == NS - 1, -2.0, ids_of(lax.rem(me + 1, NS)).T[0:HALO])
    R.hp[...] = jnp.zeros((2, 8, 128), F32)
    R.ct[...] = jnp.zeros((2, 8, 1280), F32)
    for l in (0, 1):
        for i, ref in enumerate((R.dtb, R.alog, R.skip)):
            R.hp[l, i : i + 1, 0:HL] = ref[l : l + 1]
        R.ct[l, 0:4, 0:IL] = R.cx[l]
        R.ct[l, 0:4, IL:] = R.cbc[l]
        R.ct[l, 4:5, 0:IL] = R.cxb[l : l + 1]
        R.ct[l, 4:5, IL:] = R.cbcb[l : l + 1]
    r_of = lax.broadcasted_iota(jnp.int32, (128, 512), 0)
    c_of = lax.broadcasted_iota(jnp.int32, (128, 512), 1)
    R.pick[...] = jnp.where((c_of == 2 * r_of) | (c_of == 2 * r_of + 257), 1.0, 0.0).astype(BF)
    h_of = lax.broadcasted_iota(jnp.int32, (128, IL), 0)
    c_of = lax.broadcasted_iota(jnp.int32, (128, IL), 1)
    R.E[...] = jnp.where(c_of // 64 == h_of, 1.0, 0.0).astype(BF)
    c_of = lax.broadcasted_iota(jnp.int32, (IL, 128), 0)
    h_of = lax.broadcasted_iota(jnp.int32, (IL, 128), 1)
    R.Et[...] = jnp.where(c_of // 64 == h_of, 1.0, 0.0).astype(BF)
    row = lax.broadcasted_iota(jnp.int32, (TOK, TOK), 0)
    col = lax.broadcasted_iota(jnp.int32, (TOK, TOK), 1)
    R.tri[...] = jnp.where(row >= col, 1.0, 0.0).astype(BF)
    own = R.idc[HALO : HALO + TOK]
    for k in range(3):
        j = 3 - k
        R.mk[k] = jnp.where(R.idc[HALO - j : HALO + TOK - j] == own, 1.0, 0.0)
        R.mkb[k] = jnp.where(R.idc[HALO + j : HALO + TOK + j] == own, 1.0, 0.0)
    R.sm[...] = jnp.zeros((NS, 8, 128), F32)
    R.smr[...] = jnp.zeros((NS, 8, 128), F32)
    R.re[1, :, 640:] = jnp.zeros((TOK, 128), BF)
    for l in (0, 1):
        R.skE[l] = split_left(nn, R.hp[l], R.E[...], 3)

    @pl.when(me == 0)
    def _():
        R.nrm[0, 0:HALO] = jnp.zeros((HALO, D), BF)
        R.v[1, 0:HALO] = jnp.zeros((HALO, 1280), F32)

    @pl.when(me == NS - 1)
    def _():
        R.dpre[:, TOK:] = jnp.zeros((2, 8, 1280), F32)

    lo = lax.broadcasted_iota(jnp.int32, (TOK, 128), 1) < 64

    def halves(pair):
        zero = jnp.zeros_like(pair)
        return jnp.where(lo, pair, zero), jnp.where(lo, zero, pair)

    def expanded(parts, c):
        return sum(nn(p, R.E[:, c]) for p in parts)

    def mixing(l, h):
        return (R.G[l] * R.L[l, h].astype(F32)).astype(BF)

    def normalize(u, l):
        r = lax.rsqrt(jnp.mean(u * u, axis=1, keepdims=True) + EPS)
        return (u * r * R.ng[l : l + 1, :]).astype(BF)

    def halo(l):
        return R.nrm.at[l, pl.ds(TOK, HALO)], R.nrm.at[l, pl.ds(0, HALO)]

    def spread_rows(l, first, rows, at):
        @pl.loop(0, 16, unroll=8)
        def _(j):
            n = R.nrm[l, first : first + rows, lanes(j)]
            if at is None:
                both = nn(n, R.pick[...]).astype(BF)
                R.nx[0:8, :, lanes(j, 256)] = both[:, 0:256].reshape(8, 16, 256)
                R.nx[9:, :, lanes(j, 256)] = both[:, 256:].reshape(8, 16, 256)
            else:
                R.nx[at // 16, :, lanes(j, 256)] = nn(n, R.pick[:, 256:]).astype(BF)

    def v_halo():
        return R.v.at[1, pl.ds(TOK + 8, 8)], R.v.at[1, pl.ds(8, 8)]

    def project_first():
        spread_rows(0, HALO, TOK, None)
        neighbour_done(*halo(0), K.HA, 0, 1)
        spread_rows(0, 0, HALO, TOK)
        weight(K.WZ, 0).wait()

        @pl.loop(0, 4)
        def _(j):
            c = lanes(j, 256)
            both = nn(R.nx[...].reshape(17 * 16, 2 * D), R.wz[0, :, :, c].reshape(2 * D, 256))
            R.z[0, :, c] = both[0:TOK]
            R.v[0, :, c] = both[TOK:]

        weight(K.WB, 0).wait()
        R.v[0, :, IL:] = nn(R.nrm[0], R.wb[0])
        weight(K.WD, 0).wait()
        R.dtr[0] = nt(R.nrm[0, HALO:], widened(R.wd[0]))

    def widened(wd):
        return jnp.concatenate([wd, jnp.zeros((128 - HL, wd.shape[1]), BF)], axis=0)

    def project_second():
        for kind in (K.WZ, K.WB, K.WD):
            weight(kind, 1).wait()
        for p in range(4):
            here = slice(512 * p, 512 * p + 512)
            from_x(R.nrm.at[1, pl.ds(HALO, 96), pl.ds(512 * p, 512)], *AG_PIECES[p])
            for j in range(4 * p, 4 * p + 4):
                n = R.nrm[1, HALO:, 128 * j : 128 * j + 128]
                both = nn(n, R.pick[...]).astype(BF)
                at = slice(256 * j, 256 * j + 256)
                R.nx[0:8, :, at] = both[:, 0:256].reshape(8, 16, 256)
                R.nx[9:, :, at] = both[:, 256:].reshape(8, 16, 256)
            wide = slice(1024 * p, 1024 * p + 1024)
            rows = [R.nx[b : b + 8, :, wide].reshape(TOK, 1024) for b in (0, 9)]
            left = jnp.concatenate(rows, axis=0)
            n = R.nrm[1, HALO:, here]
            for j in range(4):
                c = slice(256 * j, 256 * j + 256)
                both = nn(left, R.wz[1, here, :, c].reshape(1024, 256))
                if p == 0:
                    R.z[1, :, c] = both[0:TOK]
                    R.v[1, HALO:, c] = both[TOK:]
                else:
                    R.z[1, :, c] += both[0:TOK]
                    R.v[1, HALO:, c] += both[TOK:]
            bc = nn(n, R.wb[1, here, :])
            dtr = nt(n, widened(R.wd[1, :, here]))
            if p == 0:
                R.v[1, HALO:, IL:] = bc
                R.dtr[1] = dtr
            else:
                R.v[1, HALO:, IL:] += bc
                R.dtr[1] += dtr
        neighbour(*v_halo(), K.HA, 1, 1)

    def conv_sum(l, c):
        acc = R.ct[l, 4:5, c] + R.ct[l, 3:4, c] * R.v[l, HALO:, c]
        for k in range(3):
            acc = acc + (R.ct[l, k : k + 1, c] * R.mk[k]) * (
                R.v[l, HALO - 3 + k : HALO + TOK - 3 + k, c]
            )
        return acc

    def convolve(l):
        @pl.loop(0, 10, unroll=2)
        def _(j):
            c = lanes(j)
            acc = conv_sum(l, c)
            R.xbc[l, :, c] = (acc * sigmoid(acc)).astype(BF)

    def steps(l):
        raw = R.dtr[l] + R.hp[l, 0:1]
        dt = jnp.maximum(raw, 0.0) + jnp.log1p(jnp.exp(-jnp.abs(raw)))
        rate = -dt * jnp.exp(R.hp[l, 1:2])
        cum = split_right(nn, R.tri[...], rate, 3)
        R.dt[l] = dt
        R.rate[l] = rate
        R.cum[l] = cum
        flag = jnp.where(own == R.idc[HALO - 1 : HALO], 1.0, 0.0)
        ending = jnp.where(own == R.idc[HALO + TOK - 1 : HALO + TOK], 1.0, 0.0)
        entry = jnp.exp(cum) * flag
        R.entry[l] = entry
        R.wl[l] = jnp.exp(cum[TOK - 1 : TOK] - cum) * ending
        R.last[l] = entry[TOK - 1 : TOK]
        R.dec[l, pl.ds(me, 1)] = R.last[l][None]
        for to, _ in others():
            send(R.last.at[l], R.dec.at[l, me], sem(K.DC, l, 0), sem(K.DC, l, 1), to)
        entry_t = entry.T
        heads = lax.broadcasted_iota(jnp.int32, (128, 128), 0) < HL
        R.dtot[l] = jnp.where(
            heads, jnp.broadcast_to(entry_t[:, TOK - 1 : TOK], (128, 128)), 0.0
        )

    def ssd(l):
        b_mat = R.xbc[l, :, IL : IL + ST]
        c_mat = R.xbc[l, :, IL + ST :]
        dt, wl = pieces(R.dt[l], 2), pieces(R.wl[l], 2)

        @pl.loop(0, 8, unroll=4)
        def _(j):
            c = lanes(j)
            xdt = (R.xbc[l, :, c].astype(F32) * expanded(dt, c)).astype(BF)
            R.xdt[l, :, c] = xdt
            xw = (xdt.astype(F32) * expanded(wl, c)).astype(BF)
            s = tn(xw, b_mat).astype(BF)
            R.S[l, c, :] = s
            R.sb[pl.ds(4 * j, 4)] = s.reshape(4, 32, 128)

        exchange(R.sb, R.rb, K.ST, l)
        R.G[l] = nt(c_mat, b_mat)
        keep = (own == ids_of(me)[0:1]) & (row >= col)
        cum = R.cum[l]
        cum_t = cum.T
        for h in range(HL):
            spread = cum[:, h : h + 1] - cum_t[h : h + 1, :]
            ell = jnp.where(keep, jnp.exp(jnp.where(keep, spread, 0.0)), 0.0)
            R.L[l, h] = ell.astype(BF)

        @pl.loop(0, 8, unroll=4)
        def _(j):
            c = lanes(j)
            a, b = halves(R.xdt[l, :, c])
            R.y[l, :, c] = nn(mixing(l, 2 * j), a) + nn(mixing(l, 2 * j + 1), b)

    def scan_states(l):
        exchanged(R.dec.at[l], K.DC, l)
        mine_of = lax.broadcasted_iota(jnp.int32, (NS, 128), 1) == me // 2
        decays = jnp.concatenate([R.dec[l, b] for b in range(NS)], axis=0)
        decays = jnp.sum(jnp.where(mine_of, decays, 0.0), axis=1, keepdims=True)
        R.decay[l] = jnp.broadcast_to(decays, (NS, 128))
        exchanged(R.rb, K.ST, l)

        def step(b, state):
            R.eb[b] = state.reshape(32, 128).astype(BF)
            d = R.decay[l, pl.ds(b, 1)]
            return state * d[None] + R.rb[b].astype(F32).reshape(4, 8, 128)

        lax.fori_loop(0, NS, step, jnp.zeros((4, 8, 128), F32), unroll=8)
        exchange(R.eb, R.sin.at[l], K.EN, l)

    def gate(l):
        c_mat = R.xbc[l, :, IL + ST :]
        entry = pieces(R.entry[l], 2)
        exchanged(R.sin.at[l], K.EN, l)

        def block(j, acc):
            c = lanes(j)
            sin = R.sin[l, pl.ds(4 * j, 4)].reshape(128, 128)
            xs = R.xbc[l, :, c].astype(F32)
            y = R.y[l, :, c] + nt(c_mat, sin) * expanded(entry, c) + R.skE[l, 2:3, c] * xs
            R.y[l, :, c] = y
            z = R.z[l, :, c]
            g = y * (z * sigmoid(z))
            gg = g * R.gg[l : l + 1, c]
            if l == 0:
                R.dye[:, c] = gg.astype(BF)
            else:
                R.ro[1, :, c] = gg.astype(BF)
            if l == 0:
                return (acc[0] + g * g,)
            return (acc[0] + g * g, acc[1] + gg * R.ds[:, c])

        sums = lax.fori_loop(0, 8, block, (jnp.zeros((TOK, 128), F32),) * (l + 1), unroll=4)
        ones = jnp.ones((8, 128), BF)
        parts = [split_right(nt, ones, s, 2) for s in sums]
        if l == 0:
            R.sq[l] = parts[0]
        else:
            at = lax.broadcasted_iota(jnp.int32, (8, 128), 0)
            R.sq[l] = jnp.where(at == 0, parts[0], parts[1])
        R.sqx[l, pl.ds(mx, 1)] = R.sq[l][None]
        to_x(lambda d: (R.sq.at[l], R.sqx.at[l, mx]), K.SQ, l)

    def root(l):
        from_x(R.sqx.at[l, pl.ds(0, 3)], K.SQ, l)
        total = R.sqx[l, 0] + R.sqx[l, 1] + R.sqx[l, 2] + R.sqx[l, 3]
        q = lax.rsqrt(total[0:1] * (1.0 / INNER) + EPS)
        R.q[l] = jnp.broadcast_to(q, (128, 128)).T
        if l == 1:
            R.scol[...] = jnp.broadcast_to(total[1:2], (128, 128)).T
            R.qrow[...] = q
            to_second(lambda a: R.qrow, lambda a, slot: R.qx.at[a, slot], (K.QY, K.QZ), 1)

    def project_out(l):
        if l == 0:
            weight(K.WO, l).wait()

        for p in range(4):
            for j in range(2):
                c = slice(512 * p + 256 * j, 512 * p + 256 * j + 256)
                left = R.dye[...] if l == 0 else R.ro[1]
                R.pb[:, c] = nn(left, R.wo[l, :, :, c].reshape(IL, 256)).astype(BF)
            scatter_x(R.rs.at[l], K.RS, l, p)

    def next_resid(l, before):
        from_x(R.rs.at[l, pl.ds(0, 3)], K.RS, l)
        total = sum(R.rs[l, k].astype(F32) for k in range(NX))
        if l == 0:
            R.br[...] = total
        return before + R.q[l, mine][:, 0:1] * total

    AG_PIECES = ((K.AP, 0), (K.AP, 1), (K.AQ, 0), (K.AQ, 1))
    BG_PIECES = ((K.BP, 0), (K.BP, 1), (K.BQ, 0), (K.BQ, 1))

    def gather_x(ref, kind, l):
        to_x(lambda d: (ref, ref), kind, l)

    def backward_gate(l):
        entry = pieces(R.entry[l], 2)

        def block(j, acc):
            c = lanes(j)
            z, y = R.z[l, :, c], R.y[l, :, c]
            xs = R.xbc[l, :, c].astype(F32)
            sg = sigmoid(z)
            silu = z * sg
            g = y * silu
            ds, gain, q = R.ds[:, c], R.gg[l : l + 1, c], R.q[l]
            gq = g * q
            dg = ds * gain * q - gq * (q * q * R.scol[...] * (1.0 / INNER))
            dy = dg * silu
            R.ro[0, :, c] = (dg * y * (sg * (1.0 + z * (1.0 - sg)))).astype(BF)
            R.sm[17 + l, pl.ds(j, 1)] = jnp.sum(ds * gq, axis=0, keepdims=True)
            R.dsk[:, c] = jnp.broadcast_to(
                jnp.sum(dy * xs, axis=0, keepdims=True), (8, 128)
            )
            sk = R.skE[l, 2:3, c]
            dyb = dy.astype(BF)
            dyf = dyb.astype(F32)
            R.dyb[:, c] = dyb
            R.dye[:, c] = (dyf * expanded(entry, c)).astype(BF)
            R.ds[:, c] = sk * dy
            direct = tn(R.dye[:, c], R.xbc[l, :, IL + ST :])
            R.sb[pl.ds(4 * j, 4)] = direct.astype(BF).reshape(4, 32, 128)
            return acc + split_left(nn, dyf * (y - sk * xs), R.Et[c, :])

        R.rows[...] = lax.fori_loop(0, 8, block, jnp.zeros((TOK, 128), F32), unroll=4)
        exchange(R.sb, R.rb, K.SB, l)

    def backward_local(l):
        b_mat = R.xbc[l, :, IL : IL + ST]
        c_mat = R.xbc[l, :, IL + ST :]

        def block(j, dgram):
            c = lanes(j)
            a, b = halves(R.dyb[:, c])
            R.U[j] = tn(mixing(l, 2 * j), a) + tn(mixing(l, 2 * j + 1), b)
            xdt = R.xdt[l, :, c]
            return (
                dgram
                + nt(a, xdt) * R.L[l, 2 * j].astype(F32)
                + nt(b, xdt) * R.L[l, 2 * j + 1].astype(F32)
            )

        dgram = lax.fori_loop(0, 8, block, jnp.zeros((TOK, TOK), F32), unroll=4).astype(BF)
        sin = R.sin[l].reshape(IL, ST)
        R.dbc[:, ST:] = nn(dgram, b_mat) + nn(R.dye[...], sin)
        R.dbc[:, 0:ST] = tn(dgram, c_mat)

    def scan_back(l):
        exchanged(R.rb, K.SB, l)

        def step(i, state):
            b = NS - 1 - i
            R.eb[b] = state.reshape(32, 128).astype(BF)
            d = R.decay[l, pl.ds(b, 1)]
            return state * d[None] + R.rb[b].astype(F32).reshape(4, 8, 128)

        lax.fori_loop(0, NS, step, jnp.zeros((4, 8, 128), F32), unroll=8)
        exchange(R.eb, R.lam, K.EB, l)

    def backward_state(l):
        b_mat = R.xbc[l, :, IL : IL + ST]
        dt, wls = pieces(R.dt[l], 2), pieces(R.wl[l], 2)
        exchanged(R.lam, K.EB, l)

        def block(j, carry):
            c = lanes(j)
            lam = R.lam[pl.ds(4 * j, 4)].reshape(128, 128)
            wl = expanded(wls, c)
            ut = R.U[j] + wl * nt(b_mat, lam)
            xdt = R.xdt[l, :, c].astype(F32)
            R.ds[:, c] += expanded(dt, c) * ut
            xw = (xdt * wl).astype(BF)
            lamf = lam.astype(F32)
            et = R.Et[c, :]
            sin = R.sin[l, pl.ds(4 * j, 4)].reshape(128, 128).astype(F32)
            return (
                carry[0] + nn(xw, lam),
                carry[1] + split_right(tn, et, lamf * R.S[l, c, :].astype(F32)),
                carry[2] + split_right(tn, et, lamf * sin),
                carry[3] + split_left(nn, xdt * ut, et),
                carry[4] + split_left(nn, R.xbc[l, :, c].astype(F32) * ut, et),
            )

        zero = jnp.zeros((128, 128), F32)
        db, ks, kd, less, ddt = lax.fori_loop(0, 8, block, (zero,) * 5, unroll=4)
        R.dbc[:, 0:ST] += db
        held = split_right(nt, jnp.ones((8, 128), BF), ks + R.dtot[l] * kd)
        last = lax.broadcasted_iota(jnp.int32, (TOK, 128), 0) == TOK - 1
        dcum = R.rows[...] - less + jnp.where(last, held[0:1], 0.0)
        drate = split_right(tn, R.tri[...], dcum, 3)
        ddt = ddt - drate * jnp.exp(R.hp[l, 1:2])
        ddtr = ddt * sigmoid(R.dtr[l] + R.hp[l, 0:1])
        R.re[0, :, 640:] = ddtr.astype(BF)
        at = 4 * l
        R.sm[19, at : at + 1] = jnp.sum(ddtr, axis=0, keepdims=True)
        R.sm[19, at + 1 : at + 2] = jnp.sum(drate * R.rate[l], axis=0, keepdims=True)
        R.sm[19, at + 2 : at + 3] = split_left(nn, R.dsk[...], R.Et[...])[0:1]

    def backward_conv(l):
        def block(c, dact):
            pre = conv_sum(l, c)
            sg = sigmoid(pre)
            R.dpre[l, 0:TOK, c] = dact * (sg * (1.0 + pre * (1.0 - sg)))

        @pl.loop(0, 8, unroll=2)
        def _(j):
            block(lanes(j), R.ds[:, lanes(j)])

        for j in range(2):
            block(pl.ds(IL + 128 * j, 128), R.dbc[:, 128 * j : 128 * j + 128])
        head, tail = R.dpre.at[l, pl.ds(0, 8)], R.dpre.at[l, pl.ds(TOK, 8)]
        neighbour(head, tail, K.DP, l, -1)

        def tap_sums(c):
            dpre = R.dpre[l, 0:TOK, c]
            out = []
            for k in range(3):
                shifted = R.v[l, HALO - 3 + k : HALO + TOK - 3 + k, c]
                out.append(jnp.sum(dpre * shifted * R.mk[k], axis=0, keepdims=True))
            out.append(jnp.sum(dpre * R.v[l, HALO:, c], axis=0, keepdims=True))
            return [*out, jnp.sum(dpre, axis=0, keepdims=True)]

        @pl.loop(0, 8, unroll=2)
        def _(j):
            for k, s in enumerate(tap_sums(lanes(j))):
                R.sm[7 + 5 * l + k, pl.ds(j, 1)] = s

        for j in range(2):
            for k, s in enumerate(tap_sums(pl.ds(IL + 128 * j, 128))):
                at = 12 * l + 2 * k + j
                R.sm[4 + at // 8, at % 8 : at % 8 + 1] = s
        if l == 0:
            R.smr[pl.ds(me, 1)] = R.sm[pl.ds(me, 1)]
            for to, d in others():

                @pl.when(d < OWNERS)
                def _(to=to, d=d):
                    send(R.sm.at[d], R.smr.at[me], sem(K.SM, 0, 0), sem(K.SM, 0, 1), to)

        neighbour_done(head, tail, K.DP, l, -1)

        def back(c):
            out = R.ct[l, 3:4, c] * R.dpre[l, 0:TOK, c]
            for k in range(3):
                out = out + (R.ct[l, k : k + 1, c] * R.mkb[k]) * (
                    R.dpre[l, 3 - k : TOK + 3 - k, c]
                )
            return out.astype(BF)

        for j in range(2):
            R.dbp[:, 128 * j : 128 * j + 128] = back(pl.ds(IL + 128 * j, 128))
        send_bc(l)

        @pl.loop(0, 8, unroll=2)
        def _(j):
            R.re[j // 4, :, lanes(lax.rem(j, 4))] = back(lanes(j))

    def send_bc(l):
        R.bx[pl.ds(mx, 1)] = R.dbp[...][None]
        to_x(lambda d: (R.dbp, R.bx.at[mx]), K.BX, l)

    def sum_bc(l):
        from_x(R.bx.at[pl.ds(0, 3)], K.BX, l)
        both = sum(R.bx[k].astype(F32) for k in range(NX)).astype(BF)
        R.re[0, :, 512:640] = both[:, 0:128]
        R.re[1, :, 512:640] = both[:, 128:256]

    def backward_project(l):
        R.x2t[:, 0:TOK] = R.ro[0].T
        for k in range(2):
            R.x2t[512 * k : 512 * k + 512, TOK:] = R.re[k, :, 0:512].T
        dbp_t = R.dbp[...].T
        dt_t = R.re[0, :, 640:].T[0:HL]
        for p in range(4):
            for j in range(2 * p, 2 * p + 2):
                rows = slice(256 * j, 256 * j + 256)
                both = nn(R.wz[l, rows].reshape(512, IL), R.x2t[...])
                part = nn(R.wb[l, rows, :], dbp_t) + tn(R.wd[l, :, rows], dt_t)
                for k in range(2):
                    buf = R.U.reshape(2, 512, 128).at[k]
                    buf[...] = both[:, TOK * k : TOK * k + TOK]
                    part += buf[pl.ds(k, 256, stride=2), :]
                R.pb[:, rows] = part.T.astype(BF)
            scatter_x(R.rs.at[1 - l], K.RB, l, p)

    def backward_norm(l, above):
        from_x(R.rs.at[1 - l, pl.ds(0, 3)], K.RB, l)
        dn = sum(R.rs[1 - l, k].astype(F32) for k in range(NX))
        u = R.u[l]
        r = lax.rsqrt(jnp.mean(u * u, axis=1, keepdims=True) + EPS)
        gw = dn * R.ng[l : l + 1, :]
        gain = jnp.sum(dn * u * r, axis=0, keepdims=True)
        R.gain[l : l + 1] = gain
        s = jnp.sum(gw * u, axis=1, keepdims=True) * (1.0 / D)
        return above + gw * r - u * (r * r * r * s)

    def back_scaled_pieces():
        for p in range(4):
            here = slice(512 * p, 512 * p + 512)
            from_x(R.dbr0.at[pl.ds(0, 96), pl.ds(512 * p, 512)], *BG_PIECES[p])
            for j in range(4):
                c = slice(256 * j, 256 * j + 256)
                right = R.wo[0, 2 * j : 2 * j + 2, :, here].reshape(256, 512)
                part = nt(R.dbr0[:, here], right)
                if p == 0:
                    R.ds[:, c] = part
                else:
                    R.ds[:, c] += part

    def back_scaled(l, src):
        @pl.loop(0, 4, unroll=2)
        def _(j):
            R.ds[:, lanes(j, 256)] = nt(src[...], R.wo[l, pl.ds(2 * j, 2)].reshape(256, D))

    def transposed(src, dst):
        @pl.loop(0, 16, unroll=8)
        def _(j):
            dst[j // 4, lax.rem(j, 4)] = src(lanes(j)).T

    AXES = (("y", iy), ("z", iz))

    def left_block(src, a, p):
        return src.at[:, p] if a == 0 else src.at[p]

    def share_left(l, part=slice(0, 4)):
        blocks = pl.ds(part.start, part.stop - part.start)
        for a, (axis, at) in enumerate(AXES):
            slot = lanes(2 * at + ic)
            dst = R.nl.at[l, a, blocks, :, slot]
            for k in (2, 1, 3):
                p = lax.rem(at + k, 4)
                kind = (K.NY, K.NZ)[a]
                src = left_block(R.nbt, a, p).at[blocks]
                send(src, dst, sem(kind, l, 0), sem(kind, l, 1), {axis: p})
            dst[...] = left_block(R.nbt, a, at).at[blocks][...]

    def pass_left(l):
        for a, (axis, at) in enumerate(AXES):
            kind, three = (K.NY, K.NZ)[a], R.nl.at[l, a, :, :, pl.ds(0, 384)]
            wait_for(three, sem(kind, l, 1))
            wait_for(three, sem(kind, l, 0))
            for k in range(4):
                ref = R.nl.at[l, a, :, :, lanes(2 * k + ic)]
                kind = (K.FY, K.FZ)[a]
                send(ref, ref, sem(kind, l, 0), sem(kind, l, 1), {"c": 1 - ic})

    def left_done(l):
        for a in range(2):
            four = R.nl.at[l, a, :, :, pl.ds(0, 512)]
            wait_for(four, sem((K.FY, K.FZ)[a], l, 1))
            wait_for(four, sem((K.FY, K.FZ)[a], l, 0))

    def share_branch(l):
        for a, (axis, at) in enumerate(AXES):
            slot = lanes(2 * at + ic)
            dst, kind = R.dl.at[l, a, :, :, slot], (K.DY, K.DZ)[a]

            def remote(p, dst=dst, kind=kind, axis=axis, a=a):
                send(
                    left_block(R.dbt, a, p), dst, sem(kind, l, 0), sem(kind, l, 1),
                    {axis: p, "c": 1},
                )

            for k in (2, 1, 3):
                remote(lax.rem(at + k, 4))

            @pl.when(ic == 0)
            def _(remote=remote, at=at):
                remote(at)

            @pl.when(ic == 1)
            def _(dst=dst, a=a, at=at):
                dst[...] = left_block(R.dbt, a, at)[...]

    def to_second(src, dst, kinds, l):
        for a, (axis, at) in enumerate(AXES):

            def remote(p, a=a, axis=axis, at=at):
                send(
                    src(a), dst(a, 2 * at + ic), sem(kinds[a], l, 0), sem(kinds[a], l, 1),
                    {axis: p, "c": 1},
                )

            for k in (2, 1, 3):
                remote(lax.rem(at + k, 4))
            pl.when(ic == 0)(lambda remote=remote, at=at: remote(at))

            @pl.when(ic == 1)
            def _(a=a, at=at):
                here = sem((K.CY, K.CZ)[a], l, 0 if kinds[0] == K.LY else 1)
                pltpu.make_async_copy(src(a), dst(a, 2 * at + ic), here).start()

    def at_second(ref, kinds, l):
        for a in range(2):

            @pl.when(ic == 1)
            def _(a=a):
                wait_for(ref.at[a, pl.ds(0, 7)], sem(kinds[a], l, 1))
                wait_for(ref.at[a, pl.ds(0, 3)], sem(kinds[a], l, 0))
                wait_for(ref.at[a, 0], sem((K.CY, K.CZ)[a], l, 0 if kinds[0] == K.LY else 1))

            @pl.when(ic == 0)
            def _(a=a):
                wait_for(ref.at[a, pl.ds(0, 4)], sem(kinds[a], l, 0))

    def share_scaled(l):
        to_second(
            lambda a: R.ro.at[1, :, pl.ds(512 * a, 512)],
            lambda a, slot: R.late.at[l, a, slot], (K.LY, K.LZ), l,
        )

    def scaled_first():
        @pl.loop(0, 8, unroll=4)
        def _(j):
            c = lanes(j)
            z = R.z[0, :, c]
            g = R.y[0, :, c] * (z * sigmoid(z))
            R.ro[1, :, c] = (g * R.q[0] * R.gg[0:1, c]).astype(BF)

        share_scaled(0)

    def scaled_done(l):
        at_second(R.late.at[l], (K.LY, K.LZ), l)

    def scaled_load(l, a):
        dst = R.wo.at[1, :, :, pl.ds(512 * a, 512)]
        return pltpu.make_async_copy(R.late.at[l, a], dst, sem(K.OWN, l, a))

    def scaled_fetch(l):
        @pl.when(ic == 1)
        def _():
            for a in range(2):
                scaled_load(l, a).start()

    def branch_times_root():
        at_second(R.qx, (K.QY, K.QZ), 1)

        @pl.when(ic == 1)
        def _():
            for a in range(2):
                q = jnp.concatenate([R.qx[a, k] for k in range(8)], axis=1)

                @pl.loop(0, 4)
                def _(b, a=a, q=q):
                    R.dl[1, a, b] = (R.dl[1, a, b].astype(F32) * q).astype(BF)

    def branch_done(l):
        for a in range(2):

            def count(blocks, side, a=a):
                ref = R.dl.at[l, a, :, :, pl.ds(0, 128 * blocks)]
                wait_for(ref, sem((K.DY, K.DZ)[a], l, side))

            @pl.when(ic == 1)
            def _(count=count):
                count(7, 1)
                count(3, 0)

            @pl.when(ic == 0)
            def _(count=count):
                count(4, 0)

    def job(n):
        wide = n % 2 == 0
        half = (WIDE if wide else NARROW) // 2

        def land(a, slot):
            return R.wo.at[1, slot, :, pl.ds((0 if wide else 1024) + 512 * a, half)]

        return half, land, R.ro if wide else R.re

    def prod(n, a, block, width):
        at = pl.multiple_of(512 * (4 * a + block), 512)
        return R.nx.at[pl.ds(8 * (n % 2), 8), :, pl.ds(at, width)]

    def land2(n):
        return R.land.at[(0, 1, 0, 2)[n]]

    def jsem(n, kind, side):
        return R.jsem.at[n, kind, side]

    def job_share(n, cores, axes=(0, 1), piece=None):
        half, land, src = job(n)
        pieces_of = {None: ((0, half),), 0: ((0, 128), (256, 128)), 1: ((128, 128),)}[piece]
        for a in axes:
            axis, at = AXES[a]
            kind = (J.Y1, J.Z1)[a]
            slot = 2 * at + ic
            for first, width in pieces_of:
                share_columns(n, a, axis, at, kind, slot, cores, src, land, first, width, half)

    def share_columns(n, a, axis, at, kind, slot, cores, src, land, first, width, half):
        c = pl.ds(half * a + first, width)

        def dst():
            return land(a, slot).at[:, pl.ds(first, width)]

        for k in (2, 1, 3, 0):
            p = lax.rem(at + k, 4)
            for core in cores:

                def remote(core=core, p=p):
                    send(
                        src.at[core, :, c], dst(), jsem(n, kind, 0), jsem(n, kind, 1),
                        {axis: p, "c": core},
                    )

                if k:
                    remote()
                else:
                    pl.when(ic != core)(remote)

                    @pl.when(ic == core)
                    def _(core=core):
                        dst()[...] = src[core, :, c]

    def job_multiply(n, l):
        half, land, _ = job(n)
        seven = R.wo.at[1, pl.ds(0, 7), :, pl.ds(0, half)]
        for a, kind in enumerate((J.Y1, J.Z1)):
            if n % 2:
                wait_for(seven, jsem(n, kind, 1))
                wait_for(seven, jsem(n, kind, 0))
                continue

            @pl.when(ic == 0)
            def _(kind=kind):
                wait_for(seven, jsem(n, kind, 1))
                wait_for(R.wo.at[1, pl.ds(0, 3), :, pl.ds(0, half)], jsem(n, kind, 0))

            @pl.when(ic == 1)
            def _(kind=kind, a=a):
                wait_for(R.wo.at[1, pl.ds(0, 4), :, pl.ds(0, half)], jsem(n, kind, 0))
                scaled_load(l, a).wait()

        def product(left):
            for a in range(2):
                for w in range(0, half, 256):
                    width = min(256, half - w)
                    at = (0 if n % 2 == 0 else 1024) + 512 * a + w
                    right = R.wo[1, :, :, at : at + width].reshape(1024, width)
                    out = nn(left[a].reshape(512, 1024), right)
                    out = out.astype(BF).reshape(4, 8, 16, width)
                    for b in range(4):
                        at = 512 * (4 * a + b) + w
                        R.nx[8 * (n % 2) : 8 * (n % 2) + 8, :, at : at + width] = out[b]

        if n % 2:
            product(R.nl.at[l])
            return

        @pl.when(ic == 0)
        def _():
            product(R.nl.at[l])

        @pl.when(ic == 1)
        def _():
            product(R.dl.at[l])

    def job_reduce(n):
        half, _, _ = job(n)
        c = pl.ds(0, half)
        for k in (2, 1, 3):
            for a, at, axis, kind in ((0, iz, "z", J.Z2), (1, iy, "y", J.Y2)):
                p = lax.rem(at + k, 4)
                send(
                    prod(n, a, p, half), land2(n).at[a, at, :, :, c], jsem(n, kind, 0),
                    jsem(n, kind, 1), {axis: p},
                )

    def job_outputs(n, half_at, to_self):
        l = 1 - n // 2
        rows = pl.ds(pl.multiple_of(64 * half_at, 64), 64)
        kind = J.OWN if to_self else J.OUT

        def put(columns, dst):
            src = R.total.at[n % 2, rows, columns]
            if to_self:
                pltpu.make_async_copy(src, dst, jsem(n, kind, 0)).start()
            else:
                send(src, dst, jsem(n, kind, 0), jsem(n, kind, 1), {"c": 1 - ic})

        @pl.when(ic == 0)
        def _():
            if n % 2 == 0:
                put(pl.ds(0, IL), R.zx_o.at[l, :, 0])
            else:
                put(pl.ds(0, 512), R.zx_o.at[l, :, 1, pl.ds(0, 512)])
                put(pl.ds(512, 128), R.bc_o.at[l, :, pl.ds(0, 128)])
                put(pl.ds(640, 128), R.dt_o.at[l])

        @pl.when(ic == 1)
        def _():
            if n % 2 == 0:
                put(pl.ds(0, IL), R.out_o.at[l])
            else:
                put(pl.ds(0, 512), R.zx_o.at[l, :, 1, pl.ds(512, 512)])
                put(pl.ds(512, 128), R.bc_o.at[l, :, pl.ds(128, 128)])

    def job_sum2(n):
        half, _, _ = job(n)
        three = land2(n).at[0, pl.ds(0, 3), :, :, pl.ds(0, half)]
        for kind in (J.Y2, J.Z2):
            wait_for(three, jsem(n, kind, 1))
            wait_for(three, jsem(n, kind, 0))
        for a, at in ((0, iz), (1, iy)):
            for w in range(0, half, 128):
                here, w = slice(a * half + w, a * half + w + 128), slice(w, w + 128)
                first = pl.multiple_of(512 * (4 * a + at) + w.start, 128)
                s = R.nx[8 * (n % 2) : 8 * (n % 2) + 8, :, pl.ds(first, 128)].astype(F32)
                for k in (1, 2, 3):
                    s = s + land2(n)[a, lax.rem(at + k, 4), :, :, w].astype(F32)
                R.total[n % 2, :, here] = s.reshape(128, 128)
        job_outputs(n, ic, True)
        job_outputs(n, 1 - ic, False)

    def job_done(n):
        def all_of(width, kind, side):
            wait_for(R.total.at[0, pl.ds(0, 64), pl.ds(0, width)], jsem(n, kind, side))

        if n % 2 == 0:
            for kind, side in ((J.OWN, 0), (J.OUT, 0), (J.OUT, 1)):
                all_of(IL, kind, side)
            return

        @pl.when(ic == 0)
        def _():
            for kind, side, width in ((J.OWN, 0, 768), (J.OUT, 0, 768), (J.OUT, 1, 640)):
                all_of(width, kind, side)

        @pl.when(ic == 1)
        def _():
            for kind, side, width in ((J.OWN, 0, 640), (J.OUT, 0, 640), (J.OUT, 1, 768)):
                all_of(width, kind, side)

    def edge_out(i, dst, value):
        R.edge[i] = value.astype(BF)
        here = dst.at[mine]
        pltpu.make_async_copy(R.edge.at[i], here, sem(K.HID, 1, i)).start()
        kind = (K.OH, K.GI)[i]
        to_x(lambda d: (R.edge.at[i], here), kind, 0)

    def edge_done(i, dst):
        wait_for(R.edge.at[i], sem(K.HID, 1, i))
        from_x(dst.at[pl.ds(0, 96)], (K.OH, K.GI)[i], 0)

    resid_in.wait()

    @pl.loop(0, 4)
    def _(j):
        rows = pl.ds(pl.multiple_of(j * 32, 32), 32)
        at = pl.ds(pl.multiple_of(HALO + j * 32, 16), 32)
        R.nrm[0, at] = normalize(R.pb[rows].astype(F32), 0)

    R.u[0] = R.pb[mine].astype(F32)
    transposed(lambda c: R.cot[:, c], R.dbt)
    everyone_is_here()
    neighbour(*halo(0), K.HA, 0, 1)
    project_first()
    convolve(0)
    steps(0)
    ssd(0)
    transposed(lambda c: R.nrm[0, HALO:, c], R.nbt)
    scan_states(0)
    gate(0)
    share_left(0)
    share_branch(1)
    project_out(0)
    root(0)
    R.u[1] = next_resid(0, R.u[0])
    at = pl.ds(pl.multiple_of(HALO + mx * 32, 16), 32)
    R.nrm[1, at] = normalize(R.u[1], 1)

    for p in range(4):
        gather_x(R.nrm.at[1, at, pl.ds(512 * p, 512)], *AG_PIECES[p])
    scaled_first()
    pass_left(0)
    project_second()
    steps(1)
    transposed(lambda c: R.nrm[1, HALO:, c], R.nbt)
    share_left(1, slice(0, 2))
    neighbour_done(*v_halo(), K.HA, 1, 1)
    convolve(1)
    ssd(1)
    weight(K.WO, 1).wait()
    back_scaled(1, R.cot)
    scan_states(1)
    scaled_done(0)
    gate(1)
    share_scaled(1)
    share_left(1, slice(2, 4))
    project_out(1)
    root(1)
    backward_gate(1)
    backward_local(1)
    scan_back(1)
    job_share(0, (0,))
    edge_out(0, R.oh, next_resid(1, R.u[1]))
    pass_left(1)
    left_done(0)
    branch_done(1)
    scaled_done(1)
    scaled_fetch(1)
    backward_state(1)
    backward_conv(1)
    job_share(1, (0, 1), (0,))
    job_share(1, (0, 1), (1,), 0)
    backward_project(1)
    sum_bc(1)
    job_share(1, (0, 1), (1,), 1)
    left_done(1)
    branch_times_root()
    job_multiply(0, 1)
    job_reduce(0)
    R.du[...] = backward_norm(1, R.cot[mine].astype(F32))
    R.dbr0[mine] = R.du[...].astype(BF)
    for p in range(4):
        gather_x(R.dbr0.at[mine, pl.ds(512 * p, 512)], *BG_PIECES[p])
    s = jnp.sum(R.du[...].astype(BF).astype(F32) * R.br[...], axis=1, keepdims=True)
    R.scol[mine] = jnp.broadcast_to(s, (32, 128))
    gather_x(R.scol.at[mine], K.SC, 0)
    edge_done(0, R.oh)
    job_multiply(1, 1)
    job_reduce(1)
    back_scaled_pieces()
    transposed(lambda c: R.dbr0[:, c], R.dbt)
    from_x(R.scol.at[pl.ds(0, 96)], K.SC, 0)
    backward_gate(0)
    share_branch(0)
    scaled_fetch(0)
    backward_local(0)
    job_sum2(0)
    scan_back(0)
    job_share(2, (0,))
    backward_state(0)
    backward_conv(0)
    job_share(3, (0, 1), (0,))
    job_share(3, (0, 1), (1,), 0)
    backward_project(0)
    sum_bc(0)
    job_share(3, (0, 1), (1,), 1)
    branch_done(0)
    job_multiply(2, 0)
    job_reduce(2)

    def summed(l, ref, part, of_x):
        part[...] = sum(ref[k] for k in range(NS))
        of_x[pl.ds(mx, 1)] = part[...][None]
        to_x(lambda d: (part, of_x.at[mx]), K.SX, l)

    def summed_over_x(l, of_x):
        from_x(of_x.at[pl.ds(0, 3)], K.SX, l)
        return of_x[0] + of_x[1] + of_x[2] + of_x[3]

    @pl.when(me < OWNERS)
    def _():
        wait_for(R.smr.at[pl.ds(0, NS - 1)], sem(K.SM, 0, 1))
        wait_for(R.smr.at[pl.ds(0, OWNERS - 1)], sem(K.SM, 0, 0))

    @pl.when(me >= OWNERS)
    def _():
        wait_for(R.smr.at[pl.ds(0, OWNERS)], sem(K.SM, 0, 0))

    summed(0, R.smr, R.smt, R.smx)
    edge_out(1, R.gi, backward_norm(0, R.du[...]))
    for k in range(NS):
        R.gsm[k] = R.gain[:, 128 * (k // 2) : 128 * (k // 2) + 128]
    exchange(R.gsm, R.gsr, K.SM, 1)
    over_x = summed_over_x(0, R.smx)
    R.smt[...] = jnp.where(me < 7, over_x, R.smt[...])
    R.sums[pl.ds(me, 1)] = R.smt[...][None]

    @pl.when(me < OWNERS)
    def _():
        for to, _ in others():
            send(R.smt, R.sums.at[me], sem(K.SG, 0, 0), sem(K.SG, 0, 1), to)

    job_done(0)
    job_sum2(1)
    job_multiply(3, 0)
    job_reduce(3)
    job_sum2(2)
    exchanged(R.gsr, K.SM, 1)
    summed(1, R.gsr, R.gst, R.gsx)

    @pl.when(me < OWNERS)
    def _():
        wait_for(R.sums.at[pl.ds(0, OWNERS - 1)], sem(K.SG, 0, 1))
        wait_for(R.sums.at[pl.ds(0, NS - 1)], sem(K.SG, 0, 0))

    @pl.when(me >= OWNERS)
    def _():
        wait_for(R.sums.at[pl.ds(0, OWNERS)], sem(K.SG, 0, 1))

    job_done(1)
    job_sum2(3)
    R.norm[...] = summed_over_x(1, R.gsx)
    edge_done(1, R.gi)
    job_done(2)
    job_done(3)


def chain(*args):
    vmem = pl.BlockSpec(memory_space=pltpu.VMEM)
    held = pl.BlockSpec(memory_space=pl.ANY)
    return pl.pallas_call(
        chain_kernel,
        out_shape=[jax.ShapeDtypeStruct(s, t) for s, t, _ in OUT.values()],
        in_specs=[held if far else vmem for far in IN.values()],
        out_specs=[held if far else vmem for _, _, far in OUT.values()],
        scratch_shapes=[pltpu.VMEM(s, t) for s, t in SCRATCH.values()]
        + [pltpu.SemaphoreType.DMA((40, 2, 2)), pltpu.SemaphoreType.DMA((4, 6, 2))],
        compiler_params=pltpu.CompilerParams(
            collective_id=1, has_side_effects=True, vmem_limit_bytes=64 * 2**20
        ),
        name="chain",
    )(*args)


def finish_kernel(
    oh, gi, zx, out, bc, dt, sums, norm,
    oh_o, gi_o, norm_o, zx_o, bc_o, dt_o, bias_o, alog_o, skip_o, cx_o, cxb_o, cbc_o, cbcb_o,
    gate_o, out_o, sem,
):
    me = position()
    moves = [(oh, oh_o), (gi, gi_o), (out, out_o), (bc, bc_o), (zx, zx_o)]
    copies = [pltpu.make_async_copy(a, b, sem.at[i]) for i, (a, b) in enumerate(moves)]
    for c in copies:
        c.start()
    for l in range(2):
        row = norm[l : l + 1]
        norm_o[l : l + 1] = jnp.where(lax.rem(me, 2) == 0, row[:, 0:64], row[:, 64:])
        dt_o[l] = dt[l].T[0:HL]
        for i, ref in enumerate((bias_o, alog_o, skip_o)):
            ref[l : l + 1] = sums[19, 4 * l + i : 4 * l + i + 1, 0:HL]
        for j in range(8):
            c = slice(128 * j, 128 * j + 128)
            for k in range(4):
                cx_o[l, k : k + 1, c] = sums[7 + 5 * l + k, j : j + 1]
            cxb_o[l : l + 1, c] = sums[11 + 5 * l, j : j + 1]
            gate_o[l : l + 1, c] = sums[17 + l, j : j + 1]
        for j in range(2):
            c = slice(128 * j, 128 * j + 128)
            for k in range(5):
                at = 12 * l + 2 * k + j
                v = sums[4 + at // 8, at % 8 : at % 8 + 1]
                if k < 4:
                    cbc_o[l, k : k + 1, c] = v
                else:
                    cbcb_o[l : l + 1, c] = v
    for c in copies:
        c.wait()


def finish(*args):
    vmem = pl.BlockSpec(memory_space=pltpu.VMEM)
    held = pl.BlockSpec(memory_space=pl.ANY)
    shapes = [
        ((TOK, D), BF, 0), ((TOK, D), BF, 0), ((2, 64), F32, 0), ((2, 64, 2, IL), F32, 0),
        ((2, 64, 256), F32, 0), ((2, HL, 64), F32, 0), ((2, HL), F32, 0), ((2, HL), F32, 0),
        ((2, HL), F32, 0), ((2, 4, IL), F32, 0), ((2, IL), F32, 0), ((2, 4, 256), F32, 0),
        ((2, 256), F32, 0), ((2, IL), F32, 0), ((2, 64, IL), F32, 0),
    ]
    return pl.pallas_call(
        finish_kernel,
        out_shape=[jax.ShapeDtypeStruct(s, t) for s, t, _ in shapes],
        in_specs=[held] * 5 + [vmem] * 3,
        out_specs=[held if far else vmem for _, _, far in shapes],
        scratch_shapes=[pltpu.SemaphoreType.DMA((8,))],
        name="finish",
    )(*args)


def local(
    hidden_in, cotangent, segment_ids, norm_gain, weight_zx, weight_bc, weight_dt, dt_bias, a_log,
    skip_scale, conv_x, conv_x_bias, conv_bc, conv_bc_bias, gate_gain, weight_out,
):
    *raw, _ = chain(
        hidden_in, cotangent, segment_ids.reshape(NS, TOK), norm_gain, gate_gain, dt_bias,
        a_log, skip_scale, conv_x, conv_x_bias, conv_bc, conv_bc_bias, weight_zx, weight_bc,
        jnp.swapaxes(weight_dt, 1, 2), weight_out.reshape(2, 8, 128, D),
    )
    done = finish(*raw)
    return (*done[:5], jnp.swapaxes(done[5], 1, 2), *done[6:14], jnp.swapaxes(done[14], 1, 2))


def solution(mesh):
    finer = Mesh(mesh.devices.reshape(4, 4, 2, 4), ("z", "y", "c", "x"))
    in_specs = (
        P(SEQ, None), P(SEQ, None), P(), P(), P(None, None, None, "x"), P(), P(None, None, "x"),
        P(None, "x"), P(None, "x"), P(None, "x"), P(None, None, "x"), P(None, "x"), P(), P(),
        P(None, "x"), P(None, "x", None),
    )
    out_specs = (
        P(SEQ, None), P(SEQ, None), P(None, SEQ), P(None, SEQ, None, "x"), P(None, SEQ, None),
        P(None, SEQ, "x"), P(None, "x"), P(None, "x"), P(None, "x"), P(None, None, "x"),
        P(None, "x"), P(), P(), P(None, "x"), P(None, "x", SEQ),
    )
    return jax.shard_map(local, mesh=finer, in_specs=in_specs, out_specs=out_specs, check_vma=False)
```

```python
import types

import jax
import jax.numpy as jnp
from jax import lax
from jax.experimental import pallas as pl
from jax.experimental.pallas import tpu as pltpu
from jax.sharding import Mesh
from jax.sharding import PartitionSpec as P

D = 2048
INNER = 4096
IL = 1024
TOK = 128
ST = 128
HL = 16
NS = 32
NX = 4
HALO = 16
SEQ = ("z", "y", "c")
EPS = 1e-05
F32 = jnp.float32
BF = jnp.bfloat16
MESH = pl.DeviceIdType.MESH


def partners():
    left = [(z, y, c) for z in range(4) for y in range(4) for c in range(2)][1:]
    left.sort(key=lambda o: min(o[0], 4 - o[0]) + min(o[1], 4 - o[1]))
    left.reverse()
    order = []
    while left:
        z, y, c = left[0]
        for o in ((z, y), (-z % 4, -y % 4), (y, z), (-y % 4, -z % 4)):
            if (*o, c) in left:
                left.remove((*o, c))
                order.append((*o, c))
    return order


ORDER = partners()
OWNERS = 20
WIDE, NARROW = (512, 512), (256, 384)


def dot(a, b, ca, cb):
    return lax.dot_general(a, b, (((ca,), (cb,)), ((), ())), preferred_element_type=F32)


def nn(a, b):
    return dot(a, b, 1, 0)


def nt(a, b):
    return dot(a, b, 1, 1)


def tn(a, b):
    return dot(a, b, 0, 0)


def pieces(a, count):
    out = []
    for _ in range(count):
        p = a.astype(BF)
        out.append(p)
        a = a - p.astype(F32)
    return out


def split_left(f, a, exact, count=2):
    return sum(f(p, exact) for p in pieces(a, count))


def split_right(f, exact, a, count=2):
    return sum(f(exact, p) for p in pieces(a, count))


def sigmoid(v):
    return 1.0 / (1.0 + jnp.exp(-v))


def seq_at(s):
    return {"z": s // 8, "y": lax.rem(s // 2, 4), "c": lax.rem(s, 2)}


def position():
    return lax.axis_index("z") * 8 + lax.axis_index("y") * 2 + lax.axis_index("c")


def lanes(j, width=128, base=0):
    return pl.ds(pl.multiple_of(base + j * width, 128), width)


def wait_for(ref, sem):
    pltpu.make_async_copy(ref, ref, sem).wait()


IN = dict(
    hid=1, cot=0, seg=0, ng=0, gg=0, dtb=0, alog=0, skip=0, cx=0, cxb=0, cbc=0, cbcb=0,
    wzx_h=1, wbc_h=1, wdt_h=1, wout_h=1,
)
OUT = dict(
    oh=((TOK, D), BF, 1),
    gi=((TOK, D), BF, 1),
    zx_o=((2, 64, 2, IL), F32, 1),
    out_o=((2, 64, IL), F32, 1),
    mix_o=((2, NX, 64, 128), F32, 1),
    sums=((NS, 8, 128), F32, 0),
    norm=((2, 128), F32, 0),
    late=((2, 2, 8, TOK, 512), BF, 1),
)
SCRATCH = dict(
    wz=((2, D, 2, IL), BF),
    wb=((2, D, 256), BF),
    wd=((2, HL, D), BF),
    wo=((2, 8, 128, D), BF),
    nrm=((2, HALO + TOK, D), BF),
    dbr0=((TOK, D), BF),
    z=((2, TOK, IL), F32),
    v=((2, HALO + TOK, 1280), F32),
    xbc=((2, TOK, 1280), BF),
    xdt=((2, TOK, IL), BF),
    L=((2, HL, TOK, TOK), BF),
    G=((2, TOK, TOK), F32),
    y=((2, TOK, IL), F32),
    S=((2, IL, ST), BF),
    dtr=((2, TOK, 128), F32),
    dt=((2, TOK, 128), F32),
    rate=((2, TOK, 128), F32),
    cum=((2, TOK, 128), F32),
    entry=((2, TOK, 128), F32),
    wl=((2, TOK, 128), F32),
    dtot=((2, 128, 128), F32),
    q=((2, TOK, 128), F32),
    skE=((2, 8, IL), F32),
    u=((2, 32, D), F32),
    br=((32, D), F32),
    mk=((3, TOK, 128), F32),
    mkb=((3, TOK, 128), F32),
    E=((128, IL), BF),
    Et=((IL, 128), BF),
    tri=((TOK, TOK), BF),
    sb=((NS, 32, 128), BF),
    rb=((NS, 32, 128), BF),
    last=((2, 1, 128), F32),
    dec=((2, NS, 1, 128), F32),
    decay=((2, NS, 128), F32),
    eb=((NS, 32, 128), BF),
    sin=((2, NS, 32, 128), BF),
    lam=((NS, 32, 128), BF),
    sq=((2, 8, 128), F32),
    sqx=((2, NX, 8, 128), F32),
    pb=((TOK, D), BF),
    rs=((2, NX, 32, D), BF),
    ds=((TOK, IL), F32),
    dbc=((TOK, 256), F32),
    dyb=((TOK, IL), BF),
    dye=((TOK, IL), BF),
    U=((8, TOK, 128), F32),
    rows=((TOK, 128), F32),
    dsk=((8, IL), F32),
    dpre=((2, TOK + 8, 1280), F32),
    scol=((TOK, 128), F32),
    du=((32, D), F32),
    edge=((2, 32, D), BF),
    dbp=((TOK, 256), BF),
    ddt=((TOK, 128), BF),
    bx=((NX, TOK, 128), BF),
    ro=((2, TOK, IL), BF),
    re=((2, TOK, 640), BF),
    idc=((TOK + 2 * HALO, 128), F32),
    hp=((2, 8, 128), F32),
    ct=((2, 8, 1280), F32),
    nx=((17, 16, 2 * D), BF),
    pick=((128, 512), BF),
    nbt=((4, 4, 128, 128), BF),
    dbt=((4, 4, 128, 128), BF),
    nl=((2, 2, 4, 128, 1024), BF),
    dl=((2, 2, 4, 128, 1024), BF),
    land=((2, 2, 4, 8, 16, 512), BF),
    total=((2, 128, IL), F32),
    x2t=((IL, 256), BF),
    gain=((2, D), F32),
    gsm=((NS, 2, 128), F32),
    gsr=((NS, 2, 128), F32),
    qrow=((1, 128), F32),
    qx=((2, 8, 1, 128), F32),
    sm=((NS, 8, 128), F32),
    smr=((NS, 8, 128), F32),
    smt=((8, 128), F32),
    gst=((2, 128), F32),
    gsx=((NX, 2, 128), F32),
    smx=((NX, 8, 128), F32),
)


class K:
    (
        HID, WZ, WB, WD, WO, ST, EN, SB, EB, SQ, RS, RB, AG, HA, DP, SC, OH, GI, NY, NZ, DY, DZ,
        FY, FZ, LY, LZ, CY, CZ, QY, QZ, DC, BX, SM, SX, SG, OWN,
        AP, AQ, BP, BQ, MX, MS,
    ) = range(42)


class J:
    Y1, Z1, Y2, Z2, OUT, OWN = range(6)


def chain_kernel(*refs):
    R = types.SimpleNamespace(**dict(zip([*IN, *OUT, *SCRATCH, "sem", "jsem"], refs)))
    iz, iy, ic, mx = (lax.axis_index(a) for a in ("z", "y", "c", "x"))
    me = position()
    mine = pl.ds(pl.multiple_of(mx * 32, 32), 32)

    def sem(kind, l, side):
        return R.sem.at[kind, l, side]

    def send(src, dst, s, r, to):
        pltpu.make_async_remote_copy(
            src, dst, s, r, device_id=to, device_id_type=MESH
        ).start()

    def others():
        for dz, dy, dc in ORDER:
            to = {"z": lax.rem(iz + dz, 4), "y": lax.rem(iy + dy, 4), "c": lax.rem(ic + dc, 2)}
            yield to, to["z"] * 8 + to["y"] * 2 + to["c"]

    def exchange(src, dst, kind, l):
        dst[pl.ds(me, 1)] = src[pl.ds(me, 1)]
        for to, d in others():
            send(src.at[d], dst.at[me], sem(kind, l, 0), sem(kind, l, 1), to)

    def exchanged(dst, kind, l):
        wait_for(dst.at[pl.ds(0, NS - 1)], sem(kind, l, 1))
        wait_for(dst.at[pl.ds(0, NS - 1)], sem(kind, l, 0))

    def to_x(make, kind, l, also={}):
        for k in (2, 1, 3):
            d = lax.rem(mx + k, NX)
            src, dst = make(d)
            send(src, dst, sem(kind, l, 0), sem(kind, l, 1), {"x": d, **also})

    def from_x(ref, kind, l):
        wait_for(ref, sem(kind, l, 1))
        wait_for(ref, sem(kind, l, 0))

    def scatter_x(dst, kind, l, piece):
        c = pl.ds(512 * piece, 512)
        dst[mx, :, c] = R.pb[mine, c]
        to_x(
            lambda d: (
                R.pb.at[pl.ds(pl.multiple_of(d * 32, 32), 32), c], dst.at[mx, :, c]
            ),
            kind, l,
        )

    def neighbour(src, dst, kind, l, step):
        other = me + step

        @pl.when((other >= 0) & (other < NS))
        def _():
            send(src, dst, sem(kind, l, 0), sem(kind, l, 1), seq_at(other))

    def neighbour_done(src, dst, kind, l, step):
        @pl.when((me + step >= 0) & (me + step < NS))
        def _():
            wait_for(src, sem(kind, l, 0))

        @pl.when((me - step >= 0) & (me - step < NS))
        def _():
            wait_for(dst, sem(kind, l, 1))

    def weight(kind, l):
        src, dst = {
            K.WZ: (R.wzx_h.at[l], R.wz.at[l]),
            K.WB: (R.wbc_h.at[l], R.wb.at[l]),
            K.WD: (R.wdt_h.at[l], R.wd.at[l]),
            K.WO: (R.wout_h.at[l], R.wo.at[l]),
        }[kind]
        return pltpu.make_async_copy(src, dst, sem(kind, l, 0))

    resid_in = pltpu.make_async_copy(R.hid, R.pb, sem(K.HID, 0, 0))
    resid_in.start()
    for l in (0, 1):
        for kind in (K.WZ, K.WB, K.WD, K.WO):
            weight(kind, l).start()

    barrier = pltpu.get_barrier_semaphore()

    @pl.loop(1, NS)
    def _(k):
        pl.semaphore_signal(
            barrier, inc=1, device_id=seq_at(lax.rem(me + k, NS)), device_id_type=MESH
        )

    for k in range(1, NX):
        for core in (ic, 1 - ic):
            pl.semaphore_signal(
                barrier, inc=1, device_id={"x": lax.rem(mx + k, NX), "c": core},
                device_id_type=MESH,
            )

    def everyone_is_here():
        pl.semaphore_wait(barrier, NS - 1 + 2 * (NX - 1))

    def ids_of(s):
        return jnp.broadcast_to(R.seg[pl.ds(s, 1)].astype(F32), (128, 128))

    R.idc[HALO : HALO + TOK] = ids_of(me).T
    R.idc[0:HALO] = jnp.where(me == 0, -1.0, ids_of(lax.rem(me + NS - 1, NS)).T[TOK - HALO :])
    R.idc[HALO + TOK :] = jnp.where(me == NS - 1, -2.0, ids_of(lax.rem(me + 1, NS)).T[0:HALO])
    R.hp[...] = jnp.zeros((2, 8, 128), F32)
    R.ct[...] = jnp.zeros((2, 8, 1280), F32)
    for l in (0, 1):
        for i, ref in enumerate((R.dtb, R.alog, R.skip)):
            R.hp[l, i : i + 1, 0:HL] = ref[l : l + 1]
        R.ct[l, 0:4, 0:IL] = R.cx[l]
        R.ct[l, 0:4, IL:] = R.cbc[l]
        R.ct[l, 4:5, 0:IL] = R.cxb[l : l + 1]
        R.ct[l, 4:5, IL:] = R.cbcb[l : l + 1]
    r_of = lax.broadcasted_iota(jnp.int32, (128, 512), 0)
    c_of = lax.broadcasted_iota(jnp.int32, (128, 512), 1)
    R.pick[...] = jnp.where((c_of == 2 * r_of) | (c_of == 2 * r_of + 257), 1.0, 0.0).astype(BF)
    h_of = lax.broadcasted_iota(jnp.int32, (128, IL), 0)
    c_of = lax.broadcasted_iota(jnp.int32, (128, IL), 1)
    R.E[...] = jnp.where(c_of // 64 == h_of, 1.0, 0.0).astype(BF)
    c_of = lax.broadcasted_iota(jnp.int32, (IL, 128), 0)
    h_of = lax.broadcasted_iota(jnp.int32, (IL, 128), 1)
    R.Et[...] = jnp.where(c_of // 64 == h_of, 1.0, 0.0).astype(BF)
    row = lax.broadcasted_iota(jnp.int32, (TOK, TOK), 0)
    col = lax.broadcasted_iota(jnp.int32, (TOK, TOK), 1)
    R.tri[...] = jnp.where(row >= col, 1.0, 0.0).astype(BF)
    own = R.idc[HALO : HALO + TOK]
    for k in range(3):
        j = 3 - k
        R.mk[k] = jnp.where(R.idc[HALO - j : HALO + TOK - j] == own, 1.0, 0.0)
        R.mkb[k] = jnp.where(R.idc[HALO + j : HALO + TOK + j] == own, 1.0, 0.0)
    R.sm[...] = jnp.zeros((NS, 8, 128), F32)
    R.smr[...] = jnp.zeros((NS, 8, 128), F32)
    for l in (0, 1):
        R.skE[l] = split_left(nn, R.hp[l], R.E[...], 3)

    @pl.when(me == 0)
    def _():
        R.nrm[0, 0:HALO] = jnp.zeros((HALO, D), BF)
        R.v[1, 0:HALO] = jnp.zeros((HALO, 1280), F32)

    @pl.when(me == NS - 1)
    def _():
        R.dpre[:, TOK:] = jnp.zeros((2, 8, 1280), F32)

    lo = lax.broadcasted_iota(jnp.int32, (TOK, 128), 1) < 64

    def halves(pair):
        zero = jnp.zeros_like(pair)
        return jnp.where(lo, pair, zero), jnp.where(lo, zero, pair)

    def expanded(parts, c):
        return sum(nn(p, R.E[:, c]) for p in parts)

    def mixing(l, h):
        return (R.G[l] * R.L[l, h].astype(F32)).astype(BF)

    def normalize(u, l):
        r = lax.rsqrt(jnp.mean(u * u, axis=1, keepdims=True) + EPS)
        return (u * r * R.ng[l : l + 1, :]).astype(BF)

    def halo(l):
        return R.nrm.at[l, pl.ds(TOK, HALO)], R.nrm.at[l, pl.ds(0, HALO)]

    def spread_rows(l, first, rows, at):
        @pl.loop(0, 16, unroll=8)
        def _(j):
            n = R.nrm[l, first : first + rows, lanes(j)]
            if at is None:
                both = nn(n, R.pick[...]).astype(BF)
                R.nx[0:8, :, lanes(j, 256)] = both[:, 0:256].reshape(8, 16, 256)
                R.nx[9:, :, lanes(j, 256)] = both[:, 256:].reshape(8, 16, 256)
            else:
                R.nx[at // 16, :, lanes(j, 256)] = nn(n, R.pick[:, 256:]).astype(BF)

    def v_halo():
        return R.v.at[1, pl.ds(TOK + 8, 8)], R.v.at[1, pl.ds(8, 8)]

    def project_first():
        spread_rows(0, HALO, TOK, None)
        neighbour_done(*halo(0), K.HA, 0, 1)
        spread_rows(0, 0, HALO, TOK)
        weight(K.WZ, 0).wait()

        @pl.loop(0, 4)
        def _(j):
            c = lanes(j, 256)
            both = nn(R.nx[...].reshape(17 * 16, 2 * D), R.wz[0, :, :, c].reshape(2 * D, 256))
            R.z[0, :, c] = both[0:TOK]
            R.v[0, :, c] = both[TOK:]

        weight(K.WB, 0).wait()
        R.v[0, :, IL:] = nn(R.nrm[0], R.wb[0])
        weight(K.WD, 0).wait()
        R.dtr[0] = nt(R.nrm[0, HALO:], widened(R.wd[0]))

    def widened(wd):
        return jnp.concatenate([wd, jnp.zeros((128 - HL, wd.shape[1]), BF)], axis=0)

    def project_second():
        for kind in (K.WZ, K.WB, K.WD):
            weight(kind, 1).wait()
        for p in range(4):
            here = slice(512 * p, 512 * p + 512)
            from_x(R.nrm.at[1, pl.ds(HALO, 96), pl.ds(512 * p, 512)], *AG_PIECES[p])
            for j in range(4 * p, 4 * p + 4):
                n = R.nrm[1, HALO:, 128 * j : 128 * j + 128]
                both = nn(n, R.pick[...]).astype(BF)
                at = slice(256 * j, 256 * j + 256)
                R.nx[0:8, :, at] = both[:, 0:256].reshape(8, 16, 256)
                R.nx[9:, :, at] = both[:, 256:].reshape(8, 16, 256)
            wide = slice(1024 * p, 1024 * p + 1024)
            rows = [R.nx[b : b + 8, :, wide].reshape(TOK, 1024) for b in (0, 9)]
            left = jnp.concatenate(rows, axis=0)
            n = R.nrm[1, HALO:, here]
            for j in range(4):
                c = slice(256 * j, 256 * j + 256)
                both = nn(left, R.wz[1, here, :, c].reshape(1024, 256))
                if p == 0:
                    R.z[1, :, c] = both[0:TOK]
                    R.v[1, HALO:, c] = both[TOK:]
                else:
                    R.z[1, :, c] += both[0:TOK]
                    R.v[1, HALO:, c] += both[TOK:]
            bc = nn(n, R.wb[1, here, :])
            dtr = nt(n, widened(R.wd[1, :, here]))
            if p == 0:
                R.v[1, HALO:, IL:] = bc
                R.dtr[1] = dtr
            else:
                R.v[1, HALO:, IL:] += bc
                R.dtr[1] += dtr
        neighbour(*v_halo(), K.HA, 1, 1)

    def conv_sum(l, c):
        acc = R.ct[l, 4:5, c] + R.ct[l, 3:4, c] * R.v[l, HALO:, c]
        for k in range(3):
            acc = acc + (R.ct[l, k : k + 1, c] * R.mk[k]) * (
                R.v[l, HALO - 3 + k : HALO + TOK - 3 + k, c]
            )
        return acc

    def convolve(l):
        @pl.loop(0, 10, unroll=2)
        def _(j):
            c = lanes(j)
            acc = conv_sum(l, c)
            R.xbc[l, :, c] = (acc * sigmoid(acc)).astype(BF)

    def steps(l):
        raw = R.dtr[l] + R.hp[l, 0:1]
        dt = jnp.maximum(raw, 0.0) + jnp.log1p(jnp.exp(-jnp.abs(raw)))
        rate = -dt * jnp.exp(R.hp[l, 1:2])
        cum = split_right(nn, R.tri[...], rate, 3)
        R.dt[l] = dt
        R.rate[l] = rate
        R.cum[l] = cum
        flag = jnp.where(own == R.idc[HALO - 1 : HALO], 1.0, 0.0)
        ending = jnp.where(own == R.idc[HALO + TOK - 1 : HALO + TOK], 1.0, 0.0)
        entry = jnp.exp(cum) * flag
        R.entry[l] = entry
        R.wl[l] = jnp.exp(cum[TOK - 1 : TOK] - cum) * ending
        R.last[l] = entry[TOK - 1 : TOK]
        R.dec[l, pl.ds(me, 1)] = R.last[l][None]
        for to, _ in others():
            send(R.last.at[l], R.dec.at[l, me], sem(K.DC, l, 0), sem(K.DC, l, 1), to)
        entry_t = entry.T
        heads = lax.broadcasted_iota(jnp.int32, (128, 128), 0) < HL
        R.dtot[l] = jnp.where(
            heads, jnp.broadcast_to(entry_t[:, TOK - 1 : TOK], (128, 128)), 0.0
        )

    def ssd(l):
        b_mat = R.xbc[l, :, IL : IL + ST]
        c_mat = R.xbc[l, :, IL + ST :]
        dt, wl = pieces(R.dt[l], 2), pieces(R.wl[l], 2)

        @pl.loop(0, 8, unroll=4)
        def _(j):
            c = lanes(j)
            xdt = (R.xbc[l, :, c].astype(F32) * expanded(dt, c)).astype(BF)
            R.xdt[l, :, c] = xdt
            xw = (xdt.astype(F32) * expanded(wl, c)).astype(BF)
            s = tn(xw, b_mat).astype(BF)
            R.S[l, c, :] = s
            R.sb[pl.ds(4 * j, 4)] = s.reshape(4, 32, 128)

        exchange(R.sb, R.rb, K.ST, l)
        R.G[l] = nt(c_mat, b_mat)
        keep = (own == ids_of(me)[0:1]) & (row >= col)
        cum = R.cum[l]
        cum_t = cum.T
        for h in range(HL):
            spread = cum[:, h : h + 1] - cum_t[h : h + 1, :]
            ell = jnp.where(keep, jnp.exp(jnp.where(keep, spread, 0.0)), 0.0)
            R.L[l, h] = ell.astype(BF)

        @pl.loop(0, 8, unroll=4)
        def _(j):
            c = lanes(j)
            a, b = halves(R.xdt[l, :, c])
            R.y[l, :, c] = nn(mixing(l, 2 * j), a) + nn(mixing(l, 2 * j + 1), b)

    def scan_states(l):
        exchanged(R.dec.at[l], K.DC, l)
        mine_of = lax.broadcasted_iota(jnp.int32, (NS, 128), 1) == me // 2
        decays = jnp.concatenate([R.dec[l, b] for b in range(NS)], axis=0)
        decays = jnp.sum(jnp.where(mine_of, decays, 0.0), axis=1, keepdims=True)
        R.decay[l] = jnp.broadcast_to(decays, (NS, 128))
        exchanged(R.rb, K.ST, l)

        def step(b, state):
            R.eb[b] = state.reshape(32, 128).astype(BF)
            d = R.decay[l, pl.ds(b, 1)]
            return state * d[None] + R.rb[b].astype(F32).reshape(4, 8, 128)

        lax.fori_loop(0, NS, step, jnp.zeros((4, 8, 128), F32), unroll=8)
        exchange(R.eb, R.sin.at[l], K.EN, l)

    def gate(l):
        c_mat = R.xbc[l, :, IL + ST :]
        entry = pieces(R.entry[l], 2)
        exchanged(R.sin.at[l], K.EN, l)

        def block(j, acc):
            c = lanes(j)
            sin = R.sin[l, pl.ds(4 * j, 4)].reshape(128, 128)
            xs = R.xbc[l, :, c].astype(F32)
            y = R.y[l, :, c] + nt(c_mat, sin) * expanded(entry, c) + R.skE[l, 2:3, c] * xs
            R.y[l, :, c] = y
            z = R.z[l, :, c]
            g = y * (z * sigmoid(z))
            gg = g * R.gg[l : l + 1, c]
            if l == 0:
                R.dye[:, c] = gg.astype(BF)
            else:
                R.ro[1, :, c] = gg.astype(BF)
            if l == 0:
                return (acc[0] + g * g,)
            return (acc[0] + g * g, acc[1] + gg * R.ds[:, c])

        sums = lax.fori_loop(0, 8, block, (jnp.zeros((TOK, 128), F32),) * (l + 1), unroll=4)
        ones = jnp.ones((8, 128), BF)
        parts = [split_right(nt, ones, s, 2) for s in sums]
        if l == 0:
            R.sq[l] = parts[0]
        else:
            at = lax.broadcasted_iota(jnp.int32, (8, 128), 0)
            R.sq[l] = jnp.where(at == 0, parts[0], parts[1])
        R.sqx[l, pl.ds(mx, 1)] = R.sq[l][None]
        to_x(lambda d: (R.sq.at[l], R.sqx.at[l, mx]), K.SQ, l)

    def root(l):
        from_x(R.sqx.at[l, pl.ds(0, 3)], K.SQ, l)
        total = R.sqx[l, 0] + R.sqx[l, 1] + R.sqx[l, 2] + R.sqx[l, 3]
        q = lax.rsqrt(total[0:1] * (1.0 / INNER) + EPS)
        R.q[l] = jnp.broadcast_to(q, (128, 128)).T
        if l == 1:
            R.scol[...] = jnp.broadcast_to(total[1:2], (128, 128)).T
            R.qrow[...] = q
            to_second(lambda a: R.qrow, lambda a, slot: R.qx.at[a, slot], (K.QY, K.QZ), 1)

    def project_out(l):
        if l == 0:
            weight(K.WO, l).wait()

        for p in range(4):
            for j in range(2):
                c = slice(512 * p + 256 * j, 512 * p + 256 * j + 256)
                left = R.dye[...] if l == 0 else R.ro[1]
                R.pb[:, c] = nn(left, R.wo[l, :, :, c].reshape(IL, 256)).astype(BF)
            scatter_x(R.rs.at[l], K.RS, l, p)

    def next_resid(l, before):
        from_x(R.rs.at[l, pl.ds(0, 3)], K.RS, l)
        total = sum(R.rs[l, k].astype(F32) for k in range(NX))
        if l == 0:
            R.br[...] = total
        return before + R.q[l, mine][:, 0:1] * total

    AG_PIECES = ((K.AP, 0), (K.AP, 1), (K.AQ, 0), (K.AQ, 1))
    BG_PIECES = ((K.BP, 0), (K.BP, 1), (K.BQ, 0), (K.BQ, 1))

    def gather_x(ref, kind, l):
        to_x(lambda d: (ref, ref), kind, l)

    def backward_gate(l):
        entry = pieces(R.entry[l], 2)

        def block(j, acc):
            c = lanes(j)
            z, y = R.z[l, :, c], R.y[l, :, c]
            xs = R.xbc[l, :, c].astype(F32)
            sg = sigmoid(z)
            silu = z * sg
            g = y * silu
            ds, gain, q = R.ds[:, c], R.gg[l : l + 1, c], R.q[l]
            gq = g * q
            dg = ds * gain * q - gq * (q * q * R.scol[...] * (1.0 / INNER))
            dy = dg * silu
            R.ro[0, :, c] = (dg * y * (sg * (1.0 + z * (1.0 - sg)))).astype(BF)
            R.sm[17 + l, pl.ds(j, 1)] = jnp.sum(ds * gq, axis=0, keepdims=True)
            R.dsk[:, c] = jnp.broadcast_to(
                jnp.sum(dy * xs, axis=0, keepdims=True), (8, 128)
            )
            sk = R.skE[l, 2:3, c]
            dyb = dy.astype(BF)
            dyf = dyb.astype(F32)
            R.dyb[:, c] = dyb
            R.dye[:, c] = (dyf * expanded(entry, c)).astype(BF)
            R.ds[:, c] = sk * dy
            direct = tn(R.dye[:, c], R.xbc[l, :, IL + ST :])
            R.sb[pl.ds(4 * j, 4)] = direct.astype(BF).reshape(4, 32, 128)
            return acc + split_left(nn, dyf * (y - sk * xs), R.Et[c, :])

        R.rows[...] = lax.fori_loop(0, 8, block, jnp.zeros((TOK, 128), F32), unroll=4)
        exchange(R.sb, R.rb, K.SB, l)

    def backward_local(l):
        b_mat = R.xbc[l, :, IL : IL + ST]
        c_mat = R.xbc[l, :, IL + ST :]

        def block(j, dgram):
            c = lanes(j)
            a, b = halves(R.dyb[:, c])
            R.U[j] = tn(mixing(l, 2 * j), a) + tn(mixing(l, 2 * j + 1), b)
            xdt = R.xdt[l, :, c]
            return (
                dgram
                + nt(a, xdt) * R.L[l, 2 * j].astype(F32)
                + nt(b, xdt) * R.L[l, 2 * j + 1].astype(F32)
            )

        dgram = lax.fori_loop(0, 8, block, jnp.zeros((TOK, TOK), F32), unroll=4).astype(BF)
        sin = R.sin[l].reshape(IL, ST)
        R.dbc[:, ST:] = nn(dgram, b_mat) + nn(R.dye[...], sin)
        R.dbc[:, 0:ST] = tn(dgram, c_mat)

    def scan_back(l):
        exchanged(R.rb, K.SB, l)

        def step(i, state):
            b = NS - 1 - i
            R.eb[b] = state.reshape(32, 128).astype(BF)
            d = R.decay[l, pl.ds(b, 1)]
            return state * d[None] + R.rb[b].astype(F32).reshape(4, 8, 128)

        lax.fori_loop(0, NS, step, jnp.zeros((4, 8, 128), F32), unroll=8)
        exchange(R.eb, R.lam, K.EB, l)

    def backward_state(l):
        b_mat = R.xbc[l, :, IL : IL + ST]
        dt, wls = pieces(R.dt[l], 2), pieces(R.wl[l], 2)
        exchanged(R.lam, K.EB, l)

        def block(j, carry):
            c = lanes(j)
            lam = R.lam[pl.ds(4 * j, 4)].reshape(128, 128)
            wl = expanded(wls, c)
            ut = R.U[j] + wl * nt(b_mat, lam)
            xdt = R.xdt[l, :, c].astype(F32)
            R.ds[:, c] += expanded(dt, c) * ut
            xw = (xdt * wl).astype(BF)
            lamf = lam.astype(F32)
            et = R.Et[c, :]
            sin = R.sin[l, pl.ds(4 * j, 4)].reshape(128, 128).astype(F32)
            return (
                carry[0] + nn(xw, lam),
                carry[1] + split_right(tn, et, lamf * R.S[l, c, :].astype(F32)),
                carry[2] + split_right(tn, et, lamf * sin),
                carry[3] + split_left(nn, xdt * ut, et),
                carry[4] + split_left(nn, R.xbc[l, :, c].astype(F32) * ut, et),
            )

        zero = jnp.zeros((128, 128), F32)
        db, ks, kd, less, ddt = lax.fori_loop(0, 8, block, (zero,) * 5, unroll=4)
        R.dbc[:, 0:ST] += db
        held = split_right(nt, jnp.ones((8, 128), BF), ks + R.dtot[l] * kd)
        last = lax.broadcasted_iota(jnp.int32, (TOK, 128), 0) == TOK - 1
        dcum = R.rows[...] - less + jnp.where(last, held[0:1], 0.0)
        drate = split_right(tn, R.tri[...], dcum, 3)
        ddt = ddt - drate * jnp.exp(R.hp[l, 1:2])
        ddtr = ddt * sigmoid(R.dtr[l] + R.hp[l, 0:1])
        R.ddt[...] = ddtr.astype(BF)
        at = 4 * l
        R.sm[19, at : at + 1] = jnp.sum(ddtr, axis=0, keepdims=True)
        R.sm[19, at + 1 : at + 2] = jnp.sum(drate * R.rate[l], axis=0, keepdims=True)
        R.sm[19, at + 2 : at + 3] = split_left(nn, R.dsk[...], R.Et[...])[0:1]

    def backward_conv(l):
        def block(c, dact):
            pre = conv_sum(l, c)
            sg = sigmoid(pre)
            R.dpre[l, 0:TOK, c] = dact * (sg * (1.0 + pre * (1.0 - sg)))

        @pl.loop(0, 8, unroll=2)
        def _(j):
            block(lanes(j), R.ds[:, lanes(j)])

        for j in range(2):
            block(pl.ds(IL + 128 * j, 128), R.dbc[:, 128 * j : 128 * j + 128])
        head, tail = R.dpre.at[l, pl.ds(0, 8)], R.dpre.at[l, pl.ds(TOK, 8)]
        neighbour(head, tail, K.DP, l, -1)

        def tap_sums(c):
            dpre = R.dpre[l, 0:TOK, c]
            out = []
            for k in range(3):
                shifted = R.v[l, HALO - 3 + k : HALO + TOK - 3 + k, c]
                out.append(jnp.sum(dpre * shifted * R.mk[k], axis=0, keepdims=True))
            out.append(jnp.sum(dpre * R.v[l, HALO:, c], axis=0, keepdims=True))
            return [*out, jnp.sum(dpre, axis=0, keepdims=True)]

        @pl.loop(0, 8, unroll=2)
        def _(j):
            for k, s in enumerate(tap_sums(lanes(j))):
                R.sm[7 + 5 * l + k, pl.ds(j, 1)] = s

        for j in range(2):
            for k, s in enumerate(tap_sums(pl.ds(IL + 128 * j, 128))):
                at = 12 * l + 2 * k + j
                R.sm[4 + at // 8, at % 8 : at % 8 + 1] = s
        if l == 0:
            R.smr[pl.ds(me, 1)] = R.sm[pl.ds(me, 1)]
            for to, d in others():

                @pl.when(d < OWNERS)
                def _(to=to, d=d):
                    send(R.sm.at[d], R.smr.at[me], sem(K.SM, 0, 0), sem(K.SM, 0, 1), to)

        neighbour_done(head, tail, K.DP, l, -1)

        def back(c):
            out = R.ct[l, 3:4, c] * R.dpre[l, 0:TOK, c]
            for k in range(3):
                out = out + (R.ct[l, k : k + 1, c] * R.mkb[k]) * (
                    R.dpre[l, 3 - k : TOK + 3 - k, c]
                )
            return out.astype(BF)

        for j in range(2):
            R.dbp[:, 128 * j : 128 * j + 128] = back(pl.ds(IL + 128 * j, 128))
        send_bc(l)

        @pl.loop(0, 8, unroll=2)
        def _(j):
            R.re[j // 4, :, lanes(lax.rem(j, 4))] = back(lanes(j))

    def send_bc(l):
        R.bx[pl.ds(mx, 1)] = R.dbp[:, lanes(mx // 2)][None]
        to_x(lambda d: (R.dbp.at[:, lanes(d // 2)], R.bx.at[mx]), K.BX, l)

    def sum_bc(l):
        from_x(R.bx.at[pl.ds(0, 3)], K.BX, l)
        block = sum(R.bx[k].astype(F32) for k in range(NX))
        swapped = jnp.concatenate([block[:, 64:], block[:, 0:64]], axis=1)
        block = jnp.where(lax.rem(mx, 2) == 0, swapped, block)
        R.re[0, :, 512:640] = jnp.where(lo, R.ddt[...].astype(F32), block).astype(BF)

    def backward_project(l):
        R.x2t[:, 0:TOK] = R.ro[0].T
        for k in range(2):
            R.x2t[512 * k : 512 * k + 512, TOK:] = R.re[k, :, 0:512].T
        dbp_t = R.dbp[...].T
        dt_t = R.ddt[...].T[0:HL]
        for p in range(4):
            for j in range(2 * p, 2 * p + 2):
                rows = slice(256 * j, 256 * j + 256)
                both = nn(R.wz[l, rows].reshape(512, IL), R.x2t[...])
                part = nn(R.wb[l, rows, :], dbp_t) + tn(R.wd[l, :, rows], dt_t)
                for k in range(2):
                    buf = R.U.reshape(2, 512, 128).at[k]
                    buf[...] = both[:, TOK * k : TOK * k + TOK]
                    part += buf[pl.ds(k, 256, stride=2), :]
                R.pb[:, rows] = part.T.astype(BF)
            scatter_x(R.rs.at[1 - l], K.RB, l, p)

    def backward_norm(l, above):
        from_x(R.rs.at[1 - l, pl.ds(0, 3)], K.RB, l)
        dn = sum(R.rs[1 - l, k].astype(F32) for k in range(NX))
        u = R.u[l]
        r = lax.rsqrt(jnp.mean(u * u, axis=1, keepdims=True) + EPS)
        gw = dn * R.ng[l : l + 1, :]
        gain = jnp.sum(dn * u * r, axis=0, keepdims=True)
        R.gain[l : l + 1] = gain
        s = jnp.sum(gw * u, axis=1, keepdims=True) * (1.0 / D)
        return above + gw * r - u * (r * r * r * s)

    def back_scaled_pieces():
        for p in range(4):
            here = slice(512 * p, 512 * p + 512)
            from_x(R.dbr0.at[pl.ds(0, 96), pl.ds(512 * p, 512)], *BG_PIECES[p])
            for j in range(4):
                c = slice(256 * j, 256 * j + 256)
                right = R.wo[0, 2 * j : 2 * j + 2, :, here].reshape(256, 512)
                part = nt(R.dbr0[:, here], right)
                if p == 0:
                    R.ds[:, c] = part
                else:
                    R.ds[:, c] += part

    def back_scaled(l, src):
        @pl.loop(0, 4, unroll=2)
        def _(j):
            R.ds[:, lanes(j, 256)] = nt(src[...], R.wo[l, pl.ds(2 * j, 2)].reshape(256, D))

    def transposed(src, dst):
        @pl.loop(0, 16, unroll=8)
        def _(j):
            dst[j // 4, lax.rem(j, 4)] = src(lanes(j)).T

    AXES = (("y", iy), ("z", iz))

    def left_block(src, a, p):
        return src.at[:, p] if a == 0 else src.at[p]

    def share_left(l, part=slice(0, 4)):
        blocks = pl.ds(part.start, part.stop - part.start)
        for a, (axis, at) in enumerate(AXES):
            slot = lanes(2 * at + ic)
            dst = R.nl.at[l, a, blocks, :, slot]
            for k in (2, 1, 3):
                p = lax.rem(at + k, 4)
                kind = (K.NY, K.NZ)[a]
                src = left_block(R.nbt, a, p).at[blocks]
                send(src, dst, sem(kind, l, 0), sem(kind, l, 1), {axis: p})
            dst[...] = left_block(R.nbt, a, at).at[blocks][...]

    def pass_left(l):
        for a, (axis, at) in enumerate(AXES):
            kind, three = (K.NY, K.NZ)[a], R.nl.at[l, a, :, :, pl.ds(0, 384)]
            wait_for(three, sem(kind, l, 1))
            wait_for(three, sem(kind, l, 0))
            for k in range(4):
                ref = R.nl.at[l, a, :, :, lanes(2 * k + ic)]
                kind = (K.FY, K.FZ)[a]
                send(ref, ref, sem(kind, l, 0), sem(kind, l, 1), {"c": 1 - ic})

    def left_done(l):
        for a in range(2):
            four = R.nl.at[l, a, :, :, pl.ds(0, 512)]
            wait_for(four, sem((K.FY, K.FZ)[a], l, 1))
            wait_for(four, sem((K.FY, K.FZ)[a], l, 0))

    def share_branch(l):
        for a, (axis, at) in enumerate(AXES):
            slot = lanes(2 * at + ic)
            dst, kind = R.dl.at[l, a, :, :, slot], (K.DY, K.DZ)[a]

            def remote(p, dst=dst, kind=kind, axis=axis, a=a):
                send(
                    left_block(R.dbt, a, p), dst, sem(kind, l, 0), sem(kind, l, 1),
                    {axis: p, "c": 1},
                )

            for k in (2, 1, 3):
                remote(lax.rem(at + k, 4))

            @pl.when(ic == 0)
            def _(remote=remote, at=at):
                remote(at)

            @pl.when(ic == 1)
            def _(dst=dst, a=a, at=at):
                dst[...] = left_block(R.dbt, a, at)[...]

    def to_second(src, dst, kinds, l):
        for a, (axis, at) in enumerate(AXES):

            def remote(p, a=a, axis=axis, at=at):
                send(
                    src(a), dst(a, 2 * at + ic), sem(kinds[a], l, 0), sem(kinds[a], l, 1),
                    {axis: p, "c": 1},
                )

            for k in (2, 1, 3):
                remote(lax.rem(at + k, 4))
            pl.when(ic == 0)(lambda remote=remote, at=at: remote(at))

            @pl.when(ic == 1)
            def _(a=a, at=at):
                here = sem((K.CY, K.CZ)[a], l, 0 if kinds[0] == K.LY else 1)
                pltpu.make_async_copy(src(a), dst(a, 2 * at + ic), here).start()

    def at_second(ref, kinds, l):
        for a in range(2):

            @pl.when(ic == 1)
            def _(a=a):
                wait_for(ref.at[a, pl.ds(0, 7)], sem(kinds[a], l, 1))
                wait_for(ref.at[a, pl.ds(0, 3)], sem(kinds[a], l, 0))
                wait_for(ref.at[a, 0], sem((K.CY, K.CZ)[a], l, 0 if kinds[0] == K.LY else 1))

            @pl.when(ic == 0)
            def _(a=a):
                wait_for(ref.at[a, pl.ds(0, 4)], sem(kinds[a], l, 0))

    def share_scaled(l):
        to_second(
            lambda a: R.ro.at[1, :, pl.ds(512 * a, 512)],
            lambda a, slot: R.late.at[l, a, slot], (K.LY, K.LZ), l,
        )

    def scaled_first():
        @pl.loop(0, 8, unroll=4)
        def _(j):
            c = lanes(j)
            z = R.z[0, :, c]
            g = R.y[0, :, c] * (z * sigmoid(z))
            R.ro[1, :, c] = (g * R.q[0] * R.gg[0:1, c]).astype(BF)

        share_scaled(0)

    def scaled_done(l):
        at_second(R.late.at[l], (K.LY, K.LZ), l)

    def scaled_load(l, a):
        dst = R.wo.at[1, :, :, pl.ds(512 * a, 512)]
        return pltpu.make_async_copy(R.late.at[l, a], dst, sem(K.OWN, l, a))

    def scaled_fetch(l):
        @pl.when(ic == 1)
        def _():
            for a in range(2):
                scaled_load(l, a).start()

    def branch_times_root():
        at_second(R.qx, (K.QY, K.QZ), 1)

        @pl.when(ic == 1)
        def _():
            for a in range(2):
                q = jnp.concatenate([R.qx[a, k] for k in range(8)], axis=1)

                @pl.loop(0, 4)
                def _(b, a=a, q=q):
                    R.dl[1, a, b] = (R.dl[1, a, b].astype(F32) * q).astype(BF)

    def branch_done(l):
        for a in range(2):

            def count(blocks, side, a=a):
                ref = R.dl.at[l, a, :, :, pl.ds(0, 128 * blocks)]
                wait_for(ref, sem((K.DY, K.DZ)[a], l, side))

            @pl.when(ic == 1)
            def _(count=count):
                count(7, 1)
                count(3, 0)

            @pl.when(ic == 0)
            def _(count=count):
                count(4, 0)

    def job(n):
        wide = n % 2 == 0

        def land(a, slot):
            at = (0 if wide else 1024) + 512 * a
            return R.wo.at[1, slot, :, pl.ds(at, (WIDE if wide else NARROW)[a])]

        return WIDE if wide else NARROW, land, R.ro if wide else R.re

    def by_core(n, a, core):
        return 256 if n % 2 and a and core else job(n)[0][a]

    def prod(n, a, block, width):
        if n == 3:
            return R.dl.at[1, a, block, :, pl.ds(0, width)]
        at = pl.multiple_of(512 * (4 * a + block), 512)
        return R.nx.at[pl.ds(8 * (n % 2), 8), :, pl.ds(at, width)]

    def land2(n, a, slot, width):
        if n == 3:
            return R.nl.at[1, a, slot, :, pl.ds(0, width)]
        return R.land.at[n % 2, a, slot, :, :, pl.ds(0, width)]

    def jsem(n, kind, side):
        return R.jsem.at[n, kind, side]

    def job_share(n, cores, axes=(0, 1), mixed=False):
        for a in axes:
            widths, land, src = job(n)
            axis, at = AXES[a]
            kind = (J.Y1, J.Z1)[a]
            slot = 2 * at + ic
            first, width = (256, 128) if mixed else (0, by_core(n, a, 1))
            c = pl.ds(widths[0] * a + first, width)

            def dst(a=a, slot=slot, first=first, width=width, land=land):
                return land(a, slot).at[:, pl.ds(first, width)]

            for k in (2, 1, 3, 0):
                p = lax.rem(at + k, 4)
                for core in cores:

                    def remote(core=core, p=p, c=c, dst=dst, axis=axis, kind=kind, src=src):
                        send(
                            src.at[core, :, c], dst(), jsem(n, kind, 0), jsem(n, kind, 1),
                            {axis: p, "c": core},
                        )

                    if k:
                        remote()
                    else:
                        pl.when(ic != core)(remote)

                        @pl.when(ic == core)
                        def _(core=core, c=c, dst=dst, src=src):
                            dst()[...] = src[core, :, c]

    def job_multiply(n, l):
        widths, land, _ = job(n)
        cores = (0,) if n % 2 == 0 else (0, 1)

        def blocks(count, width):
            return R.wo.at[1, pl.ds(0, count), :, pl.ds(0, width)]

        for a, kind in enumerate((J.Y1, J.Z1)):
            for core in (0, 1):

                @pl.when(ic == core)
                def _(a=a, kind=kind, core=core):
                    for to in cores:
                        width = by_core(n, a, to)
                        if to == core:
                            wait_for(blocks(7, width), jsem(n, kind, 1))
                        wait_for(blocks(3 if to == core else 4, width), jsem(n, kind, 0))
                    if n % 2 == 0 and core == 1:
                        scaled_load(l, a).wait()

        def product(left):
            for a in range(2):
                for w in range(0, widths[a], 256):
                    width = min(256, widths[a] - w)
                    at = (0 if n % 2 == 0 else 1024) + 512 * a + w
                    right = R.wo[1, :, :, at : at + width].reshape(1024, width)
                    out = nn(left[a].reshape(512, 1024), right)
                    if n == 3:
                        out = out.astype(BF).reshape(4, 128, width)
                        R.dl[1, a, :, :, w : w + width] = out
                        continue
                    out = out.astype(BF).reshape(4, 8, 16, width)
                    for b in range(4):
                        at = 512 * (4 * a + b) + w
                        R.nx[8 * (n % 2) : 8 * (n % 2) + 8, :, at : at + width] = out[b]

        if n % 2:
            product(R.nl.at[l])
            return

        @pl.when(ic == 0)
        def _():
            product(R.nl.at[l])

        @pl.when(ic == 1)
        def _():
            product(R.dl.at[l])

    REDUCES = ((0, "z", iz, J.Z2), (1, "y", iy, J.Y2))

    def each_core(n, a, act):
        if by_core(n, a, 0) == by_core(n, a, 1):
            act(by_core(n, a, 0))
            return
        for core in (0, 1):
            pl.when(ic == core)(lambda core=core: act(by_core(n, a, core)))

    def job_reduce(n):
        for a, axis, at, kind in REDUCES:

            def act(width, a=a, axis=axis, at=at, kind=kind):
                for k in (2, 1, 3):
                    p = lax.rem(at + k, 4)
                    send(
                        prod(n, a, p, width), land2(n, a, at, width),
                        jsem(n, kind, 0), jsem(n, kind, 1), {axis: p},
                    )

            each_core(n, a, act)

    def job_outputs(n, half_at, to_self):
        l = 1 - n // 2
        rows = pl.ds(pl.multiple_of(64 * half_at, 64), 64)
        kind = J.OWN if to_self else J.OUT

        def put(columns, dst):
            src = R.total.at[n % 2, rows, columns]
            if to_self:
                pltpu.make_async_copy(src, dst, jsem(n, kind, 0)).start()
            else:
                send(src, dst, jsem(n, kind, 0), jsem(n, kind, 1), {"c": 1 - ic})

        @pl.when(ic == 0)
        def _():
            if n % 2 == 0:
                put(pl.ds(0, IL), R.zx_o.at[l, :, 0])
            else:
                put(pl.ds(0, 512), R.zx_o.at[l, :, 1, pl.ds(0, 512)])
                put(pl.ds(512, 128), R.mix_o.at[l, mx])
                to_x(
                    lambda d: (R.total.at[1, rows, pl.ds(512, 128)], R.mix_o.at[l, mx]),
                    K.MX if to_self else K.MS, l, {} if to_self else {"c": 1 - ic},
                )

        @pl.when(ic == 1)
        def _():
            if n % 2 == 0:
                put(pl.ds(0, IL), R.out_o.at[l])
            else:
                put(pl.ds(0, 512), R.zx_o.at[l, :, 1, pl.ds(512, 512)])

    def job_sum2(n):
        widths, _, _ = job(n)
        for a, _, _, kind in REDUCES:

            def act(width, a=a, kind=kind):
                three = R.land.at[0, 0, pl.ds(0, 3), :, :, pl.ds(0, width)]
                wait_for(three, jsem(n, kind, 1))
                wait_for(three, jsem(n, kind, 0))

            each_core(n, a, act)
        for a, _, at, _ in REDUCES:

            def act(width, a=a, at=at):
                for w in range(0, width, 128):
                    here, w = slice(a * widths[0] + w, a * widths[0] + w + 128), slice(w, w + 128)
                    parts = [prod(n, a, at, width)]
                    parts += [land2(n, a, lax.rem(at + k, 4), width) for k in (1, 2, 3)]
                    s = sum(part[..., w].astype(F32) for part in parts)
                    R.total[n % 2, :, here] = s.reshape(128, 128)

            each_core(n, a, act)
        job_outputs(n, ic, True)
        job_outputs(n, 1 - ic, False)

    def job_done(n):
        l = 1 - n // 2

        def all_of(width, kind, side):
            wait_for(R.total.at[0, pl.ds(0, 64), pl.ds(0, width)], jsem(n, kind, side))

        if n % 2 == 0:
            for kind, side in ((J.OWN, 0), (J.OUT, 0), (J.OUT, 1)):
                all_of(IL, kind, side)
            return

        @pl.when(ic == 0)
        def _():
            for kind, side, width in ((J.OWN, 0, 640), (J.OUT, 0, 640), (J.OUT, 1, 512)):
                all_of(width, kind, side)
            three = R.mix_o.at[l, pl.ds(0, 3)]
            wait_for(three, sem(K.MX, l, 0))
            wait_for(three, sem(K.MS, l, 0))
            wait_for(three, sem(K.MX, l, 1))

        @pl.when(ic == 1)
        def _():
            for kind, side, width in ((J.OWN, 0, 512), (J.OUT, 0, 512), (J.OUT, 1, 640)):
                all_of(width, kind, side)
            wait_for(R.mix_o.at[l, pl.ds(0, 3)], sem(K.MS, l, 1))

    def edge_out(i, dst, value):
        R.edge[i] = value.astype(BF)
        here = dst.at[mine]
        pltpu.make_async_copy(R.edge.at[i], here, sem(K.HID, 1, i)).start()
        kind = (K.OH, K.GI)[i]
        to_x(lambda d: (R.edge.at[i], here), kind, 0)

    def edge_done(i, dst):
        wait_for(R.edge.at[i], sem(K.HID, 1, i))
        from_x(dst.at[pl.ds(0, 96)], (K.OH, K.GI)[i], 0)

    resid_in.wait()

    @pl.loop(0, 4)
    def _(j):
        rows = pl.ds(pl.multiple_of(j * 32, 32), 32)
        at = pl.ds(pl.multiple_of(HALO + j * 32, 16), 32)
        R.nrm[0, at] = normalize(R.pb[rows].astype(F32), 0)

    R.u[0] = R.pb[mine].astype(F32)
    transposed(lambda c: R.cot[:, c], R.dbt)
    everyone_is_here()
    neighbour(*halo(0), K.HA, 0, 1)
    project_first()
    convolve(0)
    steps(0)
    ssd(0)
    transposed(lambda c: R.nrm[0, HALO:, c], R.nbt)
    scan_states(0)
    gate(0)
    share_left(0)
    share_branch(1)
    project_out(0)
    root(0)
    R.u[1] = next_resid(0, R.u[0])
    at = pl.ds(pl.multiple_of(HALO + mx * 32, 16), 32)
    R.nrm[1, at] = normalize(R.u[1], 1)

    for p in range(4):
        gather_x(R.nrm.at[1, at, pl.ds(512 * p, 512)], *AG_PIECES[p])
    scaled_first()
    pass_left(0)
    project_second()
    steps(1)
    transposed(lambda c: R.nrm[1, HALO:, c], R.nbt)
    share_left(1, slice(0, 2))
    neighbour_done(*v_halo(), K.HA, 1, 1)
    convolve(1)
    ssd(1)
    weight(K.WO, 1).wait()
    back_scaled(1, R.cot)
    scan_states(1)
    scaled_done(0)
    gate(1)
    share_scaled(1)
    project_out(1)
    root(1)
    backward_gate(1)
    backward_local(1)
    scan_back(1)
    edge_out(0, R.oh, next_resid(1, R.u[1]))
    left_done(0)
    branch_done(1)
    scaled_done(1)
    scaled_fetch(1)
    backward_state(1)
    backward_conv(1)
    share_left(1, slice(2, 4))
    job_share(0, (0,))
    backward_project(1)
    sum_bc(1)
    job_share(1, (0, 1))
    job_share(1, (0,), (1,), True)
    pass_left(1)
    branch_times_root()
    R.du[...] = backward_norm(1, R.cot[mine].astype(F32))
    R.dbr0[mine] = R.du[...].astype(BF)
    for p in range(4):
        gather_x(R.dbr0.at[mine, pl.ds(512 * p, 512)], *BG_PIECES[p])
    s = jnp.sum(R.du[...].astype(BF).astype(F32) * R.br[...], axis=1, keepdims=True)
    R.scol[mine] = jnp.broadcast_to(s, (32, 128))
    gather_x(R.scol.at[mine], K.SC, 0)
    edge_done(0, R.oh)
    left_done(1)
    job_multiply(0, 1)
    job_reduce(0)
    back_scaled_pieces()
    transposed(lambda c: R.dbr0[:, c], R.dbt)
    from_x(R.scol.at[pl.ds(0, 96)], K.SC, 0)
    backward_gate(0)
    share_branch(0)
    scaled_fetch(0)
    backward_local(0)
    job_multiply(1, 1)
    job_sum2(0)
    scan_back(0)
    job_share(2, (0,))
    backward_state(0)
    backward_conv(0)
    job_share(3, (0, 1))
    backward_project(0)
    sum_bc(0)
    job_share(3, (0,), (1,), True)
    job_reduce(1)
    branch_done(0)
    job_multiply(2, 0)
    job_reduce(2)
    job_multiply(3, 0)
    job_reduce(3)

    def summed(l, ref, part, of_x):
        part[...] = sum(ref[k] for k in range(NS))
        of_x[pl.ds(mx, 1)] = part[...][None]
        to_x(lambda d: (part, of_x.at[mx]), K.SX, l)

    def summed_over_x(l, of_x):
        from_x(of_x.at[pl.ds(0, 3)], K.SX, l)
        return of_x[0] + of_x[1] + of_x[2] + of_x[3]

    @pl.when(me < OWNERS)
    def _():
        wait_for(R.smr.at[pl.ds(0, NS - 1)], sem(K.SM, 0, 1))
        wait_for(R.smr.at[pl.ds(0, OWNERS - 1)], sem(K.SM, 0, 0))

    @pl.when(me >= OWNERS)
    def _():
        wait_for(R.smr.at[pl.ds(0, OWNERS)], sem(K.SM, 0, 0))

    summed(0, R.smr, R.smt, R.smx)
    edge_out(1, R.gi, backward_norm(0, R.du[...]))
    for k in range(NS):
        R.gsm[k] = R.gain[:, 128 * (k // 2) : 128 * (k // 2) + 128]
    exchange(R.gsm, R.gsr, K.SM, 1)
    over_x = summed_over_x(0, R.smx)
    R.smt[...] = jnp.where(me < 7, over_x, R.smt[...])
    R.sums[pl.ds(me, 1)] = R.smt[...][None]

    @pl.when(me < OWNERS)
    def _():
        for to, _ in others():
            send(R.smt, R.sums.at[me], sem(K.SG, 0, 0), sem(K.SG, 0, 1), to)

    job_done(0)
    job_sum2(1)
    job_sum2(2)
    exchanged(R.gsr, K.SM, 1)
    summed(1, R.gsr, R.gst, R.gsx)

    @pl.when(me < OWNERS)
    def _():
        wait_for(R.sums.at[pl.ds(0, OWNERS - 1)], sem(K.SG, 0, 1))
        wait_for(R.sums.at[pl.ds(0, NS - 1)], sem(K.SG, 0, 0))

    @pl.when(me >= OWNERS)
    def _():
        wait_for(R.sums.at[pl.ds(0, OWNERS)], sem(K.SG, 0, 1))

    job_done(1)
    job_sum2(3)
    R.norm[...] = summed_over_x(1, R.gsx)
    edge_done(1, R.gi)
    job_done(2)
    job_done(3)


def chain(*args):
    vmem = pl.BlockSpec(memory_space=pltpu.VMEM)
    held = pl.BlockSpec(memory_space=pl.ANY)
    return pl.pallas_call(
        chain_kernel,
        out_shape=[jax.ShapeDtypeStruct(s, t) for s, t, _ in OUT.values()],
        in_specs=[held if far else vmem for far in IN.values()],
        out_specs=[held if far else vmem for _, _, far in OUT.values()],
        scratch_shapes=[pltpu.VMEM(s, t) for s, t in SCRATCH.values()]
        + [pltpu.SemaphoreType.DMA((42, 2, 2)), pltpu.SemaphoreType.DMA((4, 6, 2))],
        compiler_params=pltpu.CompilerParams(
            collective_id=1, has_side_effects=True, vmem_limit_bytes=64 * 2**20
        ),
        name="chain",
    )(*args)


def finish_kernel(
    oh, gi, zx, out, mix, sums, norm,
    oh_o, gi_o, norm_o, zx_o, bc_o, dt_o, bias_o, alog_o, skip_o, cx_o, cxb_o, cbc_o, cbcb_o,
    gate_o, out_o, sem,
):
    me = position()
    moves = [(oh, oh_o), (gi, gi_o), (out, out_o), (zx, zx_o)]
    copies = [pltpu.make_async_copy(a, b, sem.at[i]) for i, (a, b) in enumerate(moves)]
    for c in copies:
        c.start()
    for l in range(2):
        row = norm[l : l + 1]
        norm_o[l : l + 1] = jnp.where(lax.rem(me, 2) == 0, row[:, 0:64], row[:, 64:])
        dt_o[l] = mix[l, lax.axis_index("x")].T[0:HL]
        for x in range(NX):
            bc_o[l, :, 64 * x : 64 * x + 64] = mix[l, x][:, 64:]
        for i, ref in enumerate((bias_o, alog_o, skip_o)):
            ref[l : l + 1] = sums[19, 4 * l + i : 4 * l + i + 1, 0:HL]
        for j in range(8):
            c = slice(128 * j, 128 * j + 128)
            for k in range(4):
                cx_o[l, k : k + 1, c] = sums[7 + 5 * l + k, j : j + 1]
            cxb_o[l : l + 1, c] = sums[11 + 5 * l, j : j + 1]
            gate_o[l : l + 1, c] = sums[17 + l, j : j + 1]
        for j in range(2):
            c = slice(128 * j, 128 * j + 128)
            for k in range(5):
                at = 12 * l + 2 * k + j
                v = sums[4 + at // 8, at % 8 : at % 8 + 1]
                if k < 4:
                    cbc_o[l, k : k + 1, c] = v
                else:
                    cbcb_o[l : l + 1, c] = v
    for c in copies:
        c.wait()


def finish(*args):
    vmem = pl.BlockSpec(memory_space=pltpu.VMEM)
    held = pl.BlockSpec(memory_space=pl.ANY)
    shapes = [
        ((TOK, D), BF, 0), ((TOK, D), BF, 0), ((2, 64), F32, 0), ((2, 64, 2, IL), F32, 0),
        ((2, 64, 256), F32, 0), ((2, HL, 64), F32, 0), ((2, HL), F32, 0), ((2, HL), F32, 0),
        ((2, HL), F32, 0), ((2, 4, IL), F32, 0), ((2, IL), F32, 0), ((2, 4, 256), F32, 0),
        ((2, 256), F32, 0), ((2, IL), F32, 0), ((2, 64, IL), F32, 0),
    ]
    return pl.pallas_call(
        finish_kernel,
        out_shape=[jax.ShapeDtypeStruct(s, t) for s, t, _ in shapes],
        in_specs=[held] * 4 + [vmem] * 3,
        out_specs=[held if far else vmem for _, _, far in shapes],
        scratch_shapes=[pltpu.SemaphoreType.DMA((8,))],
        name="finish",
    )(*args)


def local(
    hidden_in, cotangent, segment_ids, norm_gain, weight_zx, weight_bc, weight_dt, dt_bias, a_log,
    skip_scale, conv_x, conv_x_bias, conv_bc, conv_bc_bias, gate_gain, weight_out,
):
    *raw, _ = chain(
        hidden_in, cotangent, segment_ids.reshape(NS, TOK), norm_gain, gate_gain, dt_bias,
        a_log, skip_scale, conv_x, conv_x_bias, conv_bc, conv_bc_bias, weight_zx, weight_bc,
        jnp.swapaxes(weight_dt, 1, 2), weight_out.reshape(2, 8, 128, D),
    )
    done = finish(*raw)
    return (*done[:5], jnp.swapaxes(done[5], 1, 2), *done[6:14], jnp.swapaxes(done[14], 1, 2))


def solution(mesh):
    finer = Mesh(mesh.devices.reshape(4, 4, 2, 4), ("z", "y", "c", "x"))
    in_specs = (
        P(SEQ, None), P(SEQ, None), P(), P(), P(None, None, None, "x"), P(), P(None, None, "x"),
        P(None, "x"), P(None, "x"), P(None, "x"), P(None, None, "x"), P(None, "x"), P(), P(),
        P(None, "x"), P(None, "x", None),
    )
    out_specs = (
        P(SEQ, None), P(SEQ, None), P(None, SEQ), P(None, SEQ, None, "x"), P(None, SEQ, None),
        P(None, SEQ, "x"), P(None, "x"), P(None, "x"), P(None, "x"), P(None, None, "x"),
        P(None, "x"), P(), P(), P(None, "x"), P(None, "x", SEQ),
    )
    return jax.shard_map(local, mesh=finer, in_specs=in_specs, out_specs=out_specs, check_vma=False)
```
